32 devices in a mesh: dp: 2 (over x), expert: 16 (over z, y, core).
Axes of the slice: x: 2, y: 2, z: 4, core: 2. Of those that a mesh axis runs over, the one named last changes fastest.
Arguments:
- layer_input: bfloat16 [2, 2, 2048, 2048], P('dp', None, 'expert'), may hold values from -6 to 6
- cotangent: bfloat16 [2, 2, 2048, 2048], P('dp', None, 'expert'), may hold values from -6 to 6
- doc_lengths: int32 [2, 2, 6], P('dp'), may hold values from 1 to 1024, 2048 in all within a row
- routes: int32 [2, 2, 2048, 6], P('dp', None, 'expert'), may hold values from 0 to 15, all different within a row
- attention_gain: bfloat16 [2048], P(('dp', 'expert')), may hold values from 0.099609375 to 1.8984375
- query_weight: bfloat16 [2048, 3072], P(('dp', 'expert')), may hold values from -0.125 to 0.125
- latent_weight: bfloat16 [2048, 576], P(('dp', 'expert')), may hold values from -0.125 to 0.125
- latent_gain: bfloat16 [512], P(('dp', 'expert')), may hold values from 0.099609375 to 1.8984375
- expand_weight: bfloat16 [512, 4096], P(('dp', 'expert')), may hold values from -0.25 to 0.25
- output_weight: bfloat16 [2048, 2048], P(None, ('dp', 'expert')), may hold values from -2 to 2
- feed_gain: bfloat16 [2048], P(('dp', 'expert')), may hold values from 0.099609375 to 1.8984375
- router_weight: bfloat16 [2048, 16], P(('dp', 'expert')), may hold values from -0.0625 to 0.0625
- shared_gate: bfloat16 [2048, 2816], P(('dp', 'expert')), may hold values from -0.125 to 0.125
- shared_up: bfloat16 [2048, 2816], P(('dp', 'expert')), may hold values from -0.125 to 0.125
- shared_down: bfloat16 [2816, 2048], P(('dp', 'expert')), may hold values from -0.109375 to 0.109375
- expert_gate: bfloat16 [16, 2048, 1408], P('expert', 'dp'), may hold values from -0.125 to 0.125
- expert_up: bfloat16 [16, 2048, 1408], P('expert', 'dp'), may hold values from -0.125 to 0.125
- expert_down: bfloat16 [16, 1408, 2048], P('expert', None, 'dp'), may hold values from -2.5 to 2.5
Outputs:
- layer_output: bfloat16 [2, 2, 2048, 2048], P('dp', None, 'expert')
- input_grad: float32 [2, 2, 2048, 2048], P('dp', None, 'expert')
- attention_gain_grad: float32 [2048], P(('dp', 'expert'))
- query_weight_grad: float32 [2048, 3072], P(('dp', 'expert'))
- latent_weight_grad: float32 [2048, 576], P(('dp', 'expert'))
- latent_gain_grad: float32 [512], P(('dp', 'expert'))
- expand_weight_grad: float32 [512, 4096], P(('dp', 'expert'))
- output_weight_grad: float32 [2048, 2048], P(None, ('dp', 'expert'))
- feed_gain_grad: float32 [2048], P(('dp', 'expert'))
- router_weight_grad: float32 [2048, 16], P(('dp', 'expert'))
- shared_gate_grad: float32 [2048, 2816], P(('dp', 'expert'))
- shared_up_grad: float32 [2048, 2816], P(('dp', 'expert'))
- shared_down_grad: float32 [2816, 2048], P(('dp', 'expert'))
- expert_gate_grad: float32 [16, 2048, 1408], P('expert', 'dp')
- expert_up_grad: float32 [16, 2048, 1408], P('expert', 'dp')
- expert_down_grad: float32 [16, 1408, 2048], P('expert', None, 'dp')
The draws below stay inside these ranges and needn't reach their ends.
Inputs may be any that keep to these rules, and one draw needn't show every extreme that they name: `doc_lengths`: each row holds the lengths of the 6 documents packed in order into one sequence; they sum to 2048. `routes`: each token names 6 different experts, in the order of its gates.
All inputs are finite; a program needn't handle non-finite values.
Results may differ from the reference program's by a relative error of at most 0.02.
Values may be sent and summed in bfloat16 or wider, within the bound.
A program may use at most 320 MiB of HBM per device.

```python
import math
import jax
import jax.numpy as jnp
import numpy as np
from jax import lax

D = 2048
H = 16
NOPE = 128
ROPE = 64
VDIM = 128
LAT = 512
FF = 1408
FS = 2816
TOP = 6
WINDOW = 1024
SEQ = 2048
MICRO = 2
DOCS = 6
EXPERTS = 16
TOK_MB = 128
CAP = 54
N_DP = 2
N_EXPERT = 16


def block_scale(key, shape, split, smallest, largest):
    def one(dim, shards_of):
        heights = jax.random.uniform(jax.random.fold_in(jax.random.fold_in(key, 6), dim), (shards_of,), jnp.float32, smallest / len(split), largest / len(split))
        return jnp.repeat(jnp.exp(heights), shape[dim] // shards_of).reshape((-1,) + (1,) * (len(shape) - dim - 1))

    level = one(*split[0])
    for cut in split[1:]:
        level = level * one(*cut)
    return level


def picks_of(stream_key, rows, number_of, top, lift):
    order = jax.random.permutation(jax.random.fold_in(stream_key, 1), number_of)
    pull = order
    for power in range(3):
        pull = pull * pull // number_of
    pull = pull * lift // number_of
    chance = jax.random.randint(jax.random.fold_in(stream_key, 2), (rows, number_of), 0, 4096) + pull
    fixed_rows = jax.random.permutation(jax.random.fold_in(stream_key, 3), rows)[jnp.arange(number_of) % rows]
    chance = jnp.where(jnp.arange(rows)[:, None] == fixed_rows[None, :], 1 << 14, chance)
    score = chance * number_of + jnp.arange(number_of)
    return lax.top_k(score.astype(jnp.int32), top)[1].astype(jnp.int32)


def split_up(count, total, bound, lean):
    portions = [(1 << 20) // math.isqrt(standing ** lean) + 1 for standing in range(2, count + 1)]
    surplus, holding = total - bound - (count - 1), [1] * (count - 1)
    while surplus > 0:
        movable = [i for i in range(count - 1) if holding[i] < bound]
        pool, budget = sum([portions[i] for i in movable]), surplus
        for i in movable:
            addition = min(bound - holding[i], max(1, budget * portions[i] // pool), surplus)
            holding[i] = holding[i] + addition
            surplus = surplus - addition
    return np.array([bound] + holding)


def ragged(stream_key, amount, total, reach, lean):
    if amount == 2:
        one = jax.random.randint(stream_key, (), max(1, total - reach), min(reach, total - 1) + 1)
        return jnp.stack([one, total - one])
    sizes = jnp.asarray(split_up(amount, total, reach, lean), jnp.int32)
    couples = (amount - 1) // 2
    source_of, receiver = sizes[1:1 + 2 * couples:2], sizes[2:2 + 2 * couples:2]
    margin = jnp.minimum(source_of - 1, reach - receiver)
    shifted = jax.random.randint(jax.random.fold_in(stream_key, 1), (couples,), 0, 1 << 20) % (margin + 1)
    sizes = sizes.at[1:1 + 2 * couples:2].set(source_of - shifted).at[2:2 + 2 * couples:2].set(receiver + shifted)
    return sizes[jax.random.permutation(jax.random.fold_in(stream_key, 2), amount)]


def centred(own_key, extent, width, reach, pieces=(), held_as=jnp.bfloat16):
    factor_of = block_scale(own_key, extent, pieces, -0.22, 0.18) if pieces else 1.0
    array = jax.random.normal(own_key, extent, jnp.float32) * width * factor_of
    return jnp.minimum(jnp.maximum(array, -reach), reach).astype(held_as)


def setup_inputs(seed: int = 0) -> dict:
    keys = jax.random.split(jax.random.key(seed), 19)
    return {
        "layer_input": centred(keys[0], (N_DP, MICRO, SEQ, D), 1.0, 6.0, ((0, 2), (2, 16))),
        "cotangent": centred(keys[1], (N_DP, MICRO, SEQ, D), 1.0, 6.0, ((0, 2), (2, 16))),
        "doc_lengths": jax.vmap(lambda own: ragged(own, DOCS, SEQ, SEQ // 2, 2))(jax.random.split(keys[2], N_DP * MICRO)).reshape((N_DP, MICRO, DOCS)).astype(jnp.int32),
        "routes": picks_of(keys[3], N_DP * MICRO * SEQ, EXPERTS, TOP, 3072).reshape((N_DP, MICRO, SEQ, TOP)),
        "attention_gain": jnp.clip(1.0 + 0.18 * jax.random.normal(keys[4], (D,), jnp.float32), 0.099609375, 1.8984375).astype(jnp.bfloat16),
        "query_weight": centred(keys[5], (D, H * (NOPE + ROPE)), D ** -0.5, 0.125, ((0, 32),)),
        "latent_weight": centred(keys[6], (D, LAT + ROPE), D ** -0.5, 0.125, ((0, 32),)),
        "latent_gain": jnp.clip(1.0 + 0.18 * jax.random.normal(keys[7], (LAT,), jnp.float32), 0.099609375, 1.8984375).astype(jnp.bfloat16),
        "expand_weight": centred(keys[8], (LAT, H * (NOPE + VDIM)), LAT ** -0.5, 0.25, ((0, 32),)),
        "output_weight": centred(keys[9], (H * VDIM, D), (max(H * VDIM // 256, 1)) ** -0.5, 2.0, ((1, 32),)),
        "feed_gain": jnp.clip(1.0 + 0.18 * jax.random.normal(keys[10], (D,), jnp.float32), 0.099609375, 1.8984375).astype(jnp.bfloat16),
        "router_weight": centred(keys[11], (D, EXPERTS), (4 * D) ** -0.5, 0.0625, ((0, 32),)),
        "shared_gate": centred(keys[12], (D, FS), D ** -0.5, 0.125, ((0, 32),)),
        "shared_up": centred(keys[13], (D, FS), D ** -0.5, 0.125, ((0, 32),)),
        "shared_down": centred(keys[14], (FS, D), FS ** -0.5, 0.109375, ((0, 32),)),
        "expert_gate": centred(keys[15], (EXPERTS, D, FF), D ** -0.5, 0.125, ((0, 16), (1, 2))),
        "expert_up": centred(keys[16], (EXPERTS, D, FF), D ** -0.5, 0.125, ((0, 16), (1, 2))),
        "expert_down": centred(keys[17], (EXPERTS, FF, D), (max(FF // 256, 1)) ** -0.5, 2.5, ((0, 16), (2, 2))),
    }


EPSILON = 1e-06
NEGATIVE = -1e+30
HIGHEST_PRECISION = lax.Precision.HIGHEST

@jax.custom_vjp
def low(v):
    return lax.optimization_barrier(v.astype(jnp.bfloat16)).astype(jnp.float32)

@jax.custom_vjp
def low_back(v):
    return v

def low_keep(v):
    return (low(v), None)

def low_pass(kept, grad):
    return (grad,)

def back_keep(v):
    return (v, None)

def back_low(kept, grad):
    return (low(grad),)
low.defvjp(low_keep, low_pass)
low_back.defvjp(back_keep, back_low)

def root_normalize(values, gain):
    inverse = lax.rsqrt(lax.optimization_barrier(jnp.mean(values * values, axis=-1, keepdims=True)) + EPSILON)
    return values * inverse * gain

def angles(positions):
    half_width = ROPE // 2
    frequency = jnp.exp(jnp.arange(half_width, dtype=jnp.float32) * (-math.log(10000.0) / half_width))
    turned = positions.astype(jnp.float32)[:, None] * frequency[None, :]
    return (jnp.cos(turned), jnp.sin(turned))

def rotate(values, cosine_table, sine_table):
    half_width = values.shape[-1] // 2
    first = values[..., :half_width]
    second = values[..., half_width:]
    return jnp.concatenate([first * cosine_table - second * sine_table, first * sine_table + second * cosine_table], axis=-1)

def segment_of(positions, lengths):
    boundary = jnp.cumsum(lengths)
    return lax.optimization_barrier(jnp.sum((boundary[None, :] <= positions[:, None]).astype(jnp.int32), axis=1))

def slot_table(choices, experts_count, capacity):
    flattened = choices.reshape(-1)
    onehot = (flattened[:, None] == jnp.arange(experts_count, dtype=jnp.int32)[None, :]).astype(jnp.int32)
    earlier = jnp.cumsum(onehot, axis=0) - onehot
    ranking = lax.optimization_barrier(jnp.sum(earlier * onehot, axis=1))
    return (flattened * capacity + ranking, ranking < capacity)

def attend(queries, key_heads, values, segments):
    block_rows = min(512, SEQ)
    padded_keys = jnp.concatenate([jnp.zeros((WINDOW, H, NOPE + ROPE), jnp.float32), key_heads], axis=0)
    padded_values = jnp.concatenate([jnp.zeros((WINDOW, H, VDIM), jnp.float32), values], axis=0)
    padded_segments = jnp.concatenate([jnp.full((WINDOW,), -1, jnp.int32), segments], axis=0)
    score_scale = (NOPE + ROPE) ** (-0.5)

    def one_block(block_index):
        first_row = block_index * block_rows
        query_block = lax.dynamic_slice_in_dim(queries, first_row, block_rows, 0)
        key_block = lax.dynamic_slice_in_dim(padded_keys, first_row, WINDOW + block_rows, 0)
        value_block = lax.dynamic_slice_in_dim(padded_values, first_row, WINDOW + block_rows, 0)
        key_segments = lax.dynamic_slice_in_dim(padded_segments, first_row, WINDOW + block_rows, 0)
        query_segments = lax.dynamic_slice_in_dim(segments, first_row, block_rows, 0)
        distance = jnp.arange(block_rows, dtype=jnp.int32)[:, None] + WINDOW - jnp.arange(WINDOW + block_rows, dtype=jnp.int32)[None, :]
        allowed = (distance >= 0) & (distance < WINDOW) & (query_segments[:, None] == key_segments[None, :])
        scores = low_back(jnp.einsum('qhd,khd->hqk', query_block, key_block, precision=HIGHEST_PRECISION) * score_scale)
        weights = jax.nn.softmax(jnp.where(allowed[None], scores, NEGATIVE), axis=-1)
        mixture = jnp.einsum('hqk,khd->qhd', low(weights), value_block, precision=HIGHEST_PRECISION)
        return mixture.reshape(block_rows, H * VDIM)
    result = lax.map(jax.checkpoint(one_block), jnp.arange(SEQ // block_rows, dtype=jnp.int32))
    return result.reshape(SEQ, H * VDIM)

def pack_forward(weights, inputs, lengths, choices):
    attention_gain, query_weight, latent_weight, latent_gain, expand_weight, output_weight, feed_gain, router_weight, shared_gate, shared_up, shared_down, expert_gate, expert_up, expert_down = weights
    positions = jnp.arange(SEQ, dtype=jnp.int32)
    cosine_table, sine_table = angles(positions)
    hidden = low(root_normalize(inputs, attention_gain))
    query_heads = low_back(jnp.dot(hidden, query_weight, precision=HIGHEST_PRECISION)).reshape(SEQ, H, NOPE + ROPE)
    latent = low_back(jnp.dot(hidden, latent_weight, precision=HIGHEST_PRECISION))
    compressed = low(root_normalize(latent[:, :LAT], latent_gain))
    expanded = low_back(jnp.dot(compressed, expand_weight, precision=HIGHEST_PRECISION)).reshape(SEQ, H, NOPE + VDIM)
    key_rope = rotate(latent[:, LAT:], cosine_table, sine_table)
    queries = low(jnp.concatenate([query_heads[..., :NOPE], rotate(query_heads[..., NOPE:], cosine_table[:, None, :], sine_table[:, None, :])], axis=-1))
    key_heads = low(jnp.concatenate([expanded[..., :NOPE], jnp.broadcast_to(key_rope[:, None, :], (SEQ, H, ROPE))], axis=-1))
    values = low(expanded[..., NOPE:])
    mixture = low(low_back(attend(queries, key_heads, values, segment_of(positions, lengths))))
    residual = inputs + low_back(jnp.dot(mixture, output_weight, precision=HIGHEST_PRECISION))
    normed = low(root_normalize(residual, feed_gain))
    gate_projected = low_back(jnp.dot(normed, shared_gate, precision=HIGHEST_PRECISION))
    up_projected = low_back(jnp.dot(normed, shared_up, precision=HIGHEST_PRECISION))
    shared_act = low(jax.nn.silu(gate_projected) * up_projected)
    shared_out = low_back(jnp.dot(shared_act, shared_down, precision=HIGHEST_PRECISION))
    probabilities = jax.nn.softmax(low_back(jnp.dot(normed, router_weight, precision=HIGHEST_PRECISION)), axis=-1)

    def one_device(device_items):
        normed_rows, prob_rows, choice_rows = device_items
        slot_index, slot_kept = slot_table(choice_rows, EXPERTS, CAP)
        slots_total = EXPERTS * CAP
        matches = ((slot_index[:, None] == jnp.arange(slots_total, dtype=jnp.int32)[None, :]) & slot_kept[:, None]).astype(jnp.float32).reshape(TOK_MB, TOP, slots_total)
        chosen = (choice_rows[:, :, None] == jnp.arange(EXPERTS, dtype=jnp.int32)[None, None, :]).astype(jnp.float32)
        gate_values = lax.optimization_barrier(jnp.sum(chosen * prob_rows[:, None, :], axis=-1))
        picked = lax.optimization_barrier(jnp.sum(matches, axis=1))
        blending = lax.optimization_barrier(jnp.sum(matches * gate_values[:, :, None], axis=1))
        arrived = low_back(jnp.dot(picked.T, normed_rows, precision=HIGHEST_PRECISION)).reshape(EXPERTS, CAP, D)
        expert_gate_pre = low_back(jnp.einsum('ecd,edf->ecf', arrived, expert_gate, precision=HIGHEST_PRECISION))
        expert_up_pre = low_back(jnp.einsum('ecd,edf->ecf', arrived, expert_up, precision=HIGHEST_PRECISION))
        activation = low(jax.nn.silu(expert_gate_pre) * expert_up_pre)
        returned = low(low_back(jnp.einsum('ecf,efd->ecd', activation, expert_down, precision=HIGHEST_PRECISION))).reshape(slots_total, D)
        return jnp.dot(blending, returned, precision=HIGHEST_PRECISION)
    mixture_rows = lax.map(jax.checkpoint(one_device), (normed.reshape(N_EXPERT, TOK_MB, D), probabilities.reshape(N_EXPERT, TOK_MB, EXPERTS), choices.reshape(N_EXPERT, TOK_MB, TOP)))
    return residual + shared_out + mixture_rows.reshape(SEQ, D)

def reference(layer_input, cotangent, doc_lengths, routes, attention_gain, query_weight, latent_weight, latent_gain, expand_weight, output_weight, feed_gain, router_weight, shared_gate, shared_up, shared_down, expert_gate, expert_up, expert_down):
    weights = tuple((member.astype(jnp.float32) for member in (attention_gain, query_weight, latent_weight, latent_gain, expand_weight, output_weight, feed_gain, router_weight, shared_gate, shared_up, shared_down, expert_gate, expert_up, expert_down)))
    packs = layer_input.astype(jnp.float32).reshape(N_DP * MICRO, SEQ, D)
    lengths = doc_lengths.reshape(N_DP * MICRO, DOCS)
    choices = routes.reshape(N_DP * MICRO, SEQ, TOP)

    def forward(inputs, params):

        def one_pack(pack_items):
            return pack_forward(params, pack_items[0], pack_items[1], pack_items[2])
        return lax.map(jax.checkpoint(one_pack), (inputs, lengths, choices))
    output, pullback = jax.vjp(forward, packs, weights)
    input_grad, gradients = pullback(cotangent.astype(jnp.float32).reshape(N_DP * MICRO, SEQ, D))
    shape_full = layer_input.shape
    return (output.reshape(shape_full).astype(jnp.bfloat16), input_grad.reshape(shape_full), gradients[0], gradients[1], gradients[2], gradients[3], gradients[4], gradients[5], gradients[6], gradients[7], gradients[8], gradients[9], gradients[10], gradients[11], gradients[12], gradients[13])
```

```python
import math

import jax
import jax.numpy as jnp
from jax import lax
from jax.sharding import PartitionSpec as P

D = 2048
H = 16
NOPE = 128
ROPE = 64
VDIM = 128
LAT = 512
TOP = 6
WINDOW = 1024
MICRO = 2


EPSILON = 1e-06
NEGATIVE = -1e30
HIGHEST_PRECISION = lax.Precision.HIGHEST


def root_normalize(values, gain):
    inverse = lax.rsqrt(jnp.mean(values * values, axis=-1, keepdims=True) + EPSILON)
    return values * inverse * gain


def normalize_back(values, gain, incoming):
    result, pullback = jax.vjp(root_normalize, values, gain)
    return pullback(incoming)


def silu_product(left, right):
    return jax.nn.silu(left) * right


def silu_back(left, right, incoming):
    result, pullback = jax.vjp(silu_product, left, right)
    return pullback(incoming)


def angles(positions):
    half_width = ROPE // 2
    frequency = jnp.exp(
        jnp.arange(half_width, dtype=jnp.float32) * (-math.log(10000.0) / half_width)
    )
    turned = positions.astype(jnp.float32)[:, None] * frequency[None, :]
    return (jnp.cos(turned), jnp.sin(turned))


def rotate(values, cosine_table, sine_table):
    half_width = values.shape[-1] // 2
    first = values[..., :half_width]
    second = values[..., half_width:]
    return jnp.concatenate(
        [first * cosine_table - second * sine_table, first * sine_table + second * cosine_table],
        axis=-1,
    )


def segment_of(positions, lengths):
    boundary = jnp.cumsum(lengths)
    return jnp.sum((boundary[None, :] <= positions[:, None]).astype(jnp.int32), axis=1)


def transposed_left(left, right):
    return lax.dot_general(
        left, right, (((0,), (0,)), ((), ())), preferred_element_type=jnp.float32
    )


def transposed_right(left, right):
    return lax.dot_general(
        left, right, (((1,), (1,)), ((), ())), preferred_element_type=jnp.float32
    )


BOTH = ("dp", "expert")


def gather_all(x):
    return lax.all_gather(x, BOTH, axis=0, tiled=False)


def scatter_all(x):
    return lax.psum_scatter(x, BOTH, scatter_dimension=0, tiled=False)


def gather_plane(x):
    return lax.all_gather(x, "expert", axis=0, tiled=False)


def scatter_plane(x):
    return lax.psum_scatter(x, "expert", scatter_dimension=0, tiled=False)


def low(x):
    return x.astype(jnp.bfloat16)


def dot(a, b):
    return jnp.dot(a, b, preferred_element_type=jnp.float32)


def gather_dp(x, axis):
    size = lax.axis_size("dp")
    if size != 2:
        return lax.all_gather(x, "dp", axis=axis, tiled=True)
    other = lax.ppermute(x, "dp", [(0, 1), (1, 0)])
    first = lax.axis_index("dp") == 0
    return jnp.concatenate(
        [jnp.where(first, x, other), jnp.where(first, other, x)], axis=axis
    )


def scatter_dp(x, axis):
    size = lax.axis_size("dp")
    if size != 2:
        return lax.psum_scatter(low(x), "dp", scatter_dimension=axis, tiled=True).astype(
            jnp.float32
        )
    half = x.shape[axis] // 2
    index = lax.axis_index("dp")
    away = low(lax.dynamic_slice_in_dim(x, (1 - index) * half, half, axis))
    arrived = lax.ppermute(away, "dp", [(0, 1), (1, 0)])
    return lax.dynamic_slice_in_dim(x, index * half, half, axis) + arrived.astype(jnp.float32)


def attention_forward(queries, keys, values, allowed, score_scale):
    raw = jnp.einsum("mqhd,mkhd->mhqk", queries, keys, preferred_element_type=jnp.float32)
    scores = jnp.where(allowed[:, None], raw * score_scale, NEGATIVE)
    highest = jnp.max(scores, axis=-1, keepdims=True)
    log_total = highest + jnp.log(jnp.sum(jnp.exp(scores - highest), axis=-1, keepdims=True))
    weights = low(jnp.exp(scores - log_total))
    mixture = jnp.einsum("mhqk,mkhd->mqhd", weights, values, preferred_element_type=jnp.float32)
    return low(mixture), log_total


def attention_backward(queries, keys, values, allowed, score_scale, log_total, grad_mixture):
    raw = jnp.einsum("mqhd,mkhd->mhqk", queries, keys, preferred_element_type=jnp.float32)
    scores = jnp.where(allowed[:, None], raw * score_scale, NEGATIVE)
    probs = jnp.exp(scores - log_total)
    grad_probs = jnp.einsum(
        "mqhd,mkhd->mhqk", grad_mixture, values, preferred_element_type=jnp.float32
    )
    grad_scores = low(
        probs * (grad_probs - jnp.sum(grad_probs * probs, axis=-1, keepdims=True))
    )
    grad_queries = (
        jnp.einsum("mhqk,mkhd->mqhd", grad_scores, keys, preferred_element_type=jnp.float32)
        * score_scale
    )
    grad_keys = (
        jnp.einsum("mhqk,mqhd->mkhd", grad_scores, queries, preferred_element_type=jnp.float32)
        * score_scale
    )
    grad_values = jnp.einsum(
        "mhqk,mqhd->mkhd", low(probs), grad_mixture, preferred_element_type=jnp.float32
    )
    return grad_queries, grad_keys, grad_values


def body(
    layer_input,
    cotangent,
    doc_lengths,
    routes,
    attention_gain,
    query_weight,
    latent_weight,
    latent_gain,
    expand_weight,
    output_weight,
    feed_gain,
    router_weight,
    shared_gate,
    shared_up,
    shared_down,
    expert_gate,
    expert_up,
    expert_down,
):
    n_dp = lax.axis_size("dp")
    n_expert = lax.axis_size("expert")
    devices = n_dp * n_expert
    lane = lax.axis_index("expert")
    tokens = layer_input.shape[2]
    rows = MICRO * tokens
    experts_count = router_weight.shape[1]
    score_scale = (NOPE + ROPE) ** (-0.5)
    head_width = NOPE + ROPE
    key_width = H * head_width

    expert_gate = gather_dp(expert_gate[0], 0)
    expert_up = gather_dp(expert_up[0], 0)
    expert_down = gather_dp(expert_down[0], 1)
    shard = query_weight.shape[0]
    units = shared_down.shape[0]
    mine = n_dp * units
    both = jnp.stack([shared_gate, shared_up], axis=1).reshape(shard, 2, n_dp, n_expert, units)
    both = both.transpose(3, 0, 1, 2, 4).reshape(n_expert, shard, 2 * mine)
    both = lax.all_to_all(both, "expert", split_axis=0, concat_axis=0, tiled=True)
    shared_in = gather_dp(both.reshape(n_expert * shard, 2 * mine), 0)
    shared_out_weight = gather_dp(shared_down, 0)

    small_latent = latent_gain.shape[0]
    small = jnp.concatenate(
        [
            router_weight,
            attention_gain[:, None],
            feed_gain[:, None],
            jnp.pad(latent_gain, (0, shard - small_latent))[:, None],
        ],
        axis=1,
    )
    small = jnp.pad(small, ((0, 0), (0, 128 - small.shape[1])))
    all_query = gather_all(query_weight).reshape(D, key_width)
    all_latent = gather_all(latent_weight).reshape(D, LAT + ROPE)
    all_expand = gather_all(expand_weight).reshape(LAT, H * (NOPE + VDIM))
    all_output = gather_all(output_weight.T).reshape(D, H * VDIM)
    small = gather_all(small)
    gain_latent = small[:, :small_latent, experts_count + 2].reshape(LAT).astype(jnp.float32)
    small = small.reshape(D, 128)
    all_router = small[:, :experts_count]
    gain_first = small[:, experts_count].astype(jnp.float32)
    gain_second = small[:, experts_count + 1].astype(jnp.float32)

    positions = lane * tokens + jnp.arange(tokens, dtype=jnp.int32)
    cosine_table, sine_table = angles(positions)
    cosine_rows = jnp.tile(cosine_table, (MICRO, 1))
    sine_rows = jnp.tile(sine_table, (MICRO, 1))
    head_cosine = cosine_rows[:, None, :]
    head_sine = sine_rows[:, None, :]
    inputs = layer_input[0].reshape(rows, D).astype(jnp.float32)
    hidden = low(root_normalize(inputs, gain_first))
    latent = dot(hidden, all_latent)
    compressed = low(root_normalize(latent[:, :LAT], gain_latent))
    key_rope = low(rotate(latent[:, LAT:], cosine_rows, sine_rows))
    line = gather_plane(jnp.concatenate([compressed, key_rope], axis=1))
    query_heads = dot(hidden, all_query).reshape(rows, H, head_width)
    queries = low(
        jnp.concatenate(
            [query_heads[..., :NOPE], rotate(query_heads[..., NOPE:], head_cosine, head_sine)],
            axis=-1,
        )
    ).reshape(MICRO, tokens, H, head_width)
    reach = (WINDOW + tokens - 2) // tokens
    span = reach + 1
    key_rows = span * tokens
    line = jnp.concatenate(
        [jnp.zeros((reach,) + line.shape[1:], line.dtype), line], axis=0
    )
    window = lax.dynamic_slice_in_dim(line, lane, span, 0)
    window = window.reshape(span, MICRO, tokens, LAT + ROPE).transpose(1, 0, 2, 3)
    window = window.reshape(MICRO, key_rows, LAT + ROPE)
    window_latent = window[..., :LAT].reshape(MICRO * key_rows, LAT)
    expanded = low(dot(window_latent, all_expand)).reshape(MICRO, key_rows, H, NOPE + VDIM)
    keys = jnp.concatenate(
        [
            expanded[..., :NOPE],
            jnp.broadcast_to(window[:, :, None, LAT:], (MICRO, key_rows, H, ROPE)),
        ],
        axis=-1,
    )
    values = expanded[..., NOPE:]
    key_positions = (lane - reach) * tokens + jnp.arange(key_rows, dtype=jnp.int32)
    apart = positions[:, None] - key_positions[None, :]
    reachable = (key_positions[None, :] >= 0) & (apart >= 0) & (apart < WINDOW)
    allowed = jnp.stack(
        [
            reachable
            & (
                segment_of(positions, doc_lengths[0, m])[:, None]
                == segment_of(key_positions, doc_lengths[0, m])[None, :]
            )
            for m in range(MICRO)
        ]
    )
    mixture, log_total = attention_forward(queries, keys, values, allowed, score_scale)
    mixture = mixture.reshape(rows, H * VDIM)
    residual = inputs + transposed_right(mixture, all_output)
    normed = low(root_normalize(residual, gain_second))

    all_normed = gather_plane(normed).reshape(n_expert * rows, D)
    all_cotangent = gather_plane(cotangent[0].reshape(rows, D)).reshape(n_expert * rows, D)
    all_routes = gather_plane(routes[0].reshape(rows, TOP))
    total_rows = n_expert * rows
    capacity = (9 * tokens * TOP + 8 * experts_count - 1) // (8 * experts_count)
    per_group = max(1, 256 // tokens)
    group_rows = per_group * tokens
    groups = total_rows // group_rows
    slots = -(-per_group * capacity // 16) * 16
    named = jnp.any(all_routes == lane, axis=-1).reshape(-1, tokens).astype(jnp.int32)
    rank = jnp.cumsum(named, axis=1) - named
    kept = (named > 0) & (rank < capacity)
    offset = (jnp.arange(named.shape[0], dtype=jnp.int32) % per_group) * capacity
    place = jnp.where(kept, rank + offset[:, None], -1).reshape(groups, 1, group_rows)
    picked_bool = place == jnp.arange(slots, dtype=jnp.int32)[None, :, None]
    picked = picked_bool.astype(jnp.bfloat16)
    picked_float = picked_bool.astype(jnp.float32)
    probabilities = jax.nn.softmax(dot(all_normed, all_router), axis=-1)
    own_column = jnp.arange(experts_count, dtype=jnp.int32) == lane
    gate_rows = jnp.sum(jnp.where(own_column[None, :], probabilities, 0.0), axis=1)
    gate_slots = jnp.sum(
        picked_float * gate_rows.reshape(groups, 1, group_rows), axis=2
    ).reshape(groups * slots, 1)

    def to_slots(x):
        return low(
            jnp.einsum(
                "gst,gtd->gsd",
                picked,
                x.reshape(groups, group_rows, D),
                preferred_element_type=jnp.float32,
            )
        ).reshape(groups * slots, D)

    def from_slots(x):
        return jnp.einsum(
            "gst,gsd->gtd",
            picked,
            x.reshape(groups, slots, D),
            preferred_element_type=jnp.float32,
        ).reshape(total_rows, D)

    arrived = to_slots(all_normed)
    gate_pre = dot(arrived, expert_gate)
    up_pre = dot(arrived, expert_up)
    expert_act = low(silu_product(gate_pre, up_pre))
    expert_out = low(dot(expert_act, expert_down))
    shared_pre = dot(all_normed, shared_in)
    shared_act = low(silu_product(shared_pre[:, :mine], shared_pre[:, mine:]))
    partial_out = from_slots(low(gate_slots * expert_out.astype(jnp.float32))) + dot(
        shared_act, shared_out_weight
    )
    expert_sum = scatter_plane(low(partial_out).reshape(n_expert, rows, D))
    layer_output = low(residual + expert_sum.astype(jnp.float32))

    arrived_grad = to_slots(all_cotangent)
    gate_dots = jnp.sum(
        expert_out.astype(jnp.float32) * arrived_grad.astype(jnp.float32), axis=1
    ).reshape(groups, slots, 1)
    gate_grad_rows = jnp.sum(picked_float * gate_dots, axis=1).reshape(n_expert, rows)
    gate_grads = lax.all_to_all(
        gate_grad_rows, "expert", split_axis=0, concat_axis=0, tiled=True
    ).T
    slot_grad = low(gate_slots * arrived_grad.astype(jnp.float32))
    expert_down_grad = transposed_left(expert_act, slot_grad)
    gate_back, up_back = silu_back(gate_pre, up_pre, transposed_right(slot_grad, expert_down))
    gate_back = low(gate_back)
    up_back = low(up_back)
    expert_gate_grad = transposed_left(arrived, gate_back)
    expert_up_grad = transposed_left(arrived, up_back)
    rows_grad = low(
        transposed_right(gate_back, expert_gate) + transposed_right(up_back, expert_up)
    )
    shared_back = jnp.concatenate(
        silu_back(
            shared_pre[:, :mine],
            shared_pre[:, mine:],
            transposed_right(all_cotangent, shared_out_weight),
        ),
        axis=1,
    ).astype(jnp.bfloat16)
    partial_normed = from_slots(rows_grad) + transposed_right(shared_back, shared_in)
    grad_normed = scatter_plane(low(partial_normed).reshape(n_expert, rows, D)).astype(
        jnp.float32
    )
    shared_down_grad = scatter_dp(transposed_left(shared_act, all_cotangent), 0)
    shared_in_grad = scatter_dp(transposed_left(all_normed, shared_back), 0)
    shared_in_grad = lax.all_to_all(
        low(shared_in_grad).reshape(n_expert, shard, 2 * mine),
        "expert",
        split_axis=0,
        concat_axis=0,
        tiled=True,
    ).astype(jnp.float32)
    shared_in_grad = (
        shared_in_grad.reshape(n_expert, shard, 2, n_dp, units)
        .transpose(2, 1, 3, 0, 4)
        .reshape(2, shard, n_dp * n_expert * units)
    )
    expert_grads = (
        scatter_dp(expert_gate_grad, 0)[None],
        scatter_dp(expert_up_grad, 0)[None],
        scatter_dp(expert_down_grad, 1)[None],
    )

    own_probs = lax.dynamic_slice_in_dim(probabilities, lane * rows, rows, 0)
    logit_grad = low(
        own_probs * (gate_grads - jnp.sum(gate_grads * own_probs, axis=-1, keepdims=True))
    )
    router_weight_grad = transposed_left(normed, logit_grad)
    grad_normed = grad_normed + transposed_right(logit_grad, all_router)
    residual_extra, feed_gain_grad = normalize_back(residual, gain_second, grad_normed)
    grad_residual = cotangent[0].reshape(rows, D).astype(jnp.float32) + residual_extra

    grad_attn = low(grad_residual)
    output_grad = transposed_left(grad_attn, mixture)
    grad_mixture = low(dot(grad_attn, all_output)).reshape(MICRO, tokens, H, VDIM)
    grad_queries, grad_keys, grad_values = attention_backward(
        queries, keys, values, allowed, score_scale, log_total, grad_mixture
    )
    grad_queries = grad_queries.reshape(rows, H, head_width)
    grad_expanded = low(
        jnp.concatenate([grad_keys[..., :NOPE], grad_values], axis=-1)
    ).reshape(MICRO * key_rows, H * (NOPE + VDIM))
    expand_grad = transposed_left(window_latent, grad_expanded)
    grad_window = jnp.concatenate(
        [
            transposed_right(grad_expanded, all_expand).reshape(MICRO, key_rows, LAT),
            jnp.sum(grad_keys[..., NOPE:], axis=2),
        ],
        axis=-1,
    )
    grad_window = low(grad_window).reshape(MICRO, span, tokens, LAT + ROPE)
    grad_window = grad_window.transpose(1, 0, 2, 3).reshape(span, rows, LAT + ROPE)
    grad_line = lax.dynamic_update_slice_in_dim(
        jnp.zeros((n_expert + reach, rows, LAT + ROPE), jnp.bfloat16), grad_window, lane, 0
    )[reach:]
    grad_line = scatter_plane(grad_line).astype(jnp.float32)
    latent_part, latent_gain_grad = normalize_back(
        latent[:, :LAT], gain_latent, grad_line[:, :LAT]
    )
    grad_key_rope = rotate(grad_line[:, LAT:], cosine_rows, -sine_rows)
    grad_latent = low(jnp.concatenate([latent_part, grad_key_rope], axis=1))
    latent_grad = transposed_left(hidden, grad_latent)
    grad_query = low(
        jnp.concatenate(
            [
                grad_queries[..., :NOPE],
                rotate(grad_queries[..., NOPE:], head_cosine, -head_sine),
            ],
            axis=-1,
        ).reshape(rows, key_width)
    )
    query_grad = transposed_left(hidden, grad_query)
    grad_hidden = transposed_right(grad_latent, all_latent) + transposed_right(
        grad_query, all_query
    )
    input_extra, attention_gain_grad = normalize_back(inputs, gain_first, grad_hidden)
    input_grad = grad_residual + input_extra

    small_grad = jnp.concatenate(
        [
            router_weight_grad,
            attention_gain_grad[:, None],
            feed_gain_grad[:, None],
        ],
        axis=1,
    ).reshape(devices, shard, experts_count + 2)
    latent_column = jnp.pad(
        latent_gain_grad.reshape(devices, small_latent), ((0, 0), (0, shard - small_latent))
    )[:, :, None]
    small_grad = jnp.concatenate([small_grad, latent_column], axis=2)
    small_grad = jnp.pad(small_grad, ((0, 0), (0, 0), (0, 128 - small_grad.shape[2])))
    small_grad = scatter_all(small_grad)
    query_grad = scatter_all(low(query_grad).reshape(devices, shard, key_width))
    latent_grad = scatter_all(low(latent_grad).reshape(devices, shard, LAT + ROPE))
    expand_grad = scatter_all(
        low(expand_grad).reshape(devices, expand_weight.shape[0], expand_weight.shape[1])
    )
    output_grad = scatter_all(low(output_grad).reshape(devices, shard, H * VDIM))
    return (
        layer_output.reshape(1, MICRO, tokens, D),
        input_grad.reshape(1, MICRO, tokens, D),
        small_grad[:, experts_count],
        query_grad.astype(jnp.float32),
        latent_grad.astype(jnp.float32),
        small_grad[:small_latent, experts_count + 2],
        expand_grad.astype(jnp.float32),
        output_grad.astype(jnp.float32).T,
        small_grad[:, experts_count + 1],
        small_grad[:, :experts_count],
        shared_in_grad[0],
        shared_in_grad[1],
        shared_down_grad,
        expert_grads[0],
        expert_grads[1],
        expert_grads[2],
    )


def solution(mesh):
    placed = (
        P("dp", None, "expert", None),
        P("dp", None, "expert", None),
        P("dp", None, None),
        P("dp", None, "expert", None),
        P(("dp", "expert")),
        P(("dp", "expert"), None),
        P(("dp", "expert"), None),
        P(("dp", "expert")),
        P(("dp", "expert"), None),
        P(None, ("dp", "expert")),
        P(("dp", "expert")),
        P(("dp", "expert"), None),
        P(("dp", "expert"), None),
        P(("dp", "expert"), None),
        P(("dp", "expert"), None),
        P("expert", "dp", None),
        P("expert", "dp", None),
        P("expert", None, "dp"),
    )
    return jax.shard_map(
        body,
        mesh=mesh,
        in_specs=placed,
        out_specs=(
            P("dp", None, "expert", None),
            P("dp", None, "expert", None),
            P(("dp", "expert")),
            P(("dp", "expert"), None),
            P(("dp", "expert"), None),
            P(("dp", "expert")),
            P(("dp", "expert"), None),
            P(None, ("dp", "expert")),
            P(("dp", "expert")),
            P(("dp", "expert"), None),
            P(("dp", "expert"), None),
            P(("dp", "expert"), None),
            P(("dp", "expert"), None),
            P("expert", "dp", None),
            P("expert", "dp", None),
            P("expert", None, "dp"),
        ),
        check_vma=False,
    )
```

```python
import functools
import itertools
import math

import jax
import jax.numpy as jnp
from jax import lax
from jax.experimental import pallas as pl
from jax.experimental.pallas import tpu as pltpu
from jax.sharding import PartitionSpec as P

D = 2048
H = 16
NOPE = 128
ROPE = 64
VDIM = 128
LAT = 512
TOP = 6
WINDOW = 1024
MICRO = 2


EPSILON = 1e-06
NEGATIVE = -1e30
HIGHEST_PRECISION = lax.Precision.HIGHEST


def root_normalize(values, gain):
    inverse = lax.rsqrt(jnp.mean(values * values, axis=-1, keepdims=True) + EPSILON)
    return values * inverse * gain


def normalize_back(values, gain, incoming):
    result, pullback = jax.vjp(root_normalize, values, gain)
    return pullback(incoming)


def silu_product(left, right):
    return jax.nn.silu(left) * right


def silu_back(left, right, incoming):
    result, pullback = jax.vjp(silu_product, left, right)
    return pullback(incoming)


def angles(positions):
    half_width = ROPE // 2
    frequency = jnp.exp(
        jnp.arange(half_width, dtype=jnp.float32) * (-math.log(10000.0) / half_width)
    )
    turned = positions.astype(jnp.float32)[:, None] * frequency[None, :]
    return (jnp.cos(turned), jnp.sin(turned))


def rotate(values, cosine_table, sine_table):
    half_width = values.shape[-1] // 2
    first = values[..., :half_width]
    second = values[..., half_width:]
    return jnp.concatenate(
        [first * cosine_table - second * sine_table, first * sine_table + second * cosine_table],
        axis=-1,
    )


def segment_of(positions, lengths):
    boundary = jnp.cumsum(lengths)
    return jnp.sum((boundary[None, :] <= positions[:, None]).astype(jnp.int32), axis=1)


def transposed_left(left, right):
    return lax.dot_general(
        left, right, (((0,), (0,)), ((), ())), preferred_element_type=jnp.float32
    )


def transposed_right(left, right):
    return lax.dot_general(
        left, right, (((1,), (1,)), ((), ())), preferred_element_type=jnp.float32
    )


MESH_ID = pl.DeviceIdType.MESH
ANYWHERE = pl.BlockSpec(memory_space=pl.ANY)


def dims_of():
    n_expert = lax.axis_size("expert")
    core = 2 if n_expert % 2 == 0 else 1
    z = 4 if n_expert % (4 * core) == 0 else 1
    return {"x": lax.axis_size("dp"), "z": z, "y": n_expert // (z * core), "c": core}


def place_of(sizes):
    e = lax.axis_index("expert")
    return {
        "x": lax.axis_index("dp"),
        "z": e // (sizes["y"] * sizes["c"]),
        "y": (e // sizes["c"]) % sizes["y"],
        "c": e % sizes["c"],
    }


def expert_of(sizes, at):
    return (at["z"] * sizes["y"] + at["y"]) * sizes["c"] + at["c"]


def device_of(sizes, at):
    return (at["x"], expert_of(sizes, at))


def slot_of(sizes, at, whole):
    e = expert_of(sizes, at)
    if whole:
        return at["x"] * (sizes["z"] * sizes["y"] * sizes["c"]) + e
    return e


def nearest(p, k, size):
    if k == 0:
        return p
    if size == 2:
        return 1 - p
    if size == 4:
        return (1 + p % 2, (2 + 3 * p) % 5, 3 - 3 * (p // 2))[k - 1]
    return (p + k) % size


WEIGHT = {"z": 10, "y": 10, "x": 10, "c": 2}


def visits(order, sizes):
    every = itertools.product(*[range(sizes[d]) for d in order])
    return sorted(every, key=lambda ks: (sum(k * WEIGHT[d] for k, d in zip(ks, order)), ks))


def when(condition, action):
    if condition is True:
        action()
    else:
        pl.when(condition)(action)


def greet(names, sizes, at):
    barrier = pltpu.get_barrier_semaphore()
    around = []
    for d in names:
        for step in (1, -1):
            if sizes[d] == 2 and step == 1:
                around.append((True, dict(at, **{d: 1 - at[d]})))
            elif sizes[d] > 2:
                there = at[d] < sizes[d] - 1 if step == 1 else at[d] > 0
                around.append((there, dict(at, **{d: at[d] + step})))
    for there, to in around:
        when(
            there,
            lambda to=to: pl.semaphore_signal(
                barrier, inc=1, device_id=device_of(sizes, to), device_id_type=MESH_ID
            ),
        )
    pl.semaphore_wait(barrier, sum(1 if there is True else there.astype(jnp.int32) for there, _ in around))


def ways(ks, j, order, sizes, at, where):
    d = order[j]
    size = sizes[d]
    if size == 1 or any(ks[j + 1 :]):
        return
    p, q = at[d], where[d]
    if size == 2:
        if ks[j] == 0:
            yield 0, True, dict(at, **{d: 1 - p})
        return
    if ks[j] == 0:
        yield 0, p < size - 1, dict(at, **{d: p + 1})
        yield 1, p > 0, dict(at, **{d: p - 1})
    else:
        yield 0, (q < p) & (p < size - 1), dict(at, **{d: p + 1})
        yield 1, (q > p) & (p > 0), dict(at, **{d: p - 1})


def count_sends(order, sizes):
    total = 0
    zero = {d: 0 for d in order}
    for ks in visits(order, sizes):
        for j in range(len(order)):
            total += len(list(ways(ks, j, order, sizes, zero, zero)))
    return total


def gather_kernel(items, whole, sizes, *refs):
    arrays = items[-1][0] + 1
    count = len(items)
    orders = [order for _, _, order in items]
    ins = [part_of(refs[a], chunk) for a, chunk, _ in items]
    outs = [functools.partial(slot_part, refs[arrays + a], chunk) for a, chunk, _ in items]
    own_sem = refs[2 * arrays]
    sends = refs[2 * arrays + 1 : 2 * arrays + 1 + count]
    recvs = refs[2 * arrays + 1 + count :]
    at = place_of(sizes)
    names = sorted({d for order in orders for d in order})
    greet(names, sizes, at)
    me = slot_of(sizes, at, whole)
    keep = []
    for a in range(count):
        own = pltpu.make_async_copy(ins[a], outs[a](me), own_sem.at[a])
        own.start()
        keep.append(own)
    started = []
    plan = []
    for a, order in enumerate(orders):
        for rank, ks in enumerate(visits(order, sizes)):
            weight = sum(k * WEIGHT[d] for k, d in zip(ks, order))
            plan.append((weight, rank, a, ks))
    plan.sort(key=lambda item: item[:3])
    number = [0] * count
    for _, _, a, ks in plan:
        order = orders[a]
        where = dict(at)
        for d, k in zip(order, ks):
            where[d] = nearest(at[d], k, sizes[d])
        slot = slot_of(sizes, where, whole)
        here = outs[a](slot)
        if any(ks):
            pltpu.make_async_copy(here, here, recvs[a].at[slot]).wait()
            source = here
        else:
            source = ins[a]
        for j in reversed(range(len(order))):
            for _, there, to in ways(ks, j, order, sizes, at, where):
                copy = pltpu.make_async_remote_copy(
                    src_ref=source,
                    dst_ref=here,
                    send_sem=sends[a].at[number[a]],
                    recv_sem=recvs[a].at[slot],
                    device_id=device_of(sizes, to),
                    device_id_type=MESH_ID,
                )
                number[a] += 1
                when(there, copy.start)
                started.append((there, copy))
    for there, copy in started:
        when(there, copy.wait_send)
    for own in keep:
        own.wait()


def part_of(ref, chunk):
    return ref if chunk is None else ref.at[chunk]


def slot_part(ref, chunk, slot):
    return ref.at[slot] if chunk is None else ref.at[slot, chunk]


def items_of(orders, shapes):
    items = []
    for a, (order, shape) in enumerate(zip(orders, shapes)):
        if len(shape) == 2:
            items.append((a, None, order))
        else:
            for chunk in range(shape[0]):
                items.append((a, chunk, order[chunk] if isinstance(order, list) else order))
    return items


def gather(arrays, orders, whole, identity):
    sizes = dims_of()
    total = (sizes["x"] if whole else 1) * lax.axis_size("expert")
    items = items_of(orders, [a.shape for a in arrays])
    sent = total * sum(a.size * a.dtype.itemsize for a in arrays)
    return pl.pallas_call(
        functools.partial(gather_kernel, items, whole, sizes),
        out_shape=[jax.ShapeDtypeStruct((total,) + a.shape, a.dtype) for a in arrays],
        in_specs=[ANYWHERE] * len(arrays),
        out_specs=[ANYWHERE] * len(arrays),
        scratch_shapes=[pltpu.SemaphoreType.DMA((len(items),))]
        + [pltpu.SemaphoreType.DMA((count_sends(order, sizes),)) for _, _, order in items]
        + [pltpu.SemaphoreType.DMA((total,)) for _ in items],
        compiler_params=pltpu.CompilerParams(collective_id=identity, has_side_effects=True),
        cost_estimate=pl.CostEstimate(flops=0, bytes_accessed=sent * 6, transcendentals=0),
    )(*arrays)


def box_of(j, order, sizes, where, extra):
    base = 0
    for i in range(j):
        base += math.prod(sizes[d] for d in order[:i]) * boxes_along(sizes[order[i]])
    inner = 0
    for d in order[:j]:
        inner = inner * sizes[d] + where[d]
    wide = boxes_along(sizes[order[j]])
    last = 0 if wide == 1 else (sizes[order[j]] if extra else where[order[j]])
    return base + inner * wide + last


def boxes_along(size):
    return {1: 0, 2: 1}.get(size, size + 1)


def boxes(order, sizes):
    return sum(
        math.prod(sizes[d] for d in order[:i]) * boxes_along(sizes[order[i]])
        for i in range(len(order))
    )


def staged_of(order, sizes, where):
    inner = 0
    for d in order[:-1]:
        inner = inner * sizes[d] + where[d]
    return inner


def add_up(target, terms, dtype):
    rows = target.shape[0]
    step = 16 if rows % 16 == 0 else rows

    def one(i, carry):
        part = pl.ds(pl.multiple_of(i * step, step), step)
        total = terms[0][part, :].astype(jnp.float32)
        for term in terms[1:]:
            total = total + term[part, :].astype(jnp.float32)
        target[part, :] = total.astype(dtype)
        return carry

    lax.fori_loop(0, rows // step, one, 0)


def scatter_kernel(items, whole, sizes, *refs):
    arrays = items[-1][0] + 1
    count = len(items)
    orders = [order for _, _, order in items]
    ins = [functools.partial(slot_part, refs[a], chunk) for a, chunk, _ in items]
    outs = [part_of(refs[arrays + a], chunk) for a, chunk, _ in items]
    refs = refs[2 * arrays :]
    staged, landed, sends, recvs, loads = [
        refs[i * count : (i + 1) * count] for i in range(5)
    ]
    at = place_of(sizes)
    names = sorted({d for order in orders for d in order})
    plan = []
    for a, order in enumerate(orders):
        for rank, ks in enumerate(visits(order, sizes)):
            weight = sum(k * WEIGHT[d] for k, d in zip(ks, order))
            plan.append((weight, rank, a, ks))
    plan.sort(key=lambda item: item[:3], reverse=True)
    slots = {}
    for _, _, a, ks in plan:
        order = orders[a]
        where = dict(at)
        for d, k in zip(order, ks):
            where[d] = nearest(at[d], k, sizes[d])
        slots[a, ks] = (where, slot_of(sizes, where, whole))
    for _, _, a, ks in plan:
        if ks[-1] == 0:
            where, slot = slots[a, ks]
            index = staged_of(orders[a], sizes, where)
            pltpu.make_async_copy(
                ins[a](slot), staged[a].at[index], loads[a].at[index]
            ).start()
    greet(names, sizes, at)
    started = []
    number = [0] * count

    def send(a, source, box, to, there):
        copy = pltpu.make_async_remote_copy(
            src_ref=source,
            dst_ref=landed[a].at[box],
            send_sem=sends[a].at[number[a]],
            recv_sem=recvs[a].at[box],
            device_id=device_of(sizes, to),
            device_id_type=MESH_ID,
        )
        number[a] += 1
        when(there, copy.start)
        started.append((there, copy))

    for _, _, a, ks in plan:
        if ks[-1]:
            order = orders[a]
            where, slot = slots[a, ks]
            j = len(order) - 1
            to = dict(at, **{order[j]: 1 - at[order[j]]})
            send(a, ins[a](slot), box_of(j, order, sizes, where, False), to, True)
    for _, _, a, ks in plan:
        if ks[-1]:
            continue
        order = orders[a]
        where, slot = slots[a, ks]
        index = staged_of(order, sizes, where)
        mine = staged[a].at[index]
        pltpu.make_async_copy(ins[a](slot), mine, loads[a].at[index]).wait()
        leaves = max([j for j in range(len(order)) if ks[j]], default=-1)
        terms = [mine]
        loose = []
        for j in reversed(range(len(order))):
            d = order[j]
            if j < leaves or sizes[d] == 1:
                break
            if sizes[d] == 2:
                if ks[j] == 0:
                    box = box_of(j, order, sizes, where, False)
                    terms.append((box, True))
                continue
            p, q = at[d], where[d]
            if j == leaves:
                far = ((q > p) & (p > 0)) | ((q < p) & (p < sizes[d] - 1))
                terms.append((box_of(j, order, sizes, where, False), far))
            else:
                terms.append((box_of(j, order, sizes, where, False), p > 0))
                terms.append((box_of(j, order, sizes, where, True), p < sizes[d] - 1))
        sure = [mine]
        for box, there in terms[1:]:
            ref = landed[a].at[box]
            waiting = pltpu.make_async_copy(ref, ref, recvs[a].at[box])
            if there is True:
                waiting.wait()
                sure.append(ref)
            else:

                def take(ref=ref, waiting=waiting, mine=mine):
                    waiting.wait()
                    add_up(mine, [mine, ref], mine.dtype)

                loose.append((there, take))
        if len(sure) > 1 and leaves >= 0:
            add_up(mine, sure, mine.dtype)
            sure = [mine]
        for there, take in loose:
            when(there, take)
        if leaves < 0:
            add_up(outs[a], sure, outs[a].dtype)
            continue
        d = order[leaves]
        if sizes[d] == 2:
            send(
                a,
                mine,
                box_of(leaves, order, sizes, where, False),
                dict(at, **{d: 1 - at[d]}),
                True,
            )
        else:
            p, q = at[d], where[d]
            send(
                a, mine, box_of(leaves, order, sizes, where, False), dict(at, **{d: p + 1}), q > p
            )
            send(
                a,
                mine,
                jnp.where(
                    q + 1 == p,
                    box_of(leaves, order, sizes, where, True),
                    box_of(leaves, order, sizes, where, False),
                ),
                dict(at, **{d: p - 1}),
                q < p,
            )
    for there, copy in started:
        when(there, copy.wait_send)


def scatter_sends(order, sizes):
    total = 0
    for ks in visits(order, sizes):
        leaves = max([j for j in range(len(order)) if ks[j]], default=-1)
        if leaves >= 0:
            total += 1 if sizes[order[leaves]] == 2 else 2
    return total


def scatter(arrays, orders, whole, identity, out_dtype=jnp.float32):
    sizes = dims_of()
    items = items_of(orders, [a.shape[1:] for a in arrays])
    shapes = [arrays[a].shape[-2:] for a, _, _ in items]
    types = [arrays[a].dtype for a, _, _ in items]
    orders = [order for _, _, order in items]
    stages = [math.prod(sizes[d] for d in order[:-1]) for order in orders]
    landing = [boxes(order, sizes) for order in orders]
    return pl.pallas_call(
        functools.partial(scatter_kernel, items, whole, sizes),
        out_shape=[jax.ShapeDtypeStruct(a.shape[1:], out_dtype) for a in arrays],
        in_specs=[ANYWHERE] * len(arrays),
        out_specs=[pl.BlockSpec(memory_space=pltpu.VMEM)] * len(arrays),
        scratch_shapes=[pltpu.VMEM((n,) + s, t) for n, s, t in zip(stages, shapes, types)]
        + [pltpu.VMEM((n,) + s, t) for n, s, t in zip(landing, shapes, types)]
        + [pltpu.SemaphoreType.DMA((scatter_sends(order, sizes),)) for order in orders]
        + [pltpu.SemaphoreType.DMA((n,)) for n in landing]
        + [pltpu.SemaphoreType.DMA((n,)) for n in stages],
        compiler_params=pltpu.CompilerParams(
            collective_id=identity, has_side_effects=True, vmem_limit_bytes=60 << 20
        ),
    )(*arrays)


PLANE = ("z", "y", "c")
ZYX = ("z", "y", "x", "c")
ZXY = ("z", "x", "y", "c")
XYZ = ("x", "y", "z", "c")
YZ = ("y", "z", "c")
CHUNKS = 4
CHUNK_ORDERS = [PLANE, PLANE, PLANE, YZ]
ALL_ORDERS = [ZYX, XYZ, XYZ, ZXY, XYZ]


def gather_plane(x):
    return lax.all_gather(x, "expert", axis=0, tiled=False)


def scatter_plane(x):
    return lax.psum_scatter(x, "expert", scatter_dimension=0, tiled=False)


def low(x):
    return x.astype(jnp.bfloat16)


def dot(a, b):
    return jnp.dot(a, b, preferred_element_type=jnp.float32)


def gather_dp(x, axis):
    size = lax.axis_size("dp")
    if size != 2:
        return lax.all_gather(x, "dp", axis=axis, tiled=True)
    other = lax.ppermute(x, "dp", [(0, 1), (1, 0)])
    first = lax.axis_index("dp") == 0
    return jnp.concatenate(
        [jnp.where(first, x, other), jnp.where(first, other, x)], axis=axis
    )


def scatter_dp(x, axis):
    size = lax.axis_size("dp")
    if size != 2:
        return lax.psum_scatter(low(x), "dp", scatter_dimension=axis, tiled=True).astype(
            jnp.float32
        )
    half = x.shape[axis] // 2
    index = lax.axis_index("dp")
    away = low(lax.dynamic_slice_in_dim(x, (1 - index) * half, half, axis))
    arrived = lax.ppermute(away, "dp", [(0, 1), (1, 0)])
    return lax.dynamic_slice_in_dim(x, index * half, half, axis) + arrived.astype(jnp.float32)


def cross(a, b):
    return lax.dot_general(a, b, (((1,), (1,)), ((), ())), preferred_element_type=jnp.float32)


def heads_of(quads, rows, qn, qa, qb):
    lanes = lax.broadcasted_iota(jnp.int32, (1, qa.shape[1]), 1) // (ROPE // 2)
    ours = lanes == pl.program_id(0) % quads
    nothing = jnp.zeros((), qa.dtype)
    return (
        ours,
        qn[rows, :],
        jnp.where(ours, qa[rows, :], nothing),
        jnp.where(ours, qb[rows, :], nothing),
    )


def attend_kernel(tokens, scale, qn, qa, qb, latent, ka, kb, expand, bias, out):
    quads = qa.shape[1] // (ROPE // 2)
    for m in range(MICRO):
        rows = pl.ds(m * tokens, tokens)
        pair = low(dot(latent[m], expand[...]))
        keys, values = pair[:, :NOPE], pair[:, NOPE:]
        _, own, first, second = heads_of(quads, rows, qn, qa, qb)
        scores = cross(own, keys) + cross(first, ka[m]) + cross(second, kb[m])
        scores = scores * scale + bias[m]
        raised = jnp.exp(scores - jnp.max(scores, axis=1, keepdims=True))
        weights = low(raised / jnp.sum(raised, axis=1, keepdims=True))
        out[rows, :] = low(dot(weights, values))


def attend_back_kernel(
    tokens, scale, qn, qa, qb, grad, latent, turned, ka, kb, expand, bias, gqn, gqa, gqb, glat, gka, gkb, gexp
):
    head = pl.program_id(0)
    quads = qa.shape[1] // (ROPE // 2)

    @pl.when(head == 0)
    def _():
        glat[...] = jnp.zeros_like(glat)
        gka[...] = jnp.zeros_like(gka)
        gkb[...] = jnp.zeros_like(gkb)

    @pl.when(head % quads == 0)
    def _():
        gqa[...] = jnp.zeros_like(gqa)
        gqb[...] = jnp.zeros_like(gqb)

    expand_total = None
    for m in range(MICRO):
        rows = pl.ds(m * tokens, tokens)
        pair = low(dot(latent[m], expand[...]))
        keys, values = pair[:, :NOPE], pair[:, NOPE:]
        ours, own, first, second = heads_of(quads, rows, qn, qa, qb)
        grad_rows = grad[rows, :]
        scores = cross(keys, own) + cross(ka[m], first) + cross(kb[m], second)
        scores = scores * scale + bias[m]
        raised = jnp.exp(scores - jnp.max(scores, axis=0, keepdims=True))
        probs = raised / jnp.sum(raised, axis=0, keepdims=True)
        grad_probs = cross(values, grad_rows)
        shift = jnp.sum(grad_probs * probs, axis=0, keepdims=True)
        back = low(probs * (grad_probs - shift))
        across = back.T
        gqn[rows, :] = low(dot(across, keys) * scale)
        gqa[rows, :] += jnp.where(ours, dot(across, ka[m]) * scale, 0.0)
        gqb[rows, :] += jnp.where(ours, dot(across, kb[m]) * scale, 0.0)
        gka[m] += dot(back, first) * scale
        gkb[m] += dot(back, second) * scale
        both = jnp.concatenate(
            [low(dot(back, own) * scale), low(dot(low(probs), grad_rows))], axis=1
        )
        glat[m] += cross(both, expand[...])
        part = dot(turned[m], both)
        expand_total = part if expand_total is None else expand_total + part
    gexp[...] = low(expand_total)


def whole_block(a):
    return pl.BlockSpec(a.shape, lambda h: (0,) * len(a.shape))


def attention_specs(rows, quads):
    return [
        pl.BlockSpec((rows, NOPE), lambda h: (0, h)),
        pl.BlockSpec((rows, 128), lambda h: (0, h // quads)),
        pl.BlockSpec((rows, 128), lambda h: (0, h // quads)),
    ]


def attention_forward(tokens, scale, qn, qa, qb, latent, ka, kb, expand, bias):
    rows = qn.shape[0]
    quads = 128 // (ROPE // 2)
    return pl.pallas_call(
        functools.partial(attend_kernel, tokens, scale),
        grid=(H,),
        out_shape=jax.ShapeDtypeStruct((rows, H * VDIM), jnp.bfloat16),
        in_specs=attention_specs(rows, quads)
        + [whole_block(latent), whole_block(ka), whole_block(kb)]
        + [pl.BlockSpec((LAT, NOPE + VDIM), lambda h: (0, h)), whole_block(bias)],
        out_specs=pl.BlockSpec((rows, VDIM), lambda h: (0, h)),
        compiler_params=pltpu.CompilerParams(vmem_limit_bytes=56 << 20),
        cost_estimate=pl.CostEstimate(
            flops=25 * 10**9, bytes_accessed=20 * 10**6, transcendentals=0
        ),
    )(qn, qa, qb, latent, ka, kb, expand, bias)


def attention_backward(tokens, scale, qn, qa, qb, grad, latent, ka, kb, expand, bias):
    rows = qn.shape[0]
    quads = 128 // (ROPE // 2)
    turned = jnp.swapaxes(latent, 1, 2)
    single = jax.ShapeDtypeStruct
    return pl.pallas_call(
        functools.partial(attend_back_kernel, tokens, scale),
        grid=(H,),
        out_shape=[
            single(qn.shape, jnp.bfloat16),
            single(qa.shape, jnp.float32),
            single(qb.shape, jnp.float32),
            single(latent.shape, jnp.float32),
            single(ka.shape, jnp.float32),
            single(kb.shape, jnp.float32),
            single(expand.shape, jnp.bfloat16),
        ],
        in_specs=attention_specs(rows, quads)
        + [pl.BlockSpec((rows, VDIM), lambda h: (0, h))]
        + [whole_block(latent), whole_block(turned), whole_block(ka), whole_block(kb)]
        + [pl.BlockSpec((LAT, NOPE + VDIM), lambda h: (0, h)), whole_block(bias)],
        out_specs=attention_specs(rows, quads)
        + [whole_block(latent), whole_block(ka), whole_block(kb)]
        + [pl.BlockSpec((LAT, NOPE + VDIM), lambda h: (0, h))],
        compiler_params=pltpu.CompilerParams(vmem_limit_bytes=56 << 20),
        cost_estimate=pl.CostEstimate(
            flops=50 * 10**9, bytes_accessed=30 * 10**6, transcendentals=0
        ),
    )(qn, qa, qb, grad, latent, turned, ka, kb, expand, bias)


def combine_kernel(picked, rows, left, right, out):
    out[...] = low(dot(picked[0], rows[0]) + dot(left[...], right[...]))


def combine(picked, rows, left, right):
    groups, group_rows, slots = picked.shape
    total, inner = left.shape
    return pl.pallas_call(
        combine_kernel,
        grid=(groups,),
        out_shape=jax.ShapeDtypeStruct((total, D), jnp.bfloat16),
        in_specs=[
            pl.BlockSpec((1, group_rows, slots), lambda g: (g, 0, 0)),
            pl.BlockSpec((1, slots, D), lambda g: (g, 0, 0)),
            pl.BlockSpec((group_rows, inner), lambda g: (g, 0)),
            pl.BlockSpec((inner, D), lambda g: (0, 0)),
        ],
        out_specs=pl.BlockSpec((group_rows, D), lambda g: (g, 0)),
        compiler_params=pltpu.CompilerParams(vmem_limit_bytes=48 << 20),
        cost_estimate=pl.CostEstimate(
            flops=2 * total * (slots + inner) * D,
            bytes_accessed=total * D * 4,
            transcendentals=0,
        ),
    )(picked, rows.reshape(groups, slots, D), left, right)


def body(
    layer_input,
    cotangent,
    doc_lengths,
    routes,
    attention_gain,
    query_weight,
    latent_weight,
    latent_gain,
    expand_weight,
    output_weight,
    feed_gain,
    router_weight,
    shared_gate,
    shared_up,
    shared_down,
    expert_gate,
    expert_up,
    expert_down,
):
    n_dp = lax.axis_size("dp")
    n_expert = lax.axis_size("expert")
    devices = n_dp * n_expert
    lane = lax.axis_index("expert")
    tokens = layer_input.shape[2]
    rows = MICRO * tokens
    experts_count = router_weight.shape[1]
    score_scale = (NOPE + ROPE) ** (-0.5)
    head_width = NOPE + ROPE
    key_width = H * head_width

    shard = query_weight.shape[0]
    small_latent = latent_gain.shape[0]
    small = jnp.concatenate(
        [
            router_weight,
            attention_gain[:, None],
            feed_gain[:, None],
            jnp.pad(latent_gain, (0, shard - small_latent))[:, None],
        ],
        axis=1,
    )
    small = jnp.pad(small, ((0, 0), (0, 128 - small.shape[1])))
    by_head = query_weight.reshape(shard, H, head_width)
    split_query = jnp.concatenate(
        [
            by_head[..., :NOPE].reshape(shard, H * NOPE),
            by_head[..., NOPE : NOPE + ROPE // 2].reshape(shard, H * ROPE // 2),
            by_head[..., NOPE + ROPE // 2 :].reshape(shard, H * ROPE // 2),
        ],
        axis=1,
    )
    all_query, all_latent, all_expand, all_output, small = gather(
        [split_query, latent_weight, expand_weight.reshape(16, -1), output_weight.T, small],
        ALL_ORDERS,
        True,
        1,
    )
    all_query = all_query.reshape(D, key_width)
    all_latent = all_latent.reshape(D, LAT + ROPE)
    all_expand = all_expand.reshape(LAT, H * (NOPE + VDIM))
    all_output = all_output.reshape(D, H * VDIM)
    gain_latent = small[:, :small_latent, experts_count + 2].reshape(LAT).astype(jnp.float32)
    small = small.reshape(D, 128)
    all_router = small[:, :experts_count]
    gain_first = small[:, experts_count].astype(jnp.float32)
    gain_second = small[:, experts_count + 1].astype(jnp.float32)

    (later, all_query) = lax.optimization_barrier(
        ((expert_gate, expert_up, expert_down, shared_gate, shared_up, shared_down, cotangent), all_query)
    )
    expert_gate, expert_up, expert_down, shared_gate, shared_up, shared_down, sent_cotangent = later
    expert_gate = gather_dp(expert_gate[0], 0)
    expert_up = gather_dp(expert_up[0], 0)
    expert_down = gather_dp(expert_down[0], 1)
    units = shared_down.shape[0]
    mine = n_dp * units
    both = jnp.stack([shared_gate, shared_up], axis=1).reshape(shard, 2, n_dp, n_expert, units)
    both = both.transpose(3, 0, 1, 2, 4).reshape(n_expert, shard, 2 * mine)
    both = lax.all_to_all(both, "expert", split_axis=0, concat_axis=0, tiled=True)
    shared_in = gather_dp(both.reshape(n_expert * shard, 2 * mine), 0)
    padded = -(-(mine + experts_count) // 128) * 128
    rest = jnp.zeros((D, padded - mine - experts_count), jnp.bfloat16)
    shared_in = jnp.concatenate(
        [
            shared_in[:, :mine],
            all_router,
            rest,
            shared_in[:, mine:],
            jnp.zeros((D, padded - mine), jnp.bfloat16),
        ],
        axis=1,
    )
    shared_out_weight = jnp.pad(gather_dp(shared_down, 0), ((0, padded - mine), (0, 0)))


    positions = lane * tokens + jnp.arange(tokens, dtype=jnp.int32)
    cosine_table, sine_table = angles(positions)
    cosine_rows = jnp.tile(cosine_table, (MICRO, 1))
    sine_rows = jnp.tile(sine_table, (MICRO, 1))
    head_cosine = jnp.tile(cosine_rows, (1, H))
    head_sine = jnp.tile(sine_rows, (1, H))
    inputs = layer_input[0].reshape(rows, D).astype(jnp.float32)
    hidden = low(root_normalize(inputs, gain_first))
    latent = dot(hidden, all_latent)
    compressed = low(root_normalize(latent[:, :LAT], gain_latent))
    key_rope = low(rotate(latent[:, LAT:], cosine_rows, sine_rows))
    (line,) = gather([jnp.concatenate([compressed, key_rope], axis=1)], [PLANE], False, 2)
    query = dot(hidden, all_query)
    plain = H * NOPE
    half = H * ROPE // 2
    query_plain = low(query[:, :plain])
    turn_first = query[:, plain : plain + half]
    turn_second = query[:, plain + half :]
    query_first = low(turn_first * head_cosine - turn_second * head_sine)
    query_second = low(turn_first * head_sine + turn_second * head_cosine)
    reach = (WINDOW + tokens - 2) // tokens
    span = reach + 1
    key_rows = span * tokens
    line = jnp.concatenate(
        [jnp.zeros((reach,) + line.shape[1:], line.dtype), line], axis=0
    )
    window = lax.dynamic_slice_in_dim(line, lane, span, 0)
    window = window.reshape(span, MICRO, tokens, LAT + ROPE).transpose(1, 0, 2, 3)
    window = window.reshape(MICRO, key_rows, LAT + ROPE)
    window_latent = window[..., :LAT]
    quads = 128 // (ROPE // 2)
    key_first = jnp.tile(window[..., LAT : LAT + ROPE // 2], (1, 1, quads))
    key_second = jnp.tile(window[..., LAT + ROPE // 2 :], (1, 1, quads))
    key_positions = (lane - reach) * tokens + jnp.arange(key_rows, dtype=jnp.int32)
    apart = positions[:, None] - key_positions[None, :]
    reachable = (key_positions[None, :] >= 0) & (apart >= 0) & (apart < WINDOW)
    allowed = jnp.stack(
        [
            reachable
            & (
                segment_of(positions, doc_lengths[0, m])[:, None]
                == segment_of(key_positions, doc_lengths[0, m])[None, :]
            )
            for m in range(MICRO)
        ]
    )
    bias = jnp.where(allowed, 0.0, NEGATIVE).astype(jnp.float32)
    mixture = attention_forward(
        tokens,
        score_scale,
        query_plain,
        query_first,
        query_second,
        window_latent,
        key_first,
        key_second,
        all_expand,
        bias,
    )
    residual = inputs + transposed_right(mixture, all_output)
    normed = low(root_normalize(residual, gain_second))

    chunked = normed.reshape(CHUNKS, rows // CHUNKS, D)
    (all_normed,) = gather([chunked], [CHUNK_ORDERS], False, 3)
    all_normed = all_normed.reshape(n_expert * rows, D)
    all_cotangent = gather_plane(sent_cotangent[0].reshape(rows, D)).reshape(n_expert * rows, D)
    all_routes = gather_plane(routes[0].reshape(rows, TOP))
    total_rows = n_expert * rows
    capacity = (9 * tokens * TOP + 8 * experts_count - 1) // (8 * experts_count)
    per_group = max(1, 256 // tokens)
    group_rows = per_group * tokens
    groups = total_rows // group_rows
    slots = -(-per_group * capacity // 16) * 16
    named = jnp.any(all_routes == lane, axis=-1).reshape(-1, tokens).astype(jnp.int32)
    rank = jnp.cumsum(named, axis=1) - named
    kept = (named > 0) & (rank < capacity)
    offset = (jnp.arange(named.shape[0], dtype=jnp.int32) % per_group) * capacity
    place = jnp.where(kept, rank + offset[:, None], -1).reshape(groups, 1, group_rows)
    picked_bool = place == jnp.arange(slots, dtype=jnp.int32)[None, :, None]
    picked = picked_bool.astype(jnp.bfloat16)
    picked_float = picked_bool.astype(jnp.float32)
    shared_pre = dot(all_normed, shared_in)
    probabilities = jax.nn.softmax(shared_pre[:, mine : mine + experts_count], axis=-1)
    own_column = jnp.arange(experts_count, dtype=jnp.int32) == lane
    gate_rows = jnp.sum(jnp.where(own_column[None, :], probabilities, 0.0), axis=1)
    gate_slots = jnp.sum(
        picked_float * gate_rows.reshape(groups, 1, group_rows), axis=2
    ).reshape(groups * slots, 1)

    def to_slots(x):
        return low(
            jnp.einsum(
                "gst,gtd->gsd",
                picked,
                x.reshape(groups, group_rows, D),
                preferred_element_type=jnp.float32,
            )
        ).reshape(groups * slots, D)

    arrived = to_slots(all_normed)
    gate_pre = dot(arrived, expert_gate)
    up_pre = dot(arrived, expert_up)
    expert_act = low(silu_product(gate_pre, up_pre))
    expert_out = low(dot(expert_act, expert_down))
    shared_act = low(silu_product(shared_pre[:, :padded], shared_pre[:, padded:]))
    spread = jnp.swapaxes(picked, 1, 2)
    partial_out = combine(
        spread, low(gate_slots * expert_out.astype(jnp.float32)), shared_act, shared_out_weight
    )
    expert_sum = scatter_plane(partial_out.reshape(n_expert, rows, D))
    layer_output = low(residual + expert_sum.astype(jnp.float32))

    arrived_grad = to_slots(all_cotangent)
    gate_dots = jnp.sum(
        expert_out.astype(jnp.float32) * arrived_grad.astype(jnp.float32), axis=1
    ).reshape(groups, slots, 1)
    gate_grad_rows = jnp.sum(picked_float * gate_dots, axis=1).reshape(n_expert, rows)
    gate_grads = lax.all_to_all(
        gate_grad_rows, "expert", split_axis=0, concat_axis=0, tiled=True
    ).T
    slot_grad = low(gate_slots * arrived_grad.astype(jnp.float32))
    expert_down_grad = transposed_left(expert_act, slot_grad)
    gate_back, up_back = silu_back(gate_pre, up_pre, transposed_right(slot_grad, expert_down))
    gate_back = low(gate_back)
    up_back = low(up_back)
    expert_gate_grad = transposed_left(arrived, gate_back)
    expert_up_grad = transposed_left(arrived, up_back)
    rows_grad = low(
        transposed_right(gate_back, expert_gate) + transposed_right(up_back, expert_up)
    )
    shared_back = jnp.concatenate(
        silu_back(
            shared_pre[:, :padded],
            shared_pre[:, padded:],
            transposed_right(all_cotangent, shared_out_weight),
        ),
        axis=1,
    ).astype(jnp.bfloat16)
    no_router = jnp.concatenate(
        [
            shared_in[:, :mine],
            jnp.zeros((D, padded - mine), jnp.bfloat16),
            shared_in[:, padded:],
        ],
        axis=1,
    )
    partial_normed = combine(spread, rows_grad, shared_back, no_router.T)
    partial_normed = partial_normed.reshape(n_expert, CHUNKS, rows // CHUNKS, D)
    (grad_normed,) = scatter([partial_normed], [CHUNK_ORDERS], False, 4)
    grad_normed = grad_normed.reshape(rows, D)
    shared_down_grad = scatter_dp(transposed_left(shared_act, all_cotangent)[:mine], 0)
    shared_in_grad = scatter_dp(transposed_left(all_normed, shared_back), 0)
    shared_in_grad = jnp.concatenate(
        [shared_in_grad[:, :mine], shared_in_grad[:, padded : padded + mine]], axis=1
    )
    shared_in_grad = lax.all_to_all(
        low(shared_in_grad).reshape(n_expert, shard, 2 * mine),
        "expert",
        split_axis=0,
        concat_axis=0,
        tiled=True,
    ).astype(jnp.float32)
    shared_in_grad = (
        shared_in_grad.reshape(n_expert, shard, 2, n_dp, units)
        .transpose(2, 1, 3, 0, 4)
        .reshape(2, shard, n_dp * n_expert * units)
    )
    expert_grads = (
        scatter_dp(expert_gate_grad, 0)[None],
        scatter_dp(expert_up_grad, 0)[None],
        scatter_dp(expert_down_grad, 1)[None],
    )

    own_probs = lax.dynamic_slice_in_dim(probabilities, lane * rows, rows, 0)
    logit_grad = low(
        own_probs * (gate_grads - jnp.sum(gate_grads * own_probs, axis=-1, keepdims=True))
    )
    router_weight_grad = transposed_left(normed, logit_grad)
    grad_normed = grad_normed + transposed_right(logit_grad, all_router)
    residual_extra, feed_gain_grad = normalize_back(residual, gain_second, grad_normed)
    grad_residual = cotangent[0].reshape(rows, D).astype(jnp.float32) + residual_extra

    grad_attn = low(grad_residual)
    output_grad = transposed_left(grad_attn, mixture)
    grad_mixture = low(dot(grad_attn, all_output))
    grad_plain, grad_first, grad_second, grad_latents, grad_kfirst, grad_ksecond, expand_grad = (
        attention_backward(
            tokens,
            score_scale,
            query_plain,
            query_first,
            query_second,
            grad_mixture,
            window_latent,
            key_first,
            key_second,
            all_expand,
            jnp.swapaxes(bias, 1, 2),
        )
    )

    def folded(x):
        return jnp.sum(x.reshape(MICRO, key_rows, quads, ROPE // 2), axis=2)

    grad_window = jnp.concatenate(
        [grad_latents, folded(grad_kfirst), folded(grad_ksecond)], axis=-1
    )
    grad_window = low(grad_window).reshape(MICRO, span, tokens, LAT + ROPE)
    grad_window = grad_window.transpose(1, 0, 2, 3).reshape(span, rows, LAT + ROPE)
    grad_line = lax.dynamic_update_slice_in_dim(
        jnp.zeros((n_expert + reach, rows, LAT + ROPE), jnp.bfloat16), grad_window, lane, 0
    )[reach:]
    (grad_line,) = scatter([grad_line], [PLANE], False, 5)
    latent_part, latent_gain_grad = normalize_back(
        latent[:, :LAT], gain_latent, grad_line[:, :LAT]
    )
    grad_key_rope = rotate(grad_line[:, LAT:], cosine_rows, -sine_rows)
    grad_latent = low(jnp.concatenate([latent_part, grad_key_rope], axis=1))
    latent_grad = transposed_left(hidden, grad_latent)
    grad_query = jnp.concatenate(
        [
            grad_plain,
            low(grad_first * head_cosine + grad_second * head_sine),
            low(grad_second * head_cosine - grad_first * head_sine),
        ],
        axis=1,
    )
    query_grad = transposed_left(hidden, grad_query)
    grad_hidden = transposed_right(grad_latent, all_latent) + transposed_right(
        grad_query, all_query
    )
    input_extra, attention_gain_grad = normalize_back(inputs, gain_first, grad_hidden)
    input_grad = grad_residual + input_extra

    small_grad = jnp.concatenate(
        [
            router_weight_grad,
            attention_gain_grad[:, None],
            feed_gain_grad[:, None],
        ],
        axis=1,
    ).reshape(devices, shard, experts_count + 2)
    latent_column = jnp.pad(
        latent_gain_grad.reshape(devices, small_latent), ((0, 0), (0, shard - small_latent))
    )[:, :, None]
    small_grad = jnp.concatenate([small_grad, latent_column], axis=2)
    small_grad = jnp.pad(small_grad, ((0, 0), (0, 0), (0, 128 - small_grad.shape[2])))
    query_grad, latent_grad, expand_grad, output_grad, small_grad = scatter(
        [
            low(query_grad).reshape(devices, shard, key_width),
            low(latent_grad).reshape(devices, shard, LAT + ROPE),
            expand_grad.reshape(devices, 16, -1),
            low(output_grad).reshape(devices, shard, H * VDIM),
            low(small_grad),
        ],
        ALL_ORDERS,
        True,
        6,
    )
    query_grad = jnp.concatenate(
        [
            query_grad[:, :plain].reshape(shard, H, NOPE),
            query_grad[:, plain : plain + half].reshape(shard, H, ROPE // 2),
            query_grad[:, plain + half :].reshape(shard, H, ROPE // 2),
        ],
        axis=2,
    ).reshape(shard, key_width)
    return (
        layer_output.reshape(1, MICRO, tokens, D),
        input_grad.reshape(1, MICRO, tokens, D),
        small_grad[:, experts_count],
        query_grad,
        latent_grad,
        small_grad[:small_latent, experts_count + 2],
        expand_grad.reshape(expand_weight.shape),
        output_grad.T,
        small_grad[:, experts_count + 1],
        small_grad[:, :experts_count],
        shared_in_grad[0],
        shared_in_grad[1],
        shared_down_grad,
        expert_grads[0],
        expert_grads[1],
        expert_grads[2],
    )


def solution(mesh):
    placed = (
        P("dp", None, "expert", None),
        P("dp", None, "expert", None),
        P("dp", None, None),
        P("dp", None, "expert", None),
        P(("dp", "expert")),
        P(("dp", "expert"), None),
        P(("dp", "expert"), None),
        P(("dp", "expert")),
        P(("dp", "expert"), None),
        P(None, ("dp", "expert")),
        P(("dp", "expert")),
        P(("dp", "expert"), None),
        P(("dp", "expert"), None),
        P(("dp", "expert"), None),
        P(("dp", "expert"), None),
        P("expert", "dp", None),
        P("expert", "dp", None),
        P("expert", None, "dp"),
    )
    return jax.shard_map(
        body,
        mesh=mesh,
        in_specs=placed,
        out_specs=(
            P("dp", None, "expert", None),
            P("dp", None, "expert", None),
            P(("dp", "expert")),
            P(("dp", "expert"), None),
            P(("dp", "expert"), None),
            P(("dp", "expert")),
            P(("dp", "expert"), None),
            P(None, ("dp", "expert")),
            P(("dp", "expert")),
            P(("dp", "expert"), None),
            P(("dp", "expert"), None),
            P(("dp", "expert"), None),
            P(("dp", "expert"), None),
            P("expert", "dp", None),
            P("expert", "dp", None),
            P("expert", None, "dp"),
        ),
        check_vma=False,
    )
```

```python
import functools
import itertools
import math

import jax
import jax.numpy as jnp
from jax import lax
from jax.experimental import pallas as pl
from jax.experimental.pallas import tpu as pltpu
from jax.sharding import PartitionSpec as P

D = 2048
H = 16
NOPE = 128
ROPE = 64
VDIM = 128
LAT = 512
TOP = 6
WINDOW = 1024
MICRO = 2


EPSILON = 1e-06
NEGATIVE = -1e30
HIGHEST_PRECISION = lax.Precision.HIGHEST


def root_normalize(values, gain):
    inverse = lax.rsqrt(jnp.mean(values * values, axis=-1, keepdims=True) + EPSILON)
    return values * inverse * gain


def normalize_back(values, gain, incoming):
    result, pullback = jax.vjp(root_normalize, values, gain)
    return pullback(incoming)


def silu_product(left, right):
    return jax.nn.silu(left) * right


def silu_back(left, right, incoming):
    result, pullback = jax.vjp(silu_product, left, right)
    return pullback(incoming)


def angles(positions):
    half_width = ROPE // 2
    frequency = jnp.exp(
        jnp.arange(half_width, dtype=jnp.float32) * (-math.log(10000.0) / half_width)
    )
    turned = positions.astype(jnp.float32)[:, None] * frequency[None, :]
    return (jnp.cos(turned), jnp.sin(turned))


def rotate(values, cosine_table, sine_table):
    half_width = values.shape[-1] // 2
    first = values[..., :half_width]
    second = values[..., half_width:]
    return jnp.concatenate(
        [first * cosine_table - second * sine_table, first * sine_table + second * cosine_table],
        axis=-1,
    )


def segment_of(positions, lengths):
    boundary = jnp.cumsum(lengths)
    return jnp.sum((boundary[None, :] <= positions[:, None]).astype(jnp.int32), axis=1)


def transposed_left(left, right):
    return lax.dot_general(
        left, right, (((0,), (0,)), ((), ())), preferred_element_type=jnp.float32
    )


def transposed_right(left, right):
    return lax.dot_general(
        left, right, (((1,), (1,)), ((), ())), preferred_element_type=jnp.float32
    )


MESH_ID = pl.DeviceIdType.MESH
ANYWHERE = pl.BlockSpec(memory_space=pl.ANY)


def dims_of():
    n_expert = lax.axis_size("expert")
    core = 2 if n_expert % 2 == 0 else 1
    z = 4 if n_expert % (4 * core) == 0 else 1
    return {"x": lax.axis_size("dp"), "z": z, "y": n_expert // (z * core), "c": core}


def place_of(sizes):
    e = lax.axis_index("expert")
    return {
        "x": lax.axis_index("dp"),
        "z": e // (sizes["y"] * sizes["c"]),
        "y": (e // sizes["c"]) % sizes["y"],
        "c": e % sizes["c"],
    }


def expert_of(sizes, at):
    return (at["z"] * sizes["y"] + at["y"]) * sizes["c"] + at["c"]


def device_of(sizes, at):
    return (at["x"], expert_of(sizes, at))


def slot_of(sizes, at, order):
    e = expert_of(sizes, at)
    if "x" in order:
        return at["x"] * (sizes["z"] * sizes["y"] * sizes["c"]) + e
    return e


def nearest(p, k, size):
    if k == 0:
        return p
    if size == 2:
        return 1 - p
    if size == 4:
        return (1 + p % 2, (2 + 3 * p) % 5, 3 - 3 * (p // 2))[k - 1]
    return (p + k) % size


WEIGHT = {"z": 10, "y": 10, "x": 10, "c": 2}


def visits(order, sizes):
    every = itertools.product(*[range(sizes[d]) for d in order])
    return sorted(every, key=lambda ks: (sum(k * WEIGHT[d] for k, d in zip(ks, order)), ks))


def when(condition, action):
    if condition is True:
        action()
    else:
        pl.when(condition)(action)


def greet(names, sizes, at):
    barrier = pltpu.get_barrier_semaphore()
    around = []
    for d in names:
        for step in (1, -1):
            if sizes[d] == 2 and step == 1:
                around.append((True, dict(at, **{d: 1 - at[d]})))
            elif sizes[d] > 2:
                there = at[d] < sizes[d] - 1 if step == 1 else at[d] > 0
                around.append((there, dict(at, **{d: at[d] + step})))
    for there, to in around:
        when(
            there,
            lambda to=to: pl.semaphore_signal(
                barrier, inc=1, device_id=device_of(sizes, to), device_id_type=MESH_ID
            ),
        )
    pl.semaphore_wait(barrier, sum(1 if there is True else there.astype(jnp.int32) for there, _ in around))


def ways(ks, j, order, sizes, at, where):
    d = order[j]
    size = sizes[d]
    if size == 1 or any(ks[j + 1 :]):
        return
    p, q = at[d], where[d]
    if size == 2:
        if ks[j] == 0:
            yield 0, True, dict(at, **{d: 1 - p})
        return
    if ks[j] == 0:
        yield 0, p < size - 1, dict(at, **{d: p + 1})
        yield 1, p > 0, dict(at, **{d: p - 1})
    else:
        yield 0, (q < p) & (p < size - 1), dict(at, **{d: p + 1})
        yield 1, (q > p) & (p > 0), dict(at, **{d: p - 1})


def count_sends(order, sizes):
    total = 0
    zero = {d: 0 for d in order}
    for ks in visits(order, sizes):
        for j in range(len(order)):
            total += len(list(ways(ks, j, order, sizes, zero, zero)))
    return total


def gather_kernel(items, sizes, *refs):
    arrays = items[-1][0] + 1
    count = len(items)
    orders = [order for _, _, order in items]
    ins = [part_of(refs[a], chunk) for a, chunk, _ in items]
    outs = [functools.partial(slot_part, refs[arrays + a], chunk) for a, chunk, _ in items]
    own_sem = refs[2 * arrays]
    sends = refs[2 * arrays + 1 : 2 * arrays + 1 + count]
    recvs = refs[2 * arrays + 1 + count :]
    at = place_of(sizes)
    names = sorted({d for order in orders for d in order})
    greet(names, sizes, at)
    keep = []
    for a in range(count):
        me = slot_of(sizes, at, orders[a])
        own = pltpu.make_async_copy(ins[a], outs[a](me), own_sem.at[a])
        own.start()
        keep.append(own)
    started = []
    plan = []
    for a, order in enumerate(orders):
        for rank, ks in enumerate(visits(order, sizes)):
            weight = sum(k * WEIGHT[d] for k, d in zip(ks, order))
            plan.append((weight, rank, a, ks))
    plan.sort(key=lambda item: item[:3])
    number = [0] * count
    for _, _, a, ks in plan:
        order = orders[a]
        where = dict(at)
        for d, k in zip(order, ks):
            where[d] = nearest(at[d], k, sizes[d])
        slot = slot_of(sizes, where, order)
        here = outs[a](slot)
        if any(ks):
            pltpu.make_async_copy(here, here, recvs[a].at[slot]).wait()
            source = here
        else:
            source = ins[a]
        for j in reversed(range(len(order))):
            for _, there, to in ways(ks, j, order, sizes, at, where):
                copy = pltpu.make_async_remote_copy(
                    src_ref=source,
                    dst_ref=here,
                    send_sem=sends[a].at[number[a]],
                    recv_sem=recvs[a].at[slot],
                    device_id=device_of(sizes, to),
                    device_id_type=MESH_ID,
                )
                number[a] += 1
                when(there, copy.start)
                started.append((there, copy))
    for there, copy in started:
        when(there, copy.wait_send)
    for own in keep:
        own.wait()


def part_of(ref, chunk):
    return ref if chunk is None else ref.at[chunk]


def slot_part(ref, chunk, slot):
    return ref.at[slot] if chunk is None else ref.at[slot, chunk]


def items_of(orders, shapes):
    items = []
    for a, (order, shape) in enumerate(zip(orders, shapes)):
        if len(shape) == 2:
            items.append((a, None, order))
        else:
            for chunk in range(shape[0]):
                items.append((a, chunk, order[chunk] if isinstance(order, list) else order))
    return items


def members(sizes, order):
    return math.prod(sizes[d] for d in order)


def gather(arrays, orders, identity):
    sizes = dims_of()
    items = items_of(orders, [a.shape for a in arrays])
    totals = {a: members(sizes, order) for a, _, order in items}
    sent = sum(totals[i] * a.size * a.dtype.itemsize for i, a in enumerate(arrays))
    return pl.pallas_call(
        functools.partial(gather_kernel, items, sizes),
        out_shape=[jax.ShapeDtypeStruct((totals[i],) + a.shape, a.dtype) for i, a in enumerate(arrays)],
        in_specs=[ANYWHERE] * len(arrays),
        out_specs=[ANYWHERE] * len(arrays),
        scratch_shapes=[pltpu.SemaphoreType.DMA((len(items),))]
        + [pltpu.SemaphoreType.DMA((count_sends(order, sizes),)) for _, _, order in items]
        + [pltpu.SemaphoreType.DMA((totals[a],)) for a, _, _ in items],
        compiler_params=pltpu.CompilerParams(collective_id=identity, has_side_effects=True),
        cost_estimate=pl.CostEstimate(flops=0, bytes_accessed=sent * 6, transcendentals=0),
    )(*arrays)


def box_of(j, order, sizes, where, extra):
    base = 0
    for i in range(j):
        base += math.prod(sizes[d] for d in order[:i]) * boxes_along(sizes[order[i]])
    inner = 0
    for d in order[:j]:
        inner = inner * sizes[d] + where[d]
    wide = boxes_along(sizes[order[j]])
    last = 0 if wide == 1 else (sizes[order[j]] if extra else where[order[j]])
    return base + inner * wide + last


def boxes_along(size):
    return {1: 0, 2: 1}.get(size, size + 1)


def boxes(order, sizes):
    return sum(
        math.prod(sizes[d] for d in order[:i]) * boxes_along(sizes[order[i]])
        for i in range(len(order))
    )


def staged_of(order, sizes, where):
    inner = 0
    for d in order[:-1]:
        inner = inner * sizes[d] + where[d]
    return inner


def add_up(target, terms, dtype):
    rows = target.shape[0]
    step = 16 if rows % 16 == 0 else rows

    def one(i, carry):
        part = pl.ds(pl.multiple_of(i * step, step), step)
        total = terms[0][part, :].astype(jnp.float32)
        for term in terms[1:]:
            total = total + term[part, :].astype(jnp.float32)
        target[part, :] = total.astype(dtype)
        return carry

    lax.fori_loop(0, rows // step, one, 0)


def scatter_kernel(items, sizes, *refs):
    arrays = items[-1][0] + 1
    count = len(items)
    orders = [order for _, _, order in items]
    ins = [functools.partial(slot_part, refs[a], chunk) for a, chunk, _ in items]
    outs = [part_of(refs[arrays + a], chunk) for a, chunk, _ in items]
    refs = refs[2 * arrays :]
    staged, landed, sends, recvs, loads = [
        refs[i * count : (i + 1) * count] for i in range(5)
    ]
    at = place_of(sizes)
    names = sorted({d for order in orders for d in order})
    plan = []
    for a, order in enumerate(orders):
        for rank, ks in enumerate(visits(order, sizes)):
            weight = sum(k * WEIGHT[d] for k, d in zip(ks, order))
            plan.append((weight, rank, a, ks))
    plan.sort(key=lambda item: item[:3], reverse=True)
    slots = {}
    for _, _, a, ks in plan:
        order = orders[a]
        where = dict(at)
        for d, k in zip(order, ks):
            where[d] = nearest(at[d], k, sizes[d])
        slots[a, ks] = (where, slot_of(sizes, where, order))
    for _, _, a, ks in plan:
        if ks[-1] == 0:
            where, slot = slots[a, ks]
            index = staged_of(orders[a], sizes, where)
            pltpu.make_async_copy(
                ins[a](slot), staged[a].at[index], loads[a].at[index]
            ).start()
    greet(names, sizes, at)
    started = []
    number = [0] * count

    def send(a, source, box, to, there):
        copy = pltpu.make_async_remote_copy(
            src_ref=source,
            dst_ref=landed[a].at[box],
            send_sem=sends[a].at[number[a]],
            recv_sem=recvs[a].at[box],
            device_id=device_of(sizes, to),
            device_id_type=MESH_ID,
        )
        number[a] += 1
        when(there, copy.start)
        started.append((there, copy))

    for _, _, a, ks in plan:
        if ks[-1]:
            order = orders[a]
            where, slot = slots[a, ks]
            j = len(order) - 1
            to = dict(at, **{order[j]: 1 - at[order[j]]})
            send(a, ins[a](slot), box_of(j, order, sizes, where, False), to, True)
    for _, _, a, ks in plan:
        if ks[-1]:
            continue
        order = orders[a]
        where, slot = slots[a, ks]
        index = staged_of(order, sizes, where)
        mine = staged[a].at[index]
        pltpu.make_async_copy(ins[a](slot), mine, loads[a].at[index]).wait()
        leaves = max([j for j in range(len(order)) if ks[j]], default=-1)
        terms = [mine]
        loose = []
        for j in reversed(range(len(order))):
            d = order[j]
            if j < leaves or sizes[d] == 1:
                break
            if sizes[d] == 2:
                if ks[j] == 0:
                    box = box_of(j, order, sizes, where, False)
                    terms.append((box, True))
                continue
            p, q = at[d], where[d]
            if j == leaves:
                far = ((q > p) & (p > 0)) | ((q < p) & (p < sizes[d] - 1))
                terms.append((box_of(j, order, sizes, where, False), far))
            else:
                terms.append((box_of(j, order, sizes, where, False), p > 0))
                terms.append((box_of(j, order, sizes, where, True), p < sizes[d] - 1))
        sure = [mine]
        for box, there in terms[1:]:
            ref = landed[a].at[box]
            waiting = pltpu.make_async_copy(ref, ref, recvs[a].at[box])
            if there is True:
                waiting.wait()
                sure.append(ref)
            else:

                def take(ref=ref, waiting=waiting, mine=mine):
                    waiting.wait()
                    add_up(mine, [mine, ref], mine.dtype)

                loose.append((there, take))
        if len(sure) > 1 and leaves >= 0:
            add_up(mine, sure, mine.dtype)
            sure = [mine]
        for there, take in loose:
            when(there, take)
        if leaves < 0:
            add_up(outs[a], sure, outs[a].dtype)
            continue
        d = order[leaves]
        if sizes[d] == 2:
            send(
                a,
                mine,
                box_of(leaves, order, sizes, where, False),
                dict(at, **{d: 1 - at[d]}),
                True,
            )
        else:
            p, q = at[d], where[d]
            send(
                a, mine, box_of(leaves, order, sizes, where, False), dict(at, **{d: p + 1}), q > p
            )
            send(
                a,
                mine,
                jnp.where(
                    q + 1 == p,
                    box_of(leaves, order, sizes, where, True),
                    box_of(leaves, order, sizes, where, False),
                ),
                dict(at, **{d: p - 1}),
                q < p,
            )
    for there, copy in started:
        when(there, copy.wait_send)


def scatter_sends(order, sizes):
    total = 0
    for ks in visits(order, sizes):
        leaves = max([j for j in range(len(order)) if ks[j]], default=-1)
        if leaves >= 0:
            total += 1 if sizes[order[leaves]] == 2 else 2
    return total


def scatter(arrays, orders, identity, out_dtype=jnp.float32):
    sizes = dims_of()
    items = items_of(orders, [a.shape[1:] for a in arrays])
    shapes = [arrays[a].shape[-2:] for a, _, _ in items]
    types = [arrays[a].dtype for a, _, _ in items]
    orders = [order for _, _, order in items]
    stages = [math.prod(sizes[d] for d in order[:-1]) for order in orders]
    landing = [boxes(order, sizes) for order in orders]
    return pl.pallas_call(
        functools.partial(scatter_kernel, items, sizes),
        out_shape=[jax.ShapeDtypeStruct(a.shape[1:], out_dtype) for a in arrays],
        in_specs=[ANYWHERE] * len(arrays),
        out_specs=[pl.BlockSpec(memory_space=pltpu.VMEM)] * len(arrays),
        scratch_shapes=[pltpu.VMEM((n,) + s, t) for n, s, t in zip(stages, shapes, types)]
        + [pltpu.VMEM((n,) + s, t) for n, s, t in zip(landing, shapes, types)]
        + [pltpu.SemaphoreType.DMA((scatter_sends(order, sizes),)) for order in orders]
        + [pltpu.SemaphoreType.DMA((n,)) for n in landing]
        + [pltpu.SemaphoreType.DMA((n,)) for n in stages],
        compiler_params=pltpu.CompilerParams(
            collective_id=identity, has_side_effects=True, vmem_limit_bytes=60 << 20
        ),
    )(*arrays)


PLANE = ("z", "y", "c")
ZYX = ("z", "y", "x", "c")
ZXY = ("z", "x", "y", "c")
XYZ = ("x", "y", "z", "c")
YZ = ("y", "z", "c")
CHUNKS = 4
CHUNK_ORDERS = [PLANE, PLANE, PLANE, YZ]
YZX = ("y", "z", "x", "c")
ALL_ORDERS = [[ZYX, ZXY], YZX, XYZ, XYZ]


def gather_plane(x):
    return lax.all_gather(x, "expert", axis=0, tiled=False)


def scatter_plane(x):
    return lax.psum_scatter(x, "expert", scatter_dimension=0, tiled=False)


def low(x):
    return x.astype(jnp.bfloat16)


def wide(x):
    return x.astype(jnp.float32)


def dot(a, b):
    return jnp.dot(a, b, preferred_element_type=jnp.float32)


def fetch_dp(x, axis):
    if lax.axis_size("dp") != 2:
        return x, lax.all_gather(x, "dp", axis=axis, tiled=True)
    return x, lax.ppermute(x, "dp", [(0, 1), (1, 0)])


def joined(pair, axis):
    own, other = pair
    if lax.axis_size("dp") != 2:
        return other
    first = lax.axis_index("dp") == 0
    return jnp.concatenate(
        [jnp.where(first, own, other), jnp.where(first, other, own)], axis=axis
    )


def send_dp(x, axis):
    if lax.axis_size("dp") != 2:
        total = lax.psum_scatter(x, "dp", scatter_dimension=axis, tiled=True)
        return total, jnp.zeros_like(total)
    half = x.shape[axis] // 2
    index = lax.axis_index("dp")
    away = lax.dynamic_slice_in_dim(x, (1 - index) * half, half, axis)
    arrived = lax.ppermute(away, "dp", [(0, 1), (1, 0)])
    return lax.dynamic_slice_in_dim(x, index * half, half, axis), arrived


def added(pair):
    return pair[0].astype(jnp.float32) + pair[1].astype(jnp.float32)


def cross(a, b):
    return lax.dot_general(a, b, (((1,), (1,)), ((), ())), preferred_element_type=jnp.float32)


HEADS = 2


def spread_matrix(quads, dtype):
    half = ROPE // 2
    source = lax.broadcasted_iota(jnp.int32, (128, 256), 0)
    target = lax.broadcasted_iota(jnp.int32, (128, 256), 1)
    wanted = target % half + half * (target // (half * quads))
    return (source == wanted).astype(jnp.float32).astype(dtype)


def head_query(u, rows, qn, qa, qb):
    quads = qa.shape[1] // (ROPE // 2)
    lanes = lax.broadcasted_iota(jnp.int32, (1, qa.shape[1]), 1) // (ROPE // 2)
    ours = lanes == (pl.program_id(0) * HEADS + u) % quads
    nothing = jnp.zeros((), qa.dtype)
    parts = jnp.concatenate(
        [jnp.where(ours, qa[rows, :], nothing), jnp.where(ours, qb[rows, :], nothing)], axis=1
    )
    turned = low(cross(parts, spread_matrix(quads, jnp.bfloat16)))
    return ours, jnp.concatenate([qn[rows, u * NOPE : (u + 1) * NOPE], turned], axis=1)


def load_window(tokens, span, line, window, sems):
    lane = lax.axis_index("expert")
    copies = []
    for j in range(span):
        source = lane - (span - 1) + j
        rows = pl.ds(j * tokens, tokens)
        for m in range(MICRO):
            copy = pltpu.make_async_copy(
                line.at[jnp.maximum(source, 0), pl.ds(m * tokens, tokens)],
                window.at[m, rows],
                sems.at[m, j],
            )
            pl.when(source >= 0)(copy.start)
            copies.append((source >= 0, copy))

            @pl.when(source < 0)
            def _(m=m, rows=rows):
                window[m, rows] = jnp.zeros((tokens, window.shape[2]), window.dtype)

    left = window.shape[1] - span * tokens
    if left:
        for m in range(MICRO):
            window[m, pl.ds(span * tokens, left)] = jnp.zeros((left, window.shape[2]), window.dtype)
    for there, copy in copies:
        pl.when(there)(copy.wait)


def attend_kernel(tokens, span, scale, qn, qa, qb, line, expand, bias, out, window, sems):
    @pl.when(pl.program_id(0) == 0)
    def _():
        load_window(tokens, span, line, window, sems)

    for m in range(MICRO):
        rows = pl.ds(m * tokens, tokens)
        pairs = low(dot(window[m, :, :LAT], expand[...]))
        turns = window[m, :, LAT:]
        for u in range(HEADS):
            pair = pairs[:, u * (NOPE + VDIM) : (u + 1) * (NOPE + VDIM)]
            keys = jnp.concatenate([pair[:, :NOPE], turns], axis=1)
            _, own = head_query(u, rows, qn, qa, qb)
            scores = cross(own, keys) * scale + bias[m]
            raised = jnp.exp(scores - jnp.max(scores, axis=1, keepdims=True))
            weights = low(raised * (1.0 / jnp.sum(raised, axis=1, keepdims=True)))
            out[rows, u * VDIM : (u + 1) * VDIM] = low(dot(weights, pair[:, NOPE:]))


def attend_back_kernel(
    tokens, span, scale, qn, qa, qb, grad, line, expand, bias, gqn, gqa, gqb, gline, gexp, *scratch
):
    window, upright, glat, gturns, gwindow, zeros, sems, out_sems = scratch
    head = pl.program_id(0)
    quads = qa.shape[1] // (ROPE // 2)

    @pl.when(head == 0)
    def _():
        load_window(tokens, span, line, window, sems)
        for m in range(MICRO):
            upright[m] = window[m, :, :LAT].T
        glat[...] = jnp.zeros_like(glat)
        gturns[...] = jnp.zeros_like(gturns)

    @pl.when((head * HEADS) % quads == 0)
    def _():
        gqa[...] = jnp.zeros_like(gqa)
        gqb[...] = jnp.zeros_like(gqb)

    expand_total = None
    for m in range(MICRO):
        rows = pl.ds(m * tokens, tokens)
        pairs = low(dot(window[m, :, :LAT], expand[...]))
        turns = window[m, :, LAT:]
        grad_pairs = []
        turns_total = None
        for u in range(HEADS):
            pair = pairs[:, u * (NOPE + VDIM) : (u + 1) * (NOPE + VDIM)]
            keys = jnp.concatenate([pair[:, :NOPE], turns], axis=1)
            ours, own = head_query(u, rows, qn, qa, qb)
            grad_rows = grad[rows, u * VDIM : (u + 1) * VDIM]
            scores = cross(keys, own) * scale + bias[m]
            raised = jnp.exp(scores - jnp.max(scores, axis=0, keepdims=True))
            probs = raised * (1.0 / jnp.sum(raised, axis=0, keepdims=True))
            grad_probs = cross(pair[:, NOPE:], grad_rows)
            shift = jnp.sum(grad_probs * probs, axis=0, keepdims=True)
            back = low(probs * (grad_probs - shift))
            grad_own = dot(back.T, keys) * scale
            gqn[rows, u * NOPE : (u + 1) * NOPE] = low(grad_own[:, :NOPE])
            spread = lax.dot_general(
                grad_own[:, NOPE:],
                spread_matrix(quads, jnp.float32),
                (((1,), (0,)), ((), ())),
                precision=HIGHEST_PRECISION,
                preferred_element_type=jnp.float32,
            )
            gqa[rows, :] += jnp.where(ours, spread[:, :128], 0.0)
            gqb[rows, :] += jnp.where(ours, spread[:, 128:], 0.0)
            grad_keys = dot(back, own) * scale
            turned = grad_keys[:, NOPE:]
            turns_total = turned if turns_total is None else turns_total + turned
            grad_pairs.append(low(grad_keys[:, :NOPE]))
            grad_pairs.append(low(dot(low(probs), grad_rows)))
        gturns[m] += turns_total
        both = jnp.concatenate(grad_pairs, axis=1)
        glat[m] += cross(both, expand[...])
        part = dot(upright[m], both)
        expand_total = part if expand_total is None else expand_total + part
    gexp[...] = low(expand_total)

    @pl.when(head == pl.num_programs(0) - 1)
    def _():
        lane = lax.axis_index("expert")
        zeros[...] = jnp.zeros_like(zeros)
        for m in range(MICRO):
            gwindow[m, :, :LAT] = low(glat[m])
            gwindow[m, :, LAT:] = low(gturns[m])
        copies = []
        for slot in range(gline.shape[0]):
            j = slot - lane + span - 1
            inside = (j >= 0) & (j < span)
            start = pl.multiple_of(jnp.clip(j, 0, span - 1) * tokens, tokens)
            for m in range(MICRO):
                target = gline.at[slot, pl.ds(m * tokens, tokens)]
                sem = out_sems.at[slot, m]
                full = pltpu.make_async_copy(gwindow.at[m, pl.ds(start, tokens)], target, sem)
                empty = pltpu.make_async_copy(zeros, target, sem)
                pl.when(inside)(full.start)
                pl.when(jnp.logical_not(inside))(empty.start)
                copies.append(full)
        for copy in copies:
            copy.wait()


def whole_block(a):
    return pl.BlockSpec(a.shape, lambda h: (0,) * len(a.shape))


def attention_specs(rows, quads):
    return [
        pl.BlockSpec((rows, HEADS * NOPE), lambda h: (0, h)),
        pl.BlockSpec((rows, 128), lambda h: (0, h * HEADS // quads)),
        pl.BlockSpec((rows, 128), lambda h: (0, h * HEADS // quads)),
    ]


def attention_forward(tokens, span, scale, qn, qa, qb, line, expand, bias):
    rows = qn.shape[0]
    quads = 128 // (ROPE // 2)
    key_rows = bias.shape[2]
    return pl.pallas_call(
        functools.partial(attend_kernel, tokens, span, scale),
        grid=(H // HEADS,),
        out_shape=jax.ShapeDtypeStruct((rows, H * VDIM), jnp.bfloat16),
        in_specs=attention_specs(rows, quads)
        + [ANYWHERE, pl.BlockSpec((LAT, HEADS * (NOPE + VDIM)), lambda h: (0, h)), whole_block(bias)],
        out_specs=pl.BlockSpec((rows, HEADS * VDIM), lambda h: (0, h)),
        scratch_shapes=[
            pltpu.VMEM((MICRO, key_rows, line.shape[2]), jnp.bfloat16),
            pltpu.SemaphoreType.DMA((MICRO, span)),
        ],
        compiler_params=pltpu.CompilerParams(vmem_limit_bytes=56 << 20),
        cost_estimate=pl.CostEstimate(
            flops=25 * 10**9, bytes_accessed=20 * 10**6, transcendentals=0
        ),
    )(qn, qa, qb, line, expand, bias)


def attention_backward(tokens, span, scale, qn, qa, qb, grad, line, expand, bias):
    rows = qn.shape[0]
    quads = 128 // (ROPE // 2)
    key_rows = bias.shape[1]
    width = line.shape[2]
    single = jax.ShapeDtypeStruct
    return pl.pallas_call(
        functools.partial(attend_back_kernel, tokens, span, scale),
        grid=(H // HEADS,),
        out_shape=[
            single(qn.shape, jnp.bfloat16),
            single(qa.shape, jnp.float32),
            single(qb.shape, jnp.float32),
            single(line.shape, jnp.bfloat16),
            single(expand.shape, jnp.bfloat16),
        ],
        in_specs=attention_specs(rows, quads)
        + [pl.BlockSpec((rows, HEADS * VDIM), lambda h: (0, h)), ANYWHERE]
        + [pl.BlockSpec((LAT, HEADS * (NOPE + VDIM)), lambda h: (0, h)), whole_block(bias)],
        out_specs=attention_specs(rows, quads)
        + [ANYWHERE, pl.BlockSpec((LAT, HEADS * (NOPE + VDIM)), lambda h: (0, h))],
        scratch_shapes=[
            pltpu.VMEM((MICRO, key_rows, width), jnp.bfloat16),
            pltpu.VMEM((MICRO, LAT, key_rows), jnp.bfloat16),
            pltpu.VMEM((MICRO, key_rows, LAT), jnp.float32),
            pltpu.VMEM((MICRO, key_rows, 128), jnp.float32),
            pltpu.VMEM((MICRO, key_rows, width), jnp.bfloat16),
            pltpu.VMEM((tokens, width), jnp.bfloat16),
            pltpu.SemaphoreType.DMA((MICRO, span)),
            pltpu.SemaphoreType.DMA((line.shape[0], MICRO)),
        ],
        compiler_params=pltpu.CompilerParams(vmem_limit_bytes=56 << 20),
        cost_estimate=pl.CostEstimate(
            flops=60 * 10**9, bytes_accessed=30 * 10**6, transcendentals=0
        ),
    )(qn, qa, qb, grad, line, expand, bias)


def combine_kernel(picked, rows, left, right, out, below):
    inner = right.shape[0]

    @pl.when(pl.program_id(0) == 0)
    def _():
        below[pl.ds(0, inner), :] = right[...]

    below[pl.ds(inner, rows.shape[1]), :] = rows[0]
    out[...] = low(dot(jnp.concatenate([left[...], picked[0]], axis=1), below[...]))


def combine(picked, rows, left, right):
    groups, group_rows, slots = picked.shape
    total, inner = left.shape
    return pl.pallas_call(
        combine_kernel,
        grid=(groups,),
        out_shape=jax.ShapeDtypeStruct((total, D), jnp.bfloat16),
        in_specs=[
            pl.BlockSpec((1, group_rows, slots), lambda g: (g, 0, 0)),
            pl.BlockSpec((1, slots, D), lambda g: (g, 0, 0)),
            pl.BlockSpec((group_rows, inner), lambda g: (g, 0)),
            pl.BlockSpec((inner, D), lambda g: (0, 0)),
        ],
        out_specs=pl.BlockSpec((group_rows, D), lambda g: (g, 0)),
        scratch_shapes=[pltpu.VMEM((inner + slots, D), jnp.bfloat16)],
        compiler_params=pltpu.CompilerParams(vmem_limit_bytes=48 << 20),
        cost_estimate=pl.CostEstimate(
            flops=2 * total * (slots + inner) * D,
            bytes_accessed=total * D * 4,
            transcendentals=0,
        ),
    )(picked, rows.reshape(groups, slots, D), left, right)


def halves_of(x):
    parts = 2 if x.shape[0] % 32 == 0 else 1
    return x.reshape(parts, x.shape[0] // parts, x.shape[1])


def body(
    layer_input,
    cotangent,
    doc_lengths,
    routes,
    attention_gain,
    query_weight,
    latent_weight,
    latent_gain,
    expand_weight,
    output_weight,
    feed_gain,
    router_weight,
    shared_gate,
    shared_up,
    shared_down,
    expert_gate,
    expert_up,
    expert_down,
):
    n_dp = lax.axis_size("dp")
    n_expert = lax.axis_size("expert")
    devices = n_dp * n_expert
    lane = lax.axis_index("expert")
    tokens = layer_input.shape[2]
    rows = MICRO * tokens
    experts_count = router_weight.shape[1]
    score_scale = (NOPE + ROPE) ** (-0.5)
    head_width = NOPE + ROPE
    key_width = H * head_width

    shard = query_weight.shape[0]
    small_latent = latent_gain.shape[0]
    small = jnp.concatenate(
        [
            router_weight,
            attention_gain[:, None],
            feed_gain[:, None],
            jnp.pad(latent_gain, (0, shard - small_latent))[:, None],
        ],
        axis=1,
    )
    small = jnp.pad(small, ((0, 0), (0, 128 - small.shape[1])))
    by_head = query_weight.reshape(shard, H, head_width)
    split_query = jnp.concatenate(
        [
            by_head[..., :NOPE].reshape(shard, H * NOPE),
            by_head[..., NOPE : NOPE + ROPE // 2].reshape(shard, H * ROPE // 2),
            by_head[..., NOPE + ROPE // 2 :].reshape(shard, H * ROPE // 2),
        ],
        axis=1,
    )
    all_query, all_latent, all_expand, small = gather(
        [halves_of(split_query), latent_weight, expand_weight.reshape(16, -1), small],
        ALL_ORDERS,
        1,
    )
    all_query = all_query.reshape(D, key_width)
    all_latent = all_latent.reshape(D, LAT + ROPE)
    all_expand = all_expand.reshape(LAT, H * (NOPE + VDIM))
    gain_latent = small[:, :small_latent, experts_count + 2].reshape(LAT).astype(jnp.float32)
    small = small.reshape(D, 128)
    all_router = small[:, :experts_count]
    gain_first = small[:, experts_count].astype(jnp.float32)
    gain_second = small[:, experts_count + 1].astype(jnp.float32)

    (later, all_query) = lax.optimization_barrier(
        (
            (expert_gate, expert_up, expert_down, shared_gate, shared_up, shared_down, output_weight),
            all_query,
        )
    )
    expert_gate, expert_up, expert_down, shared_gate, shared_up, shared_down, output_weight = later
    all_output = lax.all_gather(output_weight.T, ("dp", "expert"), axis=0, tiled=True)
    parts_gate = fetch_dp(expert_gate[0], 0)
    parts_up = fetch_dp(expert_up[0], 0)
    parts_down = fetch_dp(expert_down[0], 1)
    units = shared_down.shape[0]
    mine = n_dp * units
    both = jnp.stack([shared_gate, shared_up], axis=1).reshape(shard, 2, n_dp, n_expert, units)
    both = both.transpose(3, 0, 1, 2, 4).reshape(n_expert, shard, 2 * mine)
    both = lax.all_to_all(both, "expert", split_axis=0, concat_axis=0, tiled=True)
    parts_in = fetch_dp(both.reshape(n_expert * shard, 2 * mine), 0)
    parts_out = fetch_dp(shared_down, 0)

    positions = lane * tokens + jnp.arange(tokens, dtype=jnp.int32)
    cosine_table, sine_table = angles(positions)
    cosine_rows = jnp.tile(cosine_table, (MICRO, 1))
    sine_rows = jnp.tile(sine_table, (MICRO, 1))
    head_cosine = jnp.tile(cosine_rows, (1, H))
    head_sine = jnp.tile(sine_rows, (1, H))
    inputs = layer_input[0].reshape(rows, D).astype(jnp.float32)
    hidden = low(root_normalize(inputs, gain_first))
    latent = dot(hidden, all_latent)
    compressed = low(root_normalize(latent[:, :LAT], gain_latent))
    key_rope = low(rotate(latent[:, LAT:], cosine_rows, sine_rows))
    payload = jnp.concatenate(
        [compressed, key_rope, jnp.zeros((rows, 128 - ROPE), jnp.bfloat16)], axis=1
    )
    columns = jnp.pad(routes[0].reshape(rows, TOP).T, ((0, 8 - TOP), (0, 0)))
    line, all_routes = gather([payload, columns], [PLANE, PLANE], 2)
    sent_cotangent, line = lax.optimization_barrier((cotangent, line))
    query = dot(hidden, all_query)
    plain = H * NOPE
    half = H * ROPE // 2
    query_plain = low(query[:, :plain])
    turn_first = query[:, plain : plain + half]
    turn_second = query[:, plain + half :]
    query_first = low(turn_first * head_cosine - turn_second * head_sine)
    query_second = low(turn_first * head_sine + turn_second * head_cosine)
    reach = (WINDOW + tokens - 2) // tokens
    span = reach + 1
    key_rows = -(-span * tokens // 128) * 128
    key_positions = (lane - reach) * tokens + jnp.arange(key_rows, dtype=jnp.int32)
    apart = positions[:, None] - key_positions[None, :]
    reachable = (key_positions[None, :] >= 0) & (apart >= 0) & (apart < WINDOW)
    allowed = jnp.stack(
        [
            reachable
            & (
                segment_of(positions, doc_lengths[0, m])[:, None]
                == segment_of(key_positions, doc_lengths[0, m])[None, :]
            )
            for m in range(MICRO)
        ]
    )
    bias = jnp.where(allowed, 0.0, NEGATIVE).astype(jnp.float32)
    mixture = attention_forward(
        tokens,
        span,
        score_scale,
        query_plain,
        query_first,
        query_second,
        line,
        all_expand,
        bias,
    )
    residual = inputs + transposed_right(mixture, all_output)
    normed = low(root_normalize(residual, gain_second))

    chunked = normed.reshape(CHUNKS, rows // CHUNKS, D)
    own_probs = jax.nn.softmax(dot(normed, all_router), axis=-1)
    all_normed, all_probs = gather([chunked, own_probs.T], [CHUNK_ORDERS, PLANE], 3)
    all_normed = all_normed.reshape(n_expert * rows, D)
    fetched = (parts_gate, parts_up, parts_down, parts_in, parts_out)
    all_normed, fetched = lax.optimization_barrier((all_normed, fetched))
    expert_gate, expert_up = joined(fetched[0], 0), joined(fetched[1], 0)
    expert_down = joined(fetched[2], 1)
    padded = -(-mine // 128) * 128
    shared_in = jnp.pad(
        joined(fetched[3], 0).reshape(D, 2, mine), ((0, 0), (0, 0), (0, padded - mine))
    ).reshape(D, 2 * padded)
    shared_out_weight = jnp.pad(joined(fetched[4], 0), ((0, padded - mine), (0, 0)))
    all_cotangent = gather_plane(sent_cotangent[0].reshape(rows, D)).reshape(n_expert * rows, D)
    total_rows = n_expert * rows
    capacity = (9 * tokens * TOP + 8 * experts_count - 1) // (8 * experts_count)
    per_group = max(1, 256 // tokens)
    group_rows = per_group * tokens
    groups = total_rows // group_rows
    slots = -(-per_group * capacity // 16) * 16
    named = jnp.any(all_routes[:, :TOP] == lane, axis=1).reshape(-1, tokens).astype(jnp.int32)
    rank = jnp.cumsum(named, axis=1) - named
    kept = (named > 0) & (rank < capacity)
    offset = (jnp.arange(named.shape[0], dtype=jnp.int32) % per_group) * capacity
    place = jnp.where(kept, rank + offset[:, None], -1).reshape(groups, 1, group_rows)
    picked_bool = place == jnp.arange(slots, dtype=jnp.int32)[None, :, None]
    picked = picked_bool.astype(jnp.bfloat16)
    picked_float = picked_bool.astype(jnp.float32)
    shared_pre = low(dot(all_normed, shared_in))
    gate_rows = lax.dynamic_index_in_dim(all_probs, lane, 1, keepdims=False)
    gate_slots = jnp.sum(
        picked_float * gate_rows.reshape(groups, 1, group_rows), axis=2
    ).reshape(groups * slots, 1)

    def to_slots(x):
        return low(
            jnp.einsum(
                "gst,gtd->gsd",
                picked,
                x.reshape(groups, group_rows, D),
                preferred_element_type=jnp.float32,
            )
        ).reshape(groups * slots, D)

    arrived = to_slots(all_normed)
    gate_pre = low(dot(arrived, expert_gate))
    up_pre = low(dot(arrived, expert_up))
    expert_act = low(silu_product(wide(gate_pre), wide(up_pre)))
    expert_out = low(dot(expert_act, expert_down))
    shared_act = low(silu_product(wide(shared_pre[:, :padded]), wide(shared_pre[:, padded:])))
    spread = jnp.swapaxes(picked, 1, 2)
    partial_out = combine(
        spread, low(gate_slots * expert_out.astype(jnp.float32)), shared_act, shared_out_weight
    )
    expert_sum = scatter_plane(partial_out.reshape(n_expert, rows, D))
    layer_output = low(residual + expert_sum.astype(jnp.float32))

    arrived_grad = to_slots(all_cotangent)
    gate_dots = jnp.sum(
        expert_out.astype(jnp.float32) * arrived_grad.astype(jnp.float32), axis=1
    ).reshape(groups, slots, 1)
    gate_grad_rows = jnp.sum(picked_float * gate_dots, axis=1).reshape(n_expert, rows)
    gate_grads = lax.all_to_all(
        gate_grad_rows, "expert", split_axis=0, concat_axis=0, tiled=True
    ).T
    slot_grad = low(gate_slots * arrived_grad.astype(jnp.float32))
    expert_down_grad = low(transposed_left(expert_act, slot_grad))
    gate_back, up_back = silu_back(
        wide(gate_pre), wide(up_pre), transposed_right(slot_grad, expert_down)
    )
    gate_back = low(gate_back)
    up_back = low(up_back)
    expert_gate_grad = low(transposed_left(arrived, gate_back))
    expert_up_grad = low(transposed_left(arrived, up_back))
    rows_grad = low(
        transposed_right(gate_back, expert_gate) + transposed_right(up_back, expert_up)
    )
    shared_back = jnp.concatenate(
        silu_back(
            wide(shared_pre[:, :padded]),
            wide(shared_pre[:, padded:]),
            transposed_right(all_cotangent, shared_out_weight),
        ),
        axis=1,
    ).astype(jnp.bfloat16)
    partial_normed = combine(spread, rows_grad, shared_back, shared_in.T)
    partial_normed = partial_normed.reshape(n_expert, CHUNKS, rows // CHUNKS, D)
    (grad_normed,) = scatter([partial_normed], [CHUNK_ORDERS], 4)
    grad_normed = grad_normed.reshape(rows, D)
    sums = [
        send_dp(expert_gate_grad, 0),
        send_dp(expert_up_grad, 0),
        send_dp(expert_down_grad, 1),
        send_dp(low(transposed_left(shared_act, all_cotangent)[:mine]), 0),
        send_dp(low(transposed_left(all_normed, shared_back)), 0),
    ]

    logit_grad = low(
        own_probs * (gate_grads - jnp.sum(gate_grads * own_probs, axis=-1, keepdims=True))
    )
    router_weight_grad = transposed_left(normed, logit_grad)
    grad_normed = grad_normed + transposed_right(logit_grad, all_router)
    residual_extra, feed_gain_grad = normalize_back(residual, gain_second, grad_normed)
    grad_residual = cotangent[0].reshape(rows, D).astype(jnp.float32) + residual_extra

    grad_attn = low(grad_residual)
    output_grad = low(transposed_left(grad_attn, mixture))
    output_grad = lax.psum_scatter(output_grad, ("dp", "expert"), scatter_dimension=0, tiled=True)
    grad_mixture = low(dot(grad_attn, all_output))
    grad_plain, grad_first, grad_second, grad_line, expand_grad = attention_backward(
        tokens,
        span,
        score_scale,
        query_plain,
        query_first,
        query_second,
        grad_mixture,
        line,
        all_expand,
        jnp.swapaxes(bias, 1, 2),
    )
    grad_query = jnp.concatenate(
        [
            grad_plain,
            low(grad_first * head_cosine + grad_second * head_sine),
            low(grad_second * head_cosine - grad_first * head_sine),
        ],
        axis=1,
    )
    query_grad = low(transposed_left(hidden, grad_query))
    grad_line, query_grad, expand_grad = scatter(
        [
            grad_line,
            query_grad.reshape(devices, shard, key_width),
            expand_grad.reshape(devices, 16, -1),
        ],
        [PLANE, ZYX, XYZ],
        5,
    )
    sums, grad_line = lax.optimization_barrier((sums, grad_line))
    expert_grads = [added(pair)[None] for pair in sums[:3]]
    shared_down_grad = added(sums[3])
    shared_in_grad = low(added(sums[4])).reshape(n_expert, shard, 2, padded)[..., :mine]
    shared_in_grad = lax.all_to_all(
        shared_in_grad.reshape(n_expert, shard, 2 * mine),
        "expert",
        split_axis=0,
        concat_axis=0,
        tiled=True,
    ).astype(jnp.float32)
    shared_in_grad = (
        shared_in_grad.reshape(n_expert, shard, 2, n_dp, units)
        .transpose(2, 1, 3, 0, 4)
        .reshape(2, shard, n_dp * n_expert * units)
    )
    latent_part, latent_gain_grad = normalize_back(
        latent[:, :LAT], gain_latent, grad_line[:, :LAT]
    )
    grad_key_rope = rotate(grad_line[:, LAT : LAT + ROPE], cosine_rows, -sine_rows)
    grad_latent = low(jnp.concatenate([latent_part, grad_key_rope], axis=1))
    latent_grad = transposed_left(hidden, grad_latent)
    grad_hidden = transposed_right(grad_latent, all_latent) + transposed_right(
        grad_query, all_query
    )
    input_extra, attention_gain_grad = normalize_back(inputs, gain_first, grad_hidden)
    input_grad = grad_residual + input_extra

    small_grad = jnp.concatenate(
        [
            router_weight_grad,
            attention_gain_grad[:, None],
            feed_gain_grad[:, None],
        ],
        axis=1,
    ).reshape(devices, shard, experts_count + 2)
    latent_column = jnp.pad(
        latent_gain_grad.reshape(devices, small_latent), ((0, 0), (0, shard - small_latent))
    )[:, :, None]
    small_grad = jnp.concatenate([small_grad, latent_column], axis=2)
    small_grad = jnp.pad(small_grad, ((0, 0), (0, 0), (0, 128 - small_grad.shape[2])))
    latent_grad, small_grad = scatter(
        [low(latent_grad).reshape(devices, shard, LAT + ROPE), low(small_grad)], [ZYX, ZXY], 6
    )
    query_grad = jnp.concatenate(
        [
            query_grad[:, :plain].reshape(shard, H, NOPE),
            query_grad[:, plain : plain + half].reshape(shard, H, ROPE // 2),
            query_grad[:, plain + half :].reshape(shard, H, ROPE // 2),
        ],
        axis=2,
    ).reshape(shard, key_width)
    return (
        layer_output.reshape(1, MICRO, tokens, D),
        input_grad.reshape(1, MICRO, tokens, D),
        small_grad[:, experts_count],
        query_grad,
        latent_grad,
        small_grad[:small_latent, experts_count + 2],
        expand_grad.reshape(expand_weight.shape),
        wide(output_grad).T,
        small_grad[:, experts_count + 1],
        small_grad[:, :experts_count],
        shared_in_grad[0],
        shared_in_grad[1],
        shared_down_grad,
        expert_grads[0],
        expert_grads[1],
        expert_grads[2],
    )


def solution(mesh):
    placed = (
        P("dp", None, "expert", None),
        P("dp", None, "expert", None),
        P("dp", None, None),
        P("dp", None, "expert", None),
        P(("dp", "expert")),
        P(("dp", "expert"), None),
        P(("dp", "expert"), None),
        P(("dp", "expert")),
        P(("dp", "expert"), None),
        P(None, ("dp", "expert")),
        P(("dp", "expert")),
        P(("dp", "expert"), None),
        P(("dp", "expert"), None),
        P(("dp", "expert"), None),
        P(("dp", "expert"), None),
        P("expert", "dp", None),
        P("expert", "dp", None),
        P("expert", None, "dp"),
    )
    return jax.shard_map(
        body,
        mesh=mesh,
        in_specs=placed,
        out_specs=(
            P("dp", None, "expert", None),
            P("dp", None, "expert", None),
            P(("dp", "expert")),
            P(("dp", "expert"), None),
            P(("dp", "expert"), None),
            P(("dp", "expert")),
            P(("dp", "expert"), None),
            P(None, ("dp", "expert")),
            P(("dp", "expert")),
            P(("dp", "expert"), None),
            P(("dp", "expert"), None),
            P(("dp", "expert"), None),
            P(("dp", "expert"), None),
            P("expert", "dp", None),
            P("expert", "dp", None),
            P("expert", None, "dp"),
        ),
        check_vma=False,
    )
```

```python
import functools
import itertools
import math

import jax
import jax.numpy as jnp
from jax import lax
from jax.experimental import pallas as pl
from jax.experimental.pallas import tpu as pltpu
from jax.sharding import PartitionSpec as P

D = 2048
H = 16
NOPE = 128
ROPE = 64
VDIM = 128
LAT = 512
TOP = 6
WINDOW = 1024
MICRO = 2


EPSILON = 1e-06
NEGATIVE = -1e30
HIGHEST_PRECISION = lax.Precision.HIGHEST


def root_normalize(values, gain):
    inverse = lax.rsqrt(jnp.mean(values * values, axis=-1, keepdims=True) + EPSILON)
    return values * inverse * gain


def normalize_back(values, gain, incoming):
    result, pullback = jax.vjp(root_normalize, values, gain)
    return pullback(incoming)


def silu_product(left, right):
    return jax.nn.silu(left) * right


def silu_back(left, right, incoming):
    result, pullback = jax.vjp(silu_product, left, right)
    return pullback(incoming)


def angles(positions):
    half_width = ROPE // 2
    frequency = jnp.exp(
        jnp.arange(half_width, dtype=jnp.float32) * (-math.log(10000.0) / half_width)
    )
    turned = positions.astype(jnp.float32)[:, None] * frequency[None, :]
    return (jnp.cos(turned), jnp.sin(turned))


def rotate(values, cosine_table, sine_table):
    half_width = values.shape[-1] // 2
    first = values[..., :half_width]
    second = values[..., half_width:]
    return jnp.concatenate(
        [first * cosine_table - second * sine_table, first * sine_table + second * cosine_table],
        axis=-1,
    )


def segment_of(positions, lengths):
    boundary = jnp.cumsum(lengths)
    return jnp.sum((boundary[None, :] <= positions[:, None]).astype(jnp.int32), axis=1)


def transposed_left(left, right):
    return lax.dot_general(
        left, right, (((0,), (0,)), ((), ())), preferred_element_type=jnp.float32
    )


def transposed_right(left, right):
    return lax.dot_general(
        left, right, (((1,), (1,)), ((), ())), preferred_element_type=jnp.float32
    )


MESH_ID = pl.DeviceIdType.MESH
ANYWHERE = pl.BlockSpec(memory_space=pl.ANY)


def dims_of():
    n_expert = lax.axis_size("expert")
    core = 2 if n_expert % 2 == 0 else 1
    z = 4 if n_expert % (4 * core) == 0 else 1
    return {"x": lax.axis_size("dp"), "z": z, "y": n_expert // (z * core), "c": core}


def place_of(sizes):
    e = lax.axis_index("expert")
    return {
        "x": lax.axis_index("dp"),
        "z": e // (sizes["y"] * sizes["c"]),
        "y": (e // sizes["c"]) % sizes["y"],
        "c": e % sizes["c"],
    }


def expert_of(sizes, at):
    return (at["z"] * sizes["y"] + at["y"]) * sizes["c"] + at["c"]


def device_of(sizes, at):
    return (at["x"], expert_of(sizes, at))


def slot_of(sizes, at, order):
    e = expert_of(sizes, at)
    if "x" in order:
        return at["x"] * (sizes["z"] * sizes["y"] * sizes["c"]) + e
    return e


def nearest(p, k, size):
    if k == 0:
        return p
    if size == 2:
        return 1 - p
    if size == 4:
        return (1 + p % 2, (2 + 3 * p) % 5, 3 - 3 * (p // 2))[k - 1]
    return (p + k) % size


WEIGHT = {"z": 10, "y": 10, "x": 10, "c": 2}


def visits(order, sizes):
    every = itertools.product(*[range(sizes[d]) for d in order])
    return sorted(every, key=lambda ks: (sum(k * WEIGHT[d] for k, d in zip(ks, order)), ks))


def when(condition, action):
    if condition is True:
        action()
    else:
        pl.when(condition)(action)


def greet(names, sizes, at):
    barrier = pltpu.get_barrier_semaphore()
    around = []
    for d in names:
        for step in (1, -1):
            if sizes[d] == 2 and step == 1:
                around.append((True, dict(at, **{d: 1 - at[d]})))
            elif sizes[d] > 2:
                there = at[d] < sizes[d] - 1 if step == 1 else at[d] > 0
                around.append((there, dict(at, **{d: at[d] + step})))
    for there, to in around:
        when(
            there,
            lambda to=to: pl.semaphore_signal(
                barrier, inc=1, device_id=device_of(sizes, to), device_id_type=MESH_ID
            ),
        )
    pl.semaphore_wait(barrier, sum(1 if there is True else there.astype(jnp.int32) for there, _ in around))


def ways(ks, j, order, sizes, at, where):
    d = order[j]
    size = sizes[d]
    if size == 1 or any(ks[j + 1 :]):
        return
    p, q = at[d], where[d]
    if size == 2:
        if ks[j] == 0:
            yield 0, True, dict(at, **{d: 1 - p})
        return
    if ks[j] == 0:
        yield 0, p < size - 1, dict(at, **{d: p + 1})
        yield 1, p > 0, dict(at, **{d: p - 1})
    else:
        yield 0, (q < p) & (p < size - 1), dict(at, **{d: p + 1})
        yield 1, (q > p) & (p > 0), dict(at, **{d: p - 1})


def count_sends(order, sizes):
    total = 0
    zero = {d: 0 for d in order}
    for ks in visits(order, sizes):
        for j in range(len(order)):
            total += len(list(ways(ks, j, order, sizes, zero, zero)))
    return total


def gather_kernel(items, sizes, *refs):
    arrays = items[-1][0] + 1
    count = len(items)
    orders = [order for _, _, order in items]
    ins = [part_of(refs[a], chunk) for a, chunk, _ in items]
    outs = [functools.partial(slot_part, refs[arrays + a], chunk) for a, chunk, _ in items]
    own_sem = refs[2 * arrays]
    sends = refs[2 * arrays + 1 : 2 * arrays + 1 + count]
    recvs = refs[2 * arrays + 1 + count :]
    at = place_of(sizes)
    names = sorted({d for order in orders for d in order})
    greet(names, sizes, at)
    keep = []
    for a in range(count):
        me = slot_of(sizes, at, orders[a])
        own = pltpu.make_async_copy(ins[a], outs[a](me), own_sem.at[a])
        own.start()
        keep.append(own)
    started = []
    plan = []
    for a, order in enumerate(orders):
        for rank, ks in enumerate(visits(order, sizes)):
            weight = sum(k * WEIGHT[d] for k, d in zip(ks, order))
            plan.append((weight, rank, a, ks))
    plan.sort(key=lambda item: item[:3])
    number = [0] * count
    for _, _, a, ks in plan:
        order = orders[a]
        where = dict(at)
        for d, k in zip(order, ks):
            where[d] = nearest(at[d], k, sizes[d])
        slot = slot_of(sizes, where, order)
        here = outs[a](slot)
        if any(ks):
            pltpu.make_async_copy(here, here, recvs[a].at[slot]).wait()
            source = here
        else:
            source = ins[a]
        for j in reversed(range(len(order))):
            for _, there, to in ways(ks, j, order, sizes, at, where):
                copy = pltpu.make_async_remote_copy(
                    src_ref=source,
                    dst_ref=here,
                    send_sem=sends[a].at[number[a]],
                    recv_sem=recvs[a].at[slot],
                    device_id=device_of(sizes, to),
                    device_id_type=MESH_ID,
                )
                number[a] += 1
                when(there, copy.start)
                started.append((there, copy))
    for there, copy in started:
        when(there, copy.wait_send)
    for own in keep:
        own.wait()


def part_of(ref, chunk):
    return ref if chunk is None else ref.at[chunk]


def slot_part(ref, chunk, slot):
    return ref.at[slot] if chunk is None else ref.at[slot, chunk]


def items_of(orders, shapes):
    items = []
    for a, (order, shape) in enumerate(zip(orders, shapes)):
        if len(shape) == 2:
            items.append((a, None, order))
        else:
            for chunk in range(shape[0]):
                items.append((a, chunk, order[chunk] if isinstance(order, list) else order))
    return items


def members(sizes, order):
    return math.prod(sizes[d] for d in order)


def gather(arrays, orders, identity):
    sizes = dims_of()
    items = items_of(orders, [a.shape for a in arrays])
    totals = {a: members(sizes, order) for a, _, order in items}
    sent = sum(totals[i] * a.size * a.dtype.itemsize for i, a in enumerate(arrays))
    return pl.pallas_call(
        functools.partial(gather_kernel, items, sizes),
        out_shape=[jax.ShapeDtypeStruct((totals[i],) + a.shape, a.dtype) for i, a in enumerate(arrays)],
        in_specs=[ANYWHERE] * len(arrays),
        out_specs=[ANYWHERE] * len(arrays),
        scratch_shapes=[pltpu.SemaphoreType.DMA((len(items),))]
        + [pltpu.SemaphoreType.DMA((count_sends(order, sizes),)) for _, _, order in items]
        + [pltpu.SemaphoreType.DMA((totals[a],)) for a, _, _ in items],
        compiler_params=pltpu.CompilerParams(collective_id=identity, has_side_effects=True),
        cost_estimate=pl.CostEstimate(flops=0, bytes_accessed=sent // 16, transcendentals=0),
    )(*arrays)


def box_of(j, order, sizes, where, extra):
    base = 0
    for i in range(j):
        base += math.prod(sizes[d] for d in order[:i]) * boxes_along(sizes[order[i]])
    inner = 0
    for d in order[:j]:
        inner = inner * sizes[d] + where[d]
    wide = boxes_along(sizes[order[j]])
    last = 0 if wide == 1 else (sizes[order[j]] if extra else where[order[j]])
    return base + inner * wide + last


def boxes_along(size):
    return {1: 0, 2: 1}.get(size, size + 1)


def boxes(order, sizes):
    return sum(
        math.prod(sizes[d] for d in order[:i]) * boxes_along(sizes[order[i]])
        for i in range(len(order))
    )


def staged_of(order, sizes, where):
    inner = 0
    for d in order[:-1]:
        inner = inner * sizes[d] + where[d]
    return inner


def add_up(target, terms, dtype):
    rows = target.shape[0]
    step = 16 if rows % 16 == 0 else rows

    def one(i, carry):
        part = pl.ds(pl.multiple_of(i * step, step), step)
        total = terms[0][part, :].astype(jnp.float32)
        for term in terms[1:]:
            total = total + term[part, :].astype(jnp.float32)
        target[part, :] = total.astype(dtype)
        return carry

    lax.fori_loop(0, rows // step, one, 0)


def scatter_kernel(items, sizes, *refs):
    arrays = items[-1][0] + 1
    count = len(items)
    orders = [order for _, _, order in items]
    ins = [functools.partial(slot_part, refs[a], chunk) for a, chunk, _ in items]
    outs = [part_of(refs[arrays + a], chunk) for a, chunk, _ in items]
    refs = refs[2 * arrays :]
    staged, landed, sends, recvs, loads = [
        refs[i * count : (i + 1) * count] for i in range(5)
    ]
    at = place_of(sizes)
    names = sorted({d for order in orders for d in order})
    plan = []
    for a, order in enumerate(orders):
        for rank, ks in enumerate(visits(order, sizes)):
            weight = sum(k * WEIGHT[d] for k, d in zip(ks, order))
            plan.append((weight, rank, a, ks))
    plan.sort(key=lambda item: item[:3], reverse=True)
    slots = {}
    for _, _, a, ks in plan:
        order = orders[a]
        where = dict(at)
        for d, k in zip(order, ks):
            where[d] = nearest(at[d], k, sizes[d])
        slots[a, ks] = (where, slot_of(sizes, where, order))
    for _, _, a, ks in plan:
        if ks[-1] == 0:
            where, slot = slots[a, ks]
            index = staged_of(orders[a], sizes, where)
            pltpu.make_async_copy(
                ins[a](slot), staged[a].at[index], loads[a].at[index]
            ).start()
    greet(names, sizes, at)
    started = []
    number = [0] * count

    def send(a, source, box, to, there):
        copy = pltpu.make_async_remote_copy(
            src_ref=source,
            dst_ref=landed[a].at[box],
            send_sem=sends[a].at[number[a]],
            recv_sem=recvs[a].at[box],
            device_id=device_of(sizes, to),
            device_id_type=MESH_ID,
        )
        number[a] += 1
        when(there, copy.start)
        started.append((there, copy))

    for _, _, a, ks in plan:
        if ks[-1]:
            order = orders[a]
            where, slot = slots[a, ks]
            j = len(order) - 1
            to = dict(at, **{order[j]: 1 - at[order[j]]})
            send(a, ins[a](slot), box_of(j, order, sizes, where, False), to, True)
    for _, _, a, ks in plan:
        if ks[-1]:
            continue
        order = orders[a]
        where, slot = slots[a, ks]
        index = staged_of(order, sizes, where)
        mine = staged[a].at[index]
        pltpu.make_async_copy(ins[a](slot), mine, loads[a].at[index]).wait()
        leaves = max([j for j in range(len(order)) if ks[j]], default=-1)
        terms = [mine]
        loose = []
        for j in reversed(range(len(order))):
            d = order[j]
            if j < leaves or sizes[d] == 1:
                break
            if sizes[d] == 2:
                if ks[j] == 0:
                    box = box_of(j, order, sizes, where, False)
                    terms.append((box, True))
                continue
            p, q = at[d], where[d]
            if j == leaves:
                far = ((q > p) & (p > 0)) | ((q < p) & (p < sizes[d] - 1))
                terms.append((box_of(j, order, sizes, where, False), far))
            else:
                terms.append((box_of(j, order, sizes, where, False), p > 0))
                terms.append((box_of(j, order, sizes, where, True), p < sizes[d] - 1))
        sure = [mine]
        for box, there in terms[1:]:
            ref = landed[a].at[box]
            waiting = pltpu.make_async_copy(ref, ref, recvs[a].at[box])
            if there is True:
                waiting.wait()
                sure.append(ref)
            else:

                def take(ref=ref, waiting=waiting, mine=mine):
                    waiting.wait()
                    add_up(mine, [mine, ref], mine.dtype)

                loose.append((there, take))
        if len(sure) > 1 and leaves >= 0:
            add_up(mine, sure, mine.dtype)
            sure = [mine]
        for there, take in loose:
            when(there, take)
        if leaves < 0:
            add_up(outs[a], sure, outs[a].dtype)
            continue
        d = order[leaves]
        if sizes[d] == 2:
            send(
                a,
                mine,
                box_of(leaves, order, sizes, where, False),
                dict(at, **{d: 1 - at[d]}),
                True,
            )
        else:
            p, q = at[d], where[d]
            send(
                a, mine, box_of(leaves, order, sizes, where, False), dict(at, **{d: p + 1}), q > p
            )
            send(
                a,
                mine,
                jnp.where(
                    q + 1 == p,
                    box_of(leaves, order, sizes, where, True),
                    box_of(leaves, order, sizes, where, False),
                ),
                dict(at, **{d: p - 1}),
                q < p,
            )
    for there, copy in started:
        when(there, copy.wait_send)


def scatter_sends(order, sizes):
    total = 0
    for ks in visits(order, sizes):
        leaves = max([j for j in range(len(order)) if ks[j]], default=-1)
        if leaves >= 0:
            total += 1 if sizes[order[leaves]] == 2 else 2
    return total


def scatter(arrays, orders, identity, out_dtype=jnp.float32):
    sizes = dims_of()
    items = items_of(orders, [a.shape[1:] for a in arrays])
    shapes = [arrays[a].shape[-2:] for a, _, _ in items]
    types = [arrays[a].dtype for a, _, _ in items]
    orders = [order for _, _, order in items]
    stages = [math.prod(sizes[d] for d in order[:-1]) for order in orders]
    landing = [boxes(order, sizes) for order in orders]
    return pl.pallas_call(
        functools.partial(scatter_kernel, items, sizes),
        out_shape=[jax.ShapeDtypeStruct(a.shape[1:], out_dtype) for a in arrays],
        in_specs=[ANYWHERE] * len(arrays),
        out_specs=[pl.BlockSpec(memory_space=pltpu.VMEM)] * len(arrays),
        scratch_shapes=[pltpu.VMEM((n,) + s, t) for n, s, t in zip(stages, shapes, types)]
        + [pltpu.VMEM((n,) + s, t) for n, s, t in zip(landing, shapes, types)]
        + [pltpu.SemaphoreType.DMA((scatter_sends(order, sizes),)) for order in orders]
        + [pltpu.SemaphoreType.DMA((n,)) for n in landing]
        + [pltpu.SemaphoreType.DMA((n,)) for n in stages],
        compiler_params=pltpu.CompilerParams(
            collective_id=identity, has_side_effects=True, vmem_limit_bytes=60 << 20
        ),
    )(*arrays)


PLANE = ("z", "y", "c")
ZYX = ("z", "y", "x", "c")
ZXY = ("z", "x", "y", "c")
XYZ = ("x", "y", "z", "c")
YZ = ("y", "z", "c")
CHUNKS = 4
CHUNK_ORDERS = [PLANE, PLANE, PLANE, YZ]
YZX = ("y", "z", "x", "c")
ALL_ORDERS = [[ZYX, ZXY], XYZ, XYZ, [ZXY, ZYX], XYZ]


def gather_plane(x):
    return lax.all_gather(x, "expert", axis=0, tiled=False)


def scatter_plane(x):
    return lax.psum_scatter(x, "expert", scatter_dimension=0, tiled=False)


def low(x):
    return x.astype(jnp.bfloat16)


def wide(x):
    return x.astype(jnp.float32)


def dot(a, b):
    return jnp.dot(a, b, preferred_element_type=jnp.float32)


def fetch_dp(x, axis):
    if lax.axis_size("dp") != 2:
        return x, lax.all_gather(x, "dp", axis=axis, tiled=True)
    return x, lax.ppermute(x, "dp", [(0, 1), (1, 0)])


def joined(pair, axis):
    own, other = pair
    if lax.axis_size("dp") != 2:
        return other
    first = lax.axis_index("dp") == 0
    return jnp.concatenate(
        [jnp.where(first, own, other), jnp.where(first, other, own)], axis=axis
    )


def send_dp(x, axis):
    if lax.axis_size("dp") != 2:
        total = lax.psum_scatter(x, "dp", scatter_dimension=axis, tiled=True)
        return total, jnp.zeros_like(total)
    half = x.shape[axis] // 2
    index = lax.axis_index("dp")
    away = lax.dynamic_slice_in_dim(x, (1 - index) * half, half, axis)
    arrived = lax.ppermute(away, "dp", [(0, 1), (1, 0)])
    return lax.dynamic_slice_in_dim(x, index * half, half, axis), arrived


def added(pair):
    return pair[0].astype(jnp.float32) + pair[1].astype(jnp.float32)


def cross(a, b):
    return lax.dot_general(a, b, (((1,), (1,)), ((), ())), preferred_element_type=jnp.float32)


HEADS = 2


def spread_matrix(quads, dtype):
    half = ROPE // 2
    source = lax.broadcasted_iota(jnp.int32, (128, 256), 0)
    target = lax.broadcasted_iota(jnp.int32, (128, 256), 1)
    wanted = target % half + half * (target // (half * quads))
    return (source == wanted).astype(jnp.float32).astype(dtype)


def head_query(u, rows, qn, qa, qb):
    quads = qa.shape[1] // (ROPE // 2)
    lanes = lax.broadcasted_iota(jnp.int32, (1, qa.shape[1]), 1) // (ROPE // 2)
    ours = lanes == (pl.program_id(0) * HEADS + u) % quads
    nothing = jnp.zeros((), qa.dtype)
    parts = jnp.concatenate(
        [jnp.where(ours, qa[rows, :], nothing), jnp.where(ours, qb[rows, :], nothing)], axis=1
    )
    turned = low(cross(parts, spread_matrix(quads, jnp.bfloat16)))
    return ours, jnp.concatenate([qn[rows, u * NOPE : (u + 1) * NOPE], turned], axis=1)


def load_window(tokens, span, line, window, sems):
    lane = lax.axis_index("expert")
    copies = []
    for j in range(span):
        source = lane - (span - 1) + j
        rows = pl.ds(j * tokens, tokens)
        for m in range(MICRO):
            copy = pltpu.make_async_copy(
                line.at[jnp.maximum(source, 0), pl.ds(m * tokens, tokens)],
                window.at[m, rows],
                sems.at[m, j],
            )
            pl.when(source >= 0)(copy.start)
            copies.append((source >= 0, copy))

            @pl.when(source < 0)
            def _(m=m, rows=rows):
                window[m, rows] = jnp.zeros((tokens, window.shape[2]), window.dtype)

    left = window.shape[1] - span * tokens
    if left:
        for m in range(MICRO):
            window[m, pl.ds(span * tokens, left)] = jnp.zeros((left, window.shape[2]), window.dtype)
    for there, copy in copies:
        pl.when(there)(copy.wait)


def attend_kernel(tokens, span, scale, qn, qa, qb, line, expand, bias, out, window, sems):
    @pl.when(pl.program_id(0) == 0)
    def _():
        load_window(tokens, span, line, window, sems)

    for m in range(MICRO):
        rows = pl.ds(m * tokens, tokens)
        pairs = low(dot(window[m, :, :LAT], expand[...]))
        turns = window[m, :, LAT:]
        for u in range(HEADS):
            pair = pairs[:, u * (NOPE + VDIM) : (u + 1) * (NOPE + VDIM)]
            keys = jnp.concatenate([pair[:, :NOPE], turns], axis=1)
            _, own = head_query(u, rows, qn, qa, qb)
            scores = cross(own, keys) * scale + bias[m]
            raised = jnp.exp(scores - jnp.max(scores, axis=1, keepdims=True))
            weights = low(raised * (1.0 / jnp.sum(raised, axis=1, keepdims=True)))
            out[rows, u * VDIM : (u + 1) * VDIM] = low(dot(weights, pair[:, NOPE:]))


def attend_back_kernel(
    tokens, span, scale, qn, qa, qb, grad, line, expand, bias, gqn, gqa, gqb, gline, gexp, *scratch
):
    window, upright, glat, gturns, gwindow, zeros, sems, out_sems = scratch
    head = pl.program_id(0)
    quads = qa.shape[1] // (ROPE // 2)

    @pl.when(head == 0)
    def _():
        load_window(tokens, span, line, window, sems)
        for m in range(MICRO):
            upright[m] = window[m, :, :LAT].T
        glat[...] = jnp.zeros_like(glat)
        gturns[...] = jnp.zeros_like(gturns)

    @pl.when((head * HEADS) % quads == 0)
    def _():
        gqa[...] = jnp.zeros_like(gqa)
        gqb[...] = jnp.zeros_like(gqb)

    expand_total = None
    for m in range(MICRO):
        rows = pl.ds(m * tokens, tokens)
        pairs = low(dot(window[m, :, :LAT], expand[...]))
        turns = window[m, :, LAT:]
        grad_pairs = []
        turns_total = None
        for u in range(HEADS):
            pair = pairs[:, u * (NOPE + VDIM) : (u + 1) * (NOPE + VDIM)]
            keys = jnp.concatenate([pair[:, :NOPE], turns], axis=1)
            ours, own = head_query(u, rows, qn, qa, qb)
            grad_rows = grad[rows, u * VDIM : (u + 1) * VDIM]
            scores = cross(keys, own) * scale + bias[m]
            raised = jnp.exp(scores - jnp.max(scores, axis=0, keepdims=True))
            probs = raised * (1.0 / jnp.sum(raised, axis=0, keepdims=True))
            grad_probs = cross(pair[:, NOPE:], grad_rows)
            shift = jnp.sum(grad_probs * probs, axis=0, keepdims=True)
            back = low(probs * (grad_probs - shift))
            grad_own = dot(back.T, keys) * scale
            gqn[rows, u * NOPE : (u + 1) * NOPE] = low(grad_own[:, :NOPE])
            spread = lax.dot_general(
                grad_own[:, NOPE:],
                spread_matrix(quads, jnp.float32),
                (((1,), (0,)), ((), ())),
                precision=HIGHEST_PRECISION,
                preferred_element_type=jnp.float32,
            )
            gqa[rows, :] += jnp.where(ours, spread[:, :128], 0.0)
            gqb[rows, :] += jnp.where(ours, spread[:, 128:], 0.0)
            grad_keys = dot(back, own) * scale
            turned = grad_keys[:, NOPE:]
            turns_total = turned if turns_total is None else turns_total + turned
            grad_pairs.append(low(grad_keys[:, :NOPE]))
            grad_pairs.append(low(dot(low(probs), grad_rows)))
        gturns[m] += turns_total
        both = jnp.concatenate(grad_pairs, axis=1)
        glat[m] += cross(both, expand[...])
        part = dot(upright[m], both)
        expand_total = part if expand_total is None else expand_total + part
    gexp[...] = low(expand_total)

    @pl.when(head == pl.num_programs(0) - 1)
    def _():
        lane = lax.axis_index("expert")
        zeros[...] = jnp.zeros_like(zeros)
        for m in range(MICRO):
            gwindow[m, :, :LAT] = low(glat[m])
            gwindow[m, :, LAT:] = low(gturns[m])
        copies = []
        for slot in range(gline.shape[0]):
            j = slot - lane + span - 1
            inside = (j >= 0) & (j < span)
            start = pl.multiple_of(jnp.clip(j, 0, span - 1) * tokens, tokens)
            for m in range(MICRO):
                target = gline.at[slot, pl.ds(m * tokens, tokens)]
                sem = out_sems.at[slot, m]
                full = pltpu.make_async_copy(gwindow.at[m, pl.ds(start, tokens)], target, sem)
                empty = pltpu.make_async_copy(zeros, target, sem)
                pl.when(inside)(full.start)
                pl.when(jnp.logical_not(inside))(empty.start)
                copies.append(full)
        for copy in copies:
            copy.wait()


def whole_block(a):
    return pl.BlockSpec(a.shape, lambda h: (0,) * len(a.shape))


def attention_specs(rows, quads):
    return [
        pl.BlockSpec((rows, HEADS * NOPE), lambda h: (0, h)),
        pl.BlockSpec((rows, 128), lambda h: (0, h * HEADS // quads)),
        pl.BlockSpec((rows, 128), lambda h: (0, h * HEADS // quads)),
    ]


def attention_forward(tokens, span, scale, qn, qa, qb, line, expand, bias):
    rows = qn.shape[0]
    quads = 128 // (ROPE // 2)
    key_rows = bias.shape[2]
    return pl.pallas_call(
        functools.partial(attend_kernel, tokens, span, scale),
        grid=(H // HEADS,),
        out_shape=jax.ShapeDtypeStruct((rows, H * VDIM), jnp.bfloat16),
        in_specs=attention_specs(rows, quads)
        + [ANYWHERE, pl.BlockSpec((LAT, HEADS * (NOPE + VDIM)), lambda h: (0, h)), whole_block(bias)],
        out_specs=pl.BlockSpec((rows, HEADS * VDIM), lambda h: (0, h)),
        scratch_shapes=[
            pltpu.VMEM((MICRO, key_rows, line.shape[2]), jnp.bfloat16),
            pltpu.SemaphoreType.DMA((MICRO, span)),
        ],
        compiler_params=pltpu.CompilerParams(vmem_limit_bytes=56 << 20),
        cost_estimate=pl.CostEstimate(
            flops=10**9, bytes_accessed=10**6, transcendentals=0
        ),
    )(qn, qa, qb, line, expand, bias)


def attention_backward(tokens, span, scale, qn, qa, qb, grad, line, expand, bias):
    rows = qn.shape[0]
    quads = 128 // (ROPE // 2)
    key_rows = bias.shape[1]
    width = line.shape[2]
    single = jax.ShapeDtypeStruct
    return pl.pallas_call(
        functools.partial(attend_back_kernel, tokens, span, scale),
        grid=(H // HEADS,),
        out_shape=[
            single(qn.shape, jnp.bfloat16),
            single(qa.shape, jnp.float32),
            single(qb.shape, jnp.float32),
            single(line.shape, jnp.bfloat16),
            single(expand.shape, jnp.bfloat16),
        ],
        in_specs=attention_specs(rows, quads)
        + [pl.BlockSpec((rows, HEADS * VDIM), lambda h: (0, h)), ANYWHERE]
        + [pl.BlockSpec((LAT, HEADS * (NOPE + VDIM)), lambda h: (0, h)), whole_block(bias)],
        out_specs=attention_specs(rows, quads)
        + [ANYWHERE, pl.BlockSpec((LAT, HEADS * (NOPE + VDIM)), lambda h: (0, h))],
        scratch_shapes=[
            pltpu.VMEM((MICRO, key_rows, width), jnp.bfloat16),
            pltpu.VMEM((MICRO, LAT, key_rows), jnp.bfloat16),
            pltpu.VMEM((MICRO, key_rows, LAT), jnp.float32),
            pltpu.VMEM((MICRO, key_rows, 128), jnp.float32),
            pltpu.VMEM((MICRO, key_rows, width), jnp.bfloat16),
            pltpu.VMEM((tokens, width), jnp.bfloat16),
            pltpu.SemaphoreType.DMA((MICRO, span)),
            pltpu.SemaphoreType.DMA((line.shape[0], MICRO)),
        ],
        compiler_params=pltpu.CompilerParams(vmem_limit_bytes=56 << 20),
        cost_estimate=pl.CostEstimate(
            flops=60 * 10**9, bytes_accessed=30 * 10**6, transcendentals=0
        ),
    )(qn, qa, qb, grad, line, expand, bias)


def combine_kernel(picked, rows, left, right, out):
    beside = dot(left[...], right[...])
    height = picked.shape[1]
    for i in range(picked.shape[0]):
        part = slice(i * height, (i + 1) * height)
        out[part, :] = low(beside[part, :] + dot(picked[i], rows[i]))


def combine(picked, rows, left, right):
    groups, group_rows, slots = picked.shape
    total, inner = left.shape
    step = 2 if groups % 2 == 0 else 1
    return pl.pallas_call(
        combine_kernel,
        grid=(groups // step,),
        out_shape=jax.ShapeDtypeStruct((total, D), jnp.bfloat16),
        in_specs=[
            pl.BlockSpec((step, group_rows, slots), lambda g: (g, 0, 0)),
            pl.BlockSpec((step, slots, D), lambda g: (g, 0, 0)),
            pl.BlockSpec((step * group_rows, inner), lambda g: (g, 0)),
            pl.BlockSpec((inner, D), lambda g: (0, 0)),
        ],
        out_specs=pl.BlockSpec((step * group_rows, D), lambda g: (g, 0)),
        compiler_params=pltpu.CompilerParams(vmem_limit_bytes=48 << 20),
        cost_estimate=pl.CostEstimate(
            flops=2 * total * (slots + inner) * D,
            bytes_accessed=total * D * 4,
            transcendentals=0,
        ),
    )(picked, rows.reshape(groups, slots, D), left, right)


def halves_of(x):
    parts = 2 if x.shape[0] % 32 == 0 else 1
    return x.reshape(parts, x.shape[0] // parts, x.shape[1])


def body(
    layer_input,
    cotangent,
    doc_lengths,
    routes,
    attention_gain,
    query_weight,
    latent_weight,
    latent_gain,
    expand_weight,
    output_weight,
    feed_gain,
    router_weight,
    shared_gate,
    shared_up,
    shared_down,
    expert_gate,
    expert_up,
    expert_down,
):
    n_dp = lax.axis_size("dp")
    n_expert = lax.axis_size("expert")
    devices = n_dp * n_expert
    lane = lax.axis_index("expert")
    tokens = layer_input.shape[2]
    rows = MICRO * tokens
    experts_count = router_weight.shape[1]
    score_scale = (NOPE + ROPE) ** (-0.5)
    head_width = NOPE + ROPE
    key_width = H * head_width

    shard = query_weight.shape[0]
    small_latent = latent_gain.shape[0]
    small = jnp.concatenate(
        [
            router_weight,
            attention_gain[:, None],
            feed_gain[:, None],
            jnp.pad(latent_gain, (0, shard - small_latent))[:, None],
        ],
        axis=1,
    )
    small = jnp.pad(small, ((0, 0), (0, 128 - small.shape[1])))
    by_head = query_weight.reshape(shard, H, head_width)
    split_query = jnp.concatenate(
        [
            by_head[..., :NOPE].reshape(shard, H * NOPE),
            by_head[..., NOPE : NOPE + ROPE // 2].reshape(shard, H * ROPE // 2),
            by_head[..., NOPE + ROPE // 2 :].reshape(shard, H * ROPE // 2),
        ],
        axis=1,
    )
    all_query, all_latent, all_expand, all_output, small = gather(
        [
            halves_of(split_query),
            latent_weight,
            expand_weight.reshape(16, -1),
            halves_of(output_weight.T),
            small,
        ],
        ALL_ORDERS,
        1,
    )
    all_query = all_query.reshape(D, key_width)
    all_latent = all_latent.reshape(D, LAT + ROPE)
    all_expand = all_expand.reshape(LAT, H * (NOPE + VDIM))
    all_output = all_output.reshape(D, H * VDIM)
    gain_latent = small[:, :small_latent, experts_count + 2].reshape(LAT).astype(jnp.float32)
    small = small.reshape(D, 128)
    all_router = small[:, :experts_count]
    gain_first = small[:, experts_count].astype(jnp.float32)
    gain_second = small[:, experts_count + 1].astype(jnp.float32)

    (later, all_query) = lax.optimization_barrier(
        (
            (expert_gate, expert_up, expert_down, shared_gate, shared_up, shared_down),
            all_query,
        )
    )
    expert_gate, expert_up, expert_down, shared_gate, shared_up, shared_down = later
    parts_gate = fetch_dp(expert_gate[0], 0)
    parts_up = fetch_dp(expert_up[0], 0)
    parts_down = fetch_dp(expert_down[0], 1)
    units = shared_down.shape[0]
    mine = n_dp * units
    both = jnp.stack([shared_gate, shared_up], axis=1).reshape(shard, 2, n_dp, n_expert, units)
    both = both.transpose(3, 0, 1, 2, 4).reshape(n_expert, shard, 2 * mine)
    both = lax.all_to_all(both, "expert", split_axis=0, concat_axis=0, tiled=True)
    parts_in = fetch_dp(both.reshape(n_expert * shard, 2 * mine), 0)
    parts_out = fetch_dp(shared_down, 0)

    positions = lane * tokens + jnp.arange(tokens, dtype=jnp.int32)
    cosine_table, sine_table = angles(positions)
    cosine_rows = jnp.tile(cosine_table, (MICRO, 1))
    sine_rows = jnp.tile(sine_table, (MICRO, 1))
    head_cosine = jnp.tile(cosine_rows, (1, H))
    head_sine = jnp.tile(sine_rows, (1, H))
    inputs = layer_input[0].reshape(rows, D).astype(jnp.float32)
    hidden = low(root_normalize(inputs, gain_first))
    latent = dot(hidden, all_latent)
    compressed = low(root_normalize(latent[:, :LAT], gain_latent))
    key_rope = low(rotate(latent[:, LAT:], cosine_rows, sine_rows))
    payload = jnp.concatenate(
        [compressed, key_rope, jnp.zeros((rows, 128 - ROPE), jnp.bfloat16)], axis=1
    )
    columns = jnp.pad(routes[0].reshape(rows, TOP).T, ((0, 8 - TOP), (0, 0)))
    line, all_routes = gather([payload, columns], [PLANE, PLANE], 2)
    cotangent_rows = cotangent[0].reshape(rows, D)
    first_half, line = lax.optimization_barrier((cotangent_rows[:, : D // 2], line))
    first_half = gather_plane(first_half).reshape(n_expert * rows, D // 2)
    query = dot(hidden, all_query)
    plain = H * NOPE
    half = H * ROPE // 2
    query_plain = low(query[:, :plain])
    turn_first = query[:, plain : plain + half]
    turn_second = query[:, plain + half :]
    query_first = low(turn_first * head_cosine - turn_second * head_sine)
    query_second = low(turn_first * head_sine + turn_second * head_cosine)
    reach = (WINDOW + tokens - 2) // tokens
    span = reach + 1
    key_rows = -(-span * tokens // 128) * 128
    key_positions = (lane - reach) * tokens + jnp.arange(key_rows, dtype=jnp.int32)
    apart = positions[:, None] - key_positions[None, :]
    reachable = (key_positions[None, :] >= 0) & (apart >= 0) & (apart < WINDOW)
    allowed = jnp.stack(
        [
            reachable
            & (
                segment_of(positions, doc_lengths[0, m])[:, None]
                == segment_of(key_positions, doc_lengths[0, m])[None, :]
            )
            for m in range(MICRO)
        ]
    )
    bias = jnp.where(allowed, 0.0, NEGATIVE).astype(jnp.float32)
    mixture = attention_forward(
        tokens,
        span,
        score_scale,
        query_plain,
        query_first,
        query_second,
        line,
        all_expand,
        bias,
    )
    residual = inputs + transposed_right(mixture, all_output)
    normed = low(root_normalize(residual, gain_second))

    chunked = normed.reshape(CHUNKS, rows // CHUNKS, D)
    own_probs = jax.nn.softmax(dot(normed, all_router), axis=-1)
    all_normed, all_probs = gather([chunked, own_probs.T], [CHUNK_ORDERS, PLANE], 3)
    all_normed = all_normed.reshape(n_expert * rows, D)
    fetched = (parts_gate, parts_up, parts_down, parts_in, parts_out)
    second_half, all_normed = lax.optimization_barrier((cotangent_rows[:, D // 2 :], all_normed))
    fetched = [lax.optimization_barrier((pair, all_normed))[0] for pair in fetched]
    second_half = gather_plane(second_half).reshape(n_expert * rows, D // 2)
    cotangent_halves = (first_half, second_half)
    expert_gate, expert_up = joined(fetched[0], 0), joined(fetched[1], 0)
    expert_down = joined(fetched[2], 1)
    padded = -(-mine // 128) * 128
    shared_in = jnp.pad(
        joined(fetched[3], 0).reshape(D, 2, mine), ((0, 0), (0, 0), (0, padded - mine))
    ).reshape(D, 2 * padded)
    shared_out_weight = jnp.pad(joined(fetched[4], 0), ((0, padded - mine), (0, 0)))
    total_rows = n_expert * rows
    capacity = (9 * tokens * TOP + 8 * experts_count - 1) // (8 * experts_count)
    per_group = max(1, 256 // tokens)
    group_rows = per_group * tokens
    groups = total_rows // group_rows
    slots = -(-per_group * capacity // 16) * 16
    named = jnp.any(all_routes[:, :TOP] == lane, axis=1).reshape(-1, tokens).astype(jnp.int32)
    rank = jnp.cumsum(named, axis=1) - named
    kept = (named > 0) & (rank < capacity)
    offset = (jnp.arange(named.shape[0], dtype=jnp.int32) % per_group) * capacity
    place = jnp.where(kept, rank + offset[:, None], -1).reshape(groups, 1, group_rows)
    picked_bool = place == jnp.arange(slots, dtype=jnp.int32)[None, :, None]
    picked = picked_bool.astype(jnp.bfloat16)
    picked_float = picked_bool.astype(jnp.float32)
    shared_pre = low(dot(all_normed, shared_in))
    gate_rows = lax.dynamic_index_in_dim(all_probs, lane, 1, keepdims=False)
    gate_slots = jnp.sum(
        picked_float * gate_rows.reshape(groups, 1, group_rows), axis=2
    ).reshape(groups * slots, 1)

    def to_slots(x):
        return low(
            jnp.einsum(
                "gst,gtd->gsd",
                picked,
                x.reshape(groups, group_rows, x.shape[1]),
                preferred_element_type=jnp.float32,
            )
        ).reshape(groups * slots, x.shape[1])

    arrived = to_slots(all_normed)
    gate_pre = low(dot(arrived, expert_gate))
    up_pre = low(dot(arrived, expert_up))
    expert_act = low(silu_product(wide(gate_pre), wide(up_pre)))
    expert_out = lax.optimization_barrier(low(dot(expert_act, expert_down)))
    shared_act = low(silu_product(wide(shared_pre[:, :padded]), wide(shared_pre[:, padded:])))
    spread = jnp.swapaxes(picked, 1, 2)
    partial_out = combine(
        spread, low(gate_slots * expert_out.astype(jnp.float32)), shared_act, shared_out_weight
    )
    expert_sum = scatter_plane(partial_out.reshape(n_expert, rows, D))
    layer_output = low(residual + expert_sum.astype(jnp.float32))

    arrived_grad = jnp.concatenate([to_slots(x) for x in cotangent_halves], axis=1)
    gate_dots = jnp.sum(
        expert_out.astype(jnp.float32) * arrived_grad.astype(jnp.float32), axis=1
    ).reshape(groups, slots, 1)
    gate_grad_rows = jnp.sum(picked_float * gate_dots, axis=1).reshape(n_expert, rows)
    gate_grads = lax.all_to_all(
        gate_grad_rows, "expert", split_axis=0, concat_axis=0, tiled=True
    ).T
    slot_grad = low(gate_slots * arrived_grad.astype(jnp.float32))
    expert_down_grad = low(transposed_left(expert_act, slot_grad))
    gate_back, up_back = silu_back(
        wide(gate_pre), wide(up_pre), transposed_right(slot_grad, expert_down)
    )
    gate_back = low(gate_back)
    up_back = low(up_back)
    expert_gate_grad = low(transposed_left(arrived, gate_back))
    expert_up_grad = low(transposed_left(arrived, up_back))
    rows_grad = low(
        transposed_right(gate_back, expert_gate) + transposed_right(up_back, expert_up)
    )
    shared_back = jnp.concatenate(
        silu_back(
            wide(shared_pre[:, :padded]),
            wide(shared_pre[:, padded:]),
            transposed_right(cotangent_halves[0], shared_out_weight[:, : D // 2])
            + transposed_right(cotangent_halves[1], shared_out_weight[:, D // 2 :]),
        ),
        axis=1,
    ).astype(jnp.bfloat16)
    partial_normed = combine(spread, rows_grad, shared_back, shared_in.T)
    partial_normed = partial_normed.reshape(n_expert, CHUNKS, rows // CHUNKS, D)
    (grad_normed,) = scatter([partial_normed], [CHUNK_ORDERS], 4)
    grad_normed = grad_normed.reshape(rows, D)
    sums = [
        send_dp(expert_gate_grad, 0),
        send_dp(expert_up_grad, 0),
        send_dp(expert_down_grad, 1),
        send_dp(
            jnp.concatenate(
                [low(transposed_left(shared_act, x)[:mine]) for x in cotangent_halves], axis=1
            ),
            0,
        ),
        send_dp(low(transposed_left(all_normed, shared_back)), 0),
    ]

    logit_grad = low(
        own_probs * (gate_grads - jnp.sum(gate_grads * own_probs, axis=-1, keepdims=True))
    )
    wide_logits = jnp.pad(logit_grad, ((0, 0), (0, 128 - experts_count)))
    router_weight_grad = transposed_left(normed, wide_logits)
    grad_normed = grad_normed + transposed_right(logit_grad, all_router)
    residual_extra, feed_gain_grad = normalize_back(residual, gain_second, grad_normed)
    grad_residual = cotangent[0].reshape(rows, D).astype(jnp.float32) + residual_extra

    grad_attn = low(grad_residual)
    output_grad = low(transposed_left(grad_attn, mixture))
    middle = output_grad.shape[1] // 2
    later_grad = output_grad[:, middle:].reshape(devices, shard, middle)
    output_grad = lax.psum_scatter(
        output_grad[:, :middle], ("dp", "expert"), scatter_dimension=0, tiled=True
    )
    grad_mixture = low(dot(grad_attn, all_output))
    grad_plain, grad_first, grad_second, grad_line, expand_grad = attention_backward(
        tokens,
        span,
        score_scale,
        query_plain,
        query_first,
        query_second,
        grad_mixture,
        line,
        all_expand,
        jnp.swapaxes(bias, 1, 2),
    )
    grad_query = jnp.concatenate(
        [
            grad_plain,
            low(grad_first * head_cosine + grad_second * head_sine),
            low(grad_second * head_cosine - grad_first * head_sine),
        ],
        axis=1,
    )
    query_grad = low(transposed_left(hidden, grad_query))
    grad_line, query_grad, expand_grad = scatter(
        [
            grad_line,
            query_grad.reshape(devices, shard, key_width),
            expand_grad.reshape(devices, 16, -1),
        ],
        [PLANE, ZYX, XYZ],
        5,
    )
    sums, grad_line = lax.optimization_barrier((sums, grad_line))
    expert_grads = [added(pair)[None] for pair in sums[:3]]
    shared_down_grad = added(sums[3])
    shared_in_grad = low(added(sums[4])).reshape(n_expert, shard, 2, padded)[..., :mine]
    shared_in_grad = lax.all_to_all(
        shared_in_grad.reshape(n_expert, shard, 2 * mine),
        "expert",
        split_axis=0,
        concat_axis=0,
        tiled=True,
    ).astype(jnp.float32)
    shared_in_grad = (
        shared_in_grad.reshape(n_expert, shard, 2, n_dp, units)
        .transpose(2, 1, 3, 0, 4)
        .reshape(2, shard, n_dp * n_expert * units)
    )
    latent_part, latent_gain_grad = normalize_back(
        latent[:, :LAT], gain_latent, grad_line[:, :LAT]
    )
    grad_key_rope = rotate(grad_line[:, LAT : LAT + ROPE], cosine_rows, -sine_rows)
    grad_latent = low(jnp.concatenate([latent_part, grad_key_rope], axis=1))
    latent_grad = transposed_left(hidden, grad_latent)
    grad_hidden = transposed_right(grad_latent, all_latent) + transposed_right(
        grad_query, all_query
    )
    input_extra, attention_gain_grad = normalize_back(inputs, gain_first, grad_hidden)
    input_grad = grad_residual + input_extra

    column = jnp.arange(128, dtype=jnp.int32)[None, :]
    latent_rows = jnp.pad(
        latent_gain_grad.reshape(devices, small_latent), ((0, 0), (0, shard - small_latent))
    ).reshape(D)
    small_grad = router_weight_grad
    for place, vector in enumerate((attention_gain_grad, feed_gain_grad, latent_rows)):
        small_grad = jnp.where(column == experts_count + place, vector[:, None], small_grad)
    small_grad = small_grad.reshape(devices, shard, 128)
    latent_grad, small_grad, later_grad = scatter(
        [low(latent_grad).reshape(devices, shard, LAT + ROPE), low(small_grad), later_grad],
        [ZYX, XYZ, ZXY],
        6,
    )
    query_grad = jnp.concatenate(
        [
            query_grad[:, :plain].reshape(shard, H, NOPE),
            query_grad[:, plain : plain + half].reshape(shard, H, ROPE // 2),
            query_grad[:, plain + half :].reshape(shard, H, ROPE // 2),
        ],
        axis=2,
    ).reshape(shard, key_width)
    return (
        layer_output.reshape(1, MICRO, tokens, D),
        input_grad.reshape(1, MICRO, tokens, D),
        small_grad[:, experts_count],
        query_grad,
        latent_grad,
        small_grad[:small_latent, experts_count + 2],
        expand_grad.reshape(expand_weight.shape),
        jnp.concatenate([wide(output_grad), later_grad], axis=1).T,
        small_grad[:, experts_count + 1],
        small_grad[:, :experts_count],
        shared_in_grad[0],
        shared_in_grad[1],
        shared_down_grad,
        expert_grads[0],
        expert_grads[1],
        expert_grads[2],
    )


def solution(mesh):
    placed = (
        P("dp", None, "expert", None),
        P("dp", None, "expert", None),
        P("dp", None, None),
        P("dp", None, "expert", None),
        P(("dp", "expert")),
        P(("dp", "expert"), None),
        P(("dp", "expert"), None),
        P(("dp", "expert")),
        P(("dp", "expert"), None),
        P(None, ("dp", "expert")),
        P(("dp", "expert")),
        P(("dp", "expert"), None),
        P(("dp", "expert"), None),
        P(("dp", "expert"), None),
        P(("dp", "expert"), None),
        P("expert", "dp", None),
        P("expert", "dp", None),
        P("expert", None, "dp"),
    )
    return jax.shard_map(
        body,
        mesh=mesh,
        in_specs=placed,
        out_specs=(
            P("dp", None, "expert", None),
            P("dp", None, "expert", None),
            P(("dp", "expert")),
            P(("dp", "expert"), None),
            P(("dp", "expert"), None),
            P(("dp", "expert")),
            P(("dp", "expert"), None),
            P(None, ("dp", "expert")),
            P(("dp", "expert")),
            P(("dp", "expert"), None),
            P(("dp", "expert"), None),
            P(("dp", "expert"), None),
            P(("dp", "expert"), None),
            P("expert", "dp", None),
            P("expert", "dp", None),
            P("expert", None, "dp"),
        ),
        check_vma=False,
    )
```

```python
import functools
import itertools
import math

import jax
import jax.numpy as jnp
from jax import lax
from jax.experimental import pallas as pl
from jax.experimental.pallas import tpu as pltpu
from jax.sharding import PartitionSpec as P

D = 2048
H = 16
NOPE = 128
ROPE = 64
VDIM = 128
LAT = 512
TOP = 6
WINDOW = 1024
MICRO = 2


EPSILON = 1e-06
NEGATIVE = -1e30
HIGHEST_PRECISION = lax.Precision.HIGHEST


def root_normalize(values, gain):
    inverse = lax.rsqrt(jnp.mean(values * values, axis=-1, keepdims=True) + EPSILON)
    return values * inverse * gain


def normalize_back(values, gain, incoming):
    result, pullback = jax.vjp(root_normalize, values, gain)
    return pullback(incoming)


def silu_product(left, right):
    return jax.nn.silu(left) * right


def silu_back(left, right, incoming):
    result, pullback = jax.vjp(silu_product, left, right)
    return pullback(incoming)


def angles(positions):
    half_width = ROPE // 2
    frequency = jnp.exp(
        jnp.arange(half_width, dtype=jnp.float32) * (-math.log(10000.0) / half_width)
    )
    turned = positions.astype(jnp.float32)[:, None] * frequency[None, :]
    return (jnp.cos(turned), jnp.sin(turned))


def rotate(values, cosine_table, sine_table):
    half_width = values.shape[-1] // 2
    first = values[..., :half_width]
    second = values[..., half_width:]
    return jnp.concatenate(
        [first * cosine_table - second * sine_table, first * sine_table + second * cosine_table],
        axis=-1,
    )


def segment_of(positions, lengths):
    boundary = jnp.cumsum(lengths)
    return jnp.sum((boundary[None, :] <= positions[:, None]).astype(jnp.int32), axis=1)


def transposed_left(left, right):
    return lax.dot_general(
        left, right, (((0,), (0,)), ((), ())), preferred_element_type=jnp.float32
    )


def transposed_right(left, right):
    return lax.dot_general(
        left, right, (((1,), (1,)), ((), ())), preferred_element_type=jnp.float32
    )


MESH_ID = pl.DeviceIdType.MESH
ANYWHERE = pl.BlockSpec(memory_space=pl.ANY)


def dims_of():
    n_expert = lax.axis_size("expert")
    core = 2 if n_expert % 2 == 0 else 1
    z = 4 if n_expert % (4 * core) == 0 else 1
    return {"x": lax.axis_size("dp"), "z": z, "y": n_expert // (z * core), "c": core}


def place_of(sizes):
    e = lax.axis_index("expert")
    return {
        "x": lax.axis_index("dp"),
        "z": e // (sizes["y"] * sizes["c"]),
        "y": (e // sizes["c"]) % sizes["y"],
        "c": e % sizes["c"],
    }


def expert_of(sizes, at):
    return (at["z"] * sizes["y"] + at["y"]) * sizes["c"] + at["c"]


def device_of(sizes, at):
    return (at["x"], expert_of(sizes, at))


def slot_of(sizes, at, order):
    e = expert_of(sizes, at)
    if "x" in order:
        return at["x"] * (sizes["z"] * sizes["y"] * sizes["c"]) + e
    return e


def nearest(p, k, size):
    if k == 0:
        return p
    if size == 2:
        return 1 - p
    if size == 4:
        return (1 + p % 2, (2 + 3 * p) % 5, 3 - 3 * (p // 2))[k - 1]
    return (p + k) % size


WEIGHT = {"z": 10, "y": 10, "x": 10, "c": 2}


def visits(order, sizes):
    every = itertools.product(*[range(sizes[d]) for d in order])
    return sorted(every, key=lambda ks: (sum(k * WEIGHT[d] for k, d in zip(ks, order)), ks))


def when(condition, action):
    if condition is True:
        action()
    else:
        pl.when(condition)(action)


def greet(names, sizes, at):
    barrier = pltpu.get_barrier_semaphore()
    around = []
    for d in names:
        for step in (1, -1):
            if sizes[d] == 2 and step == 1:
                around.append((True, dict(at, **{d: 1 - at[d]})))
            elif sizes[d] > 2:
                there = at[d] < sizes[d] - 1 if step == 1 else at[d] > 0
                around.append((there, dict(at, **{d: at[d] + step})))
    for there, to in around:
        when(
            there,
            lambda to=to: pl.semaphore_signal(
                barrier, inc=1, device_id=device_of(sizes, to), device_id_type=MESH_ID
            ),
        )
    pl.semaphore_wait(barrier, sum(1 if there is True else there.astype(jnp.int32) for there, _ in around))


def ways(ks, j, order, sizes, at, where):
    d = order[j]
    size = sizes[d]
    if size == 1 or any(ks[j + 1 :]):
        return
    p, q = at[d], where[d]
    if size == 2:
        if ks[j] == 0:
            yield 0, True, dict(at, **{d: 1 - p})
        return
    if ks[j] == 0:
        yield 0, p < size - 1, dict(at, **{d: p + 1})
        yield 1, p > 0, dict(at, **{d: p - 1})
    else:
        yield 0, (q < p) & (p < size - 1), dict(at, **{d: p + 1})
        yield 1, (q > p) & (p > 0), dict(at, **{d: p - 1})


def count_sends(order, sizes):
    total = 0
    zero = {d: 0 for d in order}
    for ks in visits(order, sizes):
        for j in range(len(order)):
            total += len(list(ways(ks, j, order, sizes, zero, zero)))
    return total


def gather_kernel(items, sizes, *refs):
    arrays = items[-1][0] + 1
    count = len(items)
    orders = [order for _, _, order in items]
    ins = [part_of(refs[a], chunk) for a, chunk, _ in items]
    outs = [functools.partial(slot_part, refs[arrays + a], chunk) for a, chunk, _ in items]
    own_sem = refs[2 * arrays]
    sends = refs[2 * arrays + 1 : 2 * arrays + 1 + count]
    recvs = refs[2 * arrays + 1 + count :]
    at = place_of(sizes)
    names = sorted({d for order in orders for d in order})
    greet(names, sizes, at)
    keep = []
    for a in range(count):
        me = slot_of(sizes, at, orders[a])
        own = pltpu.make_async_copy(ins[a], outs[a](me), own_sem.at[a])
        own.start()
        keep.append(own)
    started = []
    plan = []
    for a, order in enumerate(orders):
        for rank, ks in enumerate(visits(order, sizes)):
            weight = sum(k * WEIGHT[d] for k, d in zip(ks, order))
            plan.append((weight, rank, a, ks))
    plan.sort(key=lambda item: item[:3])
    number = [0] * count
    for _, _, a, ks in plan:
        order = orders[a]
        where = dict(at)
        for d, k in zip(order, ks):
            where[d] = nearest(at[d], k, sizes[d])
        slot = slot_of(sizes, where, order)
        here = outs[a](slot)
        if any(ks):
            pltpu.make_async_copy(here, here, recvs[a].at[slot]).wait()
            source = here
        else:
            source = ins[a]
        for j in reversed(range(len(order))):
            for _, there, to in ways(ks, j, order, sizes, at, where):
                copy = pltpu.make_async_remote_copy(
                    src_ref=source,
                    dst_ref=here,
                    send_sem=sends[a].at[number[a]],
                    recv_sem=recvs[a].at[slot],
                    device_id=device_of(sizes, to),
                    device_id_type=MESH_ID,
                )
                number[a] += 1
                when(there, copy.start)
                started.append((there, copy))
    for there, copy in started:
        when(there, copy.wait_send)
    for own in keep:
        own.wait()


def part_of(ref, chunk):
    return ref if chunk is None else ref.at[chunk]


def slot_part(ref, chunk, slot):
    return ref.at[slot] if chunk is None else ref.at[slot, chunk]


def items_of(orders, shapes):
    items = []
    for a, (order, shape) in enumerate(zip(orders, shapes)):
        if len(shape) == 2:
            items.append((a, None, order))
        else:
            for chunk in range(shape[0]):
                items.append((a, chunk, order[chunk] if isinstance(order, list) else order))
    return items


def members(sizes, order):
    return math.prod(sizes[d] for d in order)


def gather(arrays, orders, identity):
    sizes = dims_of()
    items = items_of(orders, [a.shape for a in arrays])
    totals = {a: members(sizes, order) for a, _, order in items}
    sent = sum(totals[i] * a.size * a.dtype.itemsize for i, a in enumerate(arrays))
    return pl.pallas_call(
        functools.partial(gather_kernel, items, sizes),
        out_shape=[jax.ShapeDtypeStruct((totals[i],) + a.shape, a.dtype) for i, a in enumerate(arrays)],
        in_specs=[ANYWHERE] * len(arrays),
        out_specs=[ANYWHERE] * len(arrays),
        scratch_shapes=[pltpu.SemaphoreType.DMA((len(items),))]
        + [pltpu.SemaphoreType.DMA((count_sends(order, sizes),)) for _, _, order in items]
        + [pltpu.SemaphoreType.DMA((totals[a],)) for a, _, _ in items],
        compiler_params=pltpu.CompilerParams(collective_id=identity, has_side_effects=True),
        cost_estimate=pl.CostEstimate(flops=0, bytes_accessed=sent // 16, transcendentals=0),
    )(*arrays)


def box_of(j, order, sizes, where, extra):
    base = 0
    for i in range(j):
        base += math.prod(sizes[d] for d in order[:i]) * boxes_along(sizes[order[i]])
    inner = 0
    for d in order[:j]:
        inner = inner * sizes[d] + where[d]
    wide = boxes_along(sizes[order[j]])
    last = 0 if wide == 1 else (sizes[order[j]] if extra else where[order[j]])
    return base + inner * wide + last


def boxes_along(size):
    return {1: 0, 2: 1}.get(size, size + 1)


def boxes(order, sizes):
    return sum(
        math.prod(sizes[d] for d in order[:i]) * boxes_along(sizes[order[i]])
        for i in range(len(order))
    )


def staged_of(order, sizes, where):
    inner = 0
    for d in order[:-1]:
        inner = inner * sizes[d] + where[d]
    return inner


def add_up(target, terms, dtype):
    rows = target.shape[0]
    step = 16 if rows % 16 == 0 else rows

    def one(i, carry):
        part = pl.ds(pl.multiple_of(i * step, step), step)
        total = terms[0][part, :].astype(jnp.float32)
        for term in terms[1:]:
            total = total + term[part, :].astype(jnp.float32)
        target[part, :] = total.astype(dtype)
        return carry

    lax.fori_loop(0, rows // step, one, 0)


def scatter_kernel(items, sizes, *refs):
    arrays = items[-1][0] + 1
    count = len(items)
    orders = [order for _, _, order in items]
    ins = [functools.partial(slot_part, refs[a], chunk) for a, chunk, _ in items]
    outs = [part_of(refs[arrays + a], chunk) for a, chunk, _ in items]
    refs = refs[2 * arrays :]
    staged, landed, sends, recvs, loads = [
        refs[i * count : (i + 1) * count] for i in range(5)
    ]
    at = place_of(sizes)
    names = sorted({d for order in orders for d in order})
    plan = []
    for a, order in enumerate(orders):
        for rank, ks in enumerate(visits(order, sizes)):
            weight = sum(k * WEIGHT[d] for k, d in zip(ks, order))
            plan.append((weight, rank, a, ks))
    plan.sort(key=lambda item: item[:3], reverse=True)
    slots = {}
    for _, _, a, ks in plan:
        order = orders[a]
        where = dict(at)
        for d, k in zip(order, ks):
            where[d] = nearest(at[d], k, sizes[d])
        slots[a, ks] = (where, slot_of(sizes, where, order))
    for _, _, a, ks in plan:
        if ks[-1] == 0:
            where, slot = slots[a, ks]
            index = staged_of(orders[a], sizes, where)
            pltpu.make_async_copy(
                ins[a](slot), staged[a].at[index], loads[a].at[index]
            ).start()
    greet(names, sizes, at)
    started = []
    number = [0] * count

    def send(a, source, box, to, there):
        copy = pltpu.make_async_remote_copy(
            src_ref=source,
            dst_ref=landed[a].at[box],
            send_sem=sends[a].at[number[a]],
            recv_sem=recvs[a].at[box],
            device_id=device_of(sizes, to),
            device_id_type=MESH_ID,
        )
        number[a] += 1
        when(there, copy.start)
        started.append((there, copy))

    for _, _, a, ks in plan:
        if ks[-1]:
            order = orders[a]
            where, slot = slots[a, ks]
            j = len(order) - 1
            to = dict(at, **{order[j]: 1 - at[order[j]]})
            send(a, ins[a](slot), box_of(j, order, sizes, where, False), to, True)
    for _, _, a, ks in plan:
        if ks[-1]:
            continue
        order = orders[a]
        where, slot = slots[a, ks]
        index = staged_of(order, sizes, where)
        mine = staged[a].at[index]
        pltpu.make_async_copy(ins[a](slot), mine, loads[a].at[index]).wait()
        leaves = max([j for j in range(len(order)) if ks[j]], default=-1)
        terms = [mine]
        loose = []
        for j in reversed(range(len(order))):
            d = order[j]
            if j < leaves or sizes[d] == 1:
                break
            if sizes[d] == 2:
                if ks[j] == 0:
                    box = box_of(j, order, sizes, where, False)
                    terms.append((box, True))
                continue
            p, q = at[d], where[d]
            if j == leaves:
                far = ((q > p) & (p > 0)) | ((q < p) & (p < sizes[d] - 1))
                terms.append((box_of(j, order, sizes, where, False), far))
            else:
                terms.append((box_of(j, order, sizes, where, False), p > 0))
                terms.append((box_of(j, order, sizes, where, True), p < sizes[d] - 1))
        sure = [mine]
        for box, there in terms[1:]:
            ref = landed[a].at[box]
            waiting = pltpu.make_async_copy(ref, ref, recvs[a].at[box])
            if there is True:
                waiting.wait()
                sure.append(ref)
            else:

                def take(ref=ref, waiting=waiting, mine=mine):
                    waiting.wait()
                    add_up(mine, [mine, ref], mine.dtype)

                loose.append((there, take))
        if len(sure) > 1 and leaves >= 0:
            add_up(mine, sure, mine.dtype)
            sure = [mine]
        for there, take in loose:
            when(there, take)
        if leaves < 0:
            add_up(outs[a], sure, outs[a].dtype)
            continue
        d = order[leaves]
        if sizes[d] == 2:
            send(
                a,
                mine,
                box_of(leaves, order, sizes, where, False),
                dict(at, **{d: 1 - at[d]}),
                True,
            )
        else:
            p, q = at[d], where[d]
            send(
                a, mine, box_of(leaves, order, sizes, where, False), dict(at, **{d: p + 1}), q > p
            )
            send(
                a,
                mine,
                jnp.where(
                    q + 1 == p,
                    box_of(leaves, order, sizes, where, True),
                    box_of(leaves, order, sizes, where, False),
                ),
                dict(at, **{d: p - 1}),
                q < p,
            )
    for there, copy in started:
        when(there, copy.wait_send)


def scatter_sends(order, sizes):
    total = 0
    for ks in visits(order, sizes):
        leaves = max([j for j in range(len(order)) if ks[j]], default=-1)
        if leaves >= 0:
            total += 1 if sizes[order[leaves]] == 2 else 2
    return total


def scatter(arrays, orders, identity, out_dtype=jnp.float32):
    sizes = dims_of()
    items = items_of(orders, [a.shape[1:] for a in arrays])
    shapes = [arrays[a].shape[-2:] for a, _, _ in items]
    types = [arrays[a].dtype for a, _, _ in items]
    orders = [order for _, _, order in items]
    stages = [math.prod(sizes[d] for d in order[:-1]) for order in orders]
    landing = [boxes(order, sizes) for order in orders]
    return pl.pallas_call(
        functools.partial(scatter_kernel, items, sizes),
        out_shape=[jax.ShapeDtypeStruct(a.shape[1:], out_dtype) for a in arrays],
        in_specs=[ANYWHERE] * len(arrays),
        out_specs=[pl.BlockSpec(memory_space=pltpu.VMEM)] * len(arrays),
        scratch_shapes=[pltpu.VMEM((n,) + s, t) for n, s, t in zip(stages, shapes, types)]
        + [pltpu.VMEM((n,) + s, t) for n, s, t in zip(landing, shapes, types)]
        + [pltpu.SemaphoreType.DMA((scatter_sends(order, sizes),)) for order in orders]
        + [pltpu.SemaphoreType.DMA((n,)) for n in landing]
        + [pltpu.SemaphoreType.DMA((n,)) for n in stages],
        compiler_params=pltpu.CompilerParams(
            collective_id=identity, has_side_effects=True, vmem_limit_bytes=60 << 20
        ),
    )(*arrays)


PLANE = ("z", "y", "c")
ZYX = ("z", "y", "x", "c")
ZXY = ("z", "x", "y", "c")
XYZ = ("x", "y", "z", "c")
YZ = ("y", "z", "c")
CHUNKS = 4
CHUNK_ORDERS = [PLANE, PLANE, PLANE, YZ]
YZX = ("y", "z", "x", "c")
ALL_ORDERS = [[ZYX, ZXY], XYZ, XYZ, [ZXY, ZYX], XYZ]


def gather_plane(x):
    return lax.all_gather(x, "expert", axis=0, tiled=False)


def scatter_plane(x):
    return lax.psum_scatter(x, "expert", scatter_dimension=0, tiled=False)


def low(x):
    return x.astype(jnp.bfloat16)


def wide(x):
    return x.astype(jnp.float32)


def dot(a, b):
    return jnp.dot(a, b, preferred_element_type=jnp.float32)


def fetch_dp(x, axis):
    if lax.axis_size("dp") != 2:
        return x, lax.all_gather(x, "dp", axis=axis, tiled=True)
    return x, lax.ppermute(x, "dp", [(0, 1), (1, 0)])


def joined(pair, axis):
    own, other = pair
    if lax.axis_size("dp") != 2:
        return other
    first = lax.axis_index("dp") == 0
    return jnp.concatenate(
        [jnp.where(first, own, other), jnp.where(first, other, own)], axis=axis
    )


def send_dp(x, axis):
    if lax.axis_size("dp") != 2:
        total = lax.psum_scatter(x, "dp", scatter_dimension=axis, tiled=True)
        return total, jnp.zeros_like(total)
    half = x.shape[axis] // 2
    index = lax.axis_index("dp")
    away = lax.dynamic_slice_in_dim(x, (1 - index) * half, half, axis)
    arrived = lax.ppermute(away, "dp", [(0, 1), (1, 0)])
    return lax.dynamic_slice_in_dim(x, index * half, half, axis), arrived


def added(pair):
    return pair[0].astype(jnp.float32) + pair[1].astype(jnp.float32)


def cross(a, b):
    return lax.dot_general(a, b, (((1,), (1,)), ((), ())), preferred_element_type=jnp.float32)


HEADS = 2


def spread_matrix(quads, dtype):
    half = ROPE // 2
    source = lax.broadcasted_iota(jnp.int32, (128, 256), 0)
    target = lax.broadcasted_iota(jnp.int32, (128, 256), 1)
    wanted = target % half + half * (target // (half * quads))
    return (source == wanted).astype(jnp.float32).astype(dtype)


def head_query(u, rows, qn, qa, qb):
    quads = qa.shape[1] // (ROPE // 2)
    lanes = lax.broadcasted_iota(jnp.int32, (1, qa.shape[1]), 1) // (ROPE // 2)
    ours = lanes == (pl.program_id(0) * HEADS + u) % quads
    nothing = jnp.zeros((), qa.dtype)
    parts = jnp.concatenate(
        [jnp.where(ours, qa[rows, :], nothing), jnp.where(ours, qb[rows, :], nothing)], axis=1
    )
    turned = low(cross(parts, spread_matrix(quads, jnp.bfloat16)))
    return ours, jnp.concatenate([qn[rows, u * NOPE : (u + 1) * NOPE], turned], axis=1)


def load_window(tokens, span, line, window, sems):
    lane = lax.axis_index("expert")
    copies = []
    for j in range(span):
        source = lane - (span - 1) + j
        rows = pl.ds(j * tokens, tokens)
        for m in range(MICRO):
            copy = pltpu.make_async_copy(
                line.at[jnp.maximum(source, 0), pl.ds(m * tokens, tokens)],
                window.at[m, rows],
                sems.at[m, j],
            )
            pl.when(source >= 0)(copy.start)
            copies.append((source >= 0, copy))

            @pl.when(source < 0)
            def _(m=m, rows=rows):
                window[m, rows] = jnp.zeros((tokens, window.shape[2]), window.dtype)

    left = window.shape[1] - span * tokens
    if left:
        for m in range(MICRO):
            window[m, pl.ds(span * tokens, left)] = jnp.zeros((left, window.shape[2]), window.dtype)
    for there, copy in copies:
        pl.when(there)(copy.wait)


def attend_kernel(tokens, span, scale, qn, qa, qb, line, expand, bias, out, window, sems):
    @pl.when(pl.program_id(0) == 0)
    def _():
        load_window(tokens, span, line, window, sems)

    for m in range(MICRO):
        rows = pl.ds(m * tokens, tokens)
        pairs = low(dot(window[m, :, :LAT], expand[...]))
        turns = window[m, :, LAT:]
        for u in range(HEADS):
            pair = pairs[:, u * (NOPE + VDIM) : (u + 1) * (NOPE + VDIM)]
            keys = jnp.concatenate([pair[:, :NOPE], turns], axis=1)
            _, own = head_query(u, rows, qn, qa, qb)
            scores = cross(own, keys) * scale + bias[m]
            raised = jnp.exp(scores - jnp.max(scores, axis=1, keepdims=True))
            weights = low(raised * (1.0 / jnp.sum(raised, axis=1, keepdims=True)))
            out[rows, u * VDIM : (u + 1) * VDIM] = low(dot(weights, pair[:, NOPE:]))


def attend_back_kernel(
    tokens, span, scale, qn, qa, qb, grad, line, expand, bias, gqn, gqa, gqb, gline, gexp, *scratch
):
    window, upright, glat, gturns, gwindow, zeros, sems, out_sems = scratch
    head = pl.program_id(0)
    quads = qa.shape[1] // (ROPE // 2)

    @pl.when(head == 0)
    def _():
        load_window(tokens, span, line, window, sems)
        for m in range(MICRO):
            upright[m] = window[m, :, :LAT].T
        glat[...] = jnp.zeros_like(glat)
        gturns[...] = jnp.zeros_like(gturns)

    @pl.when((head * HEADS) % quads == 0)
    def _():
        gqa[...] = jnp.zeros_like(gqa)
        gqb[...] = jnp.zeros_like(gqb)

    expand_total = None
    for m in range(MICRO):
        rows = pl.ds(m * tokens, tokens)
        pairs = low(dot(window[m, :, :LAT], expand[...]))
        turns = window[m, :, LAT:]
        grad_pairs = []
        turns_total = None
        for u in range(HEADS):
            pair = pairs[:, u * (NOPE + VDIM) : (u + 1) * (NOPE + VDIM)]
            keys = jnp.concatenate([pair[:, :NOPE], turns], axis=1)
            ours, own = head_query(u, rows, qn, qa, qb)
            grad_rows = grad[rows, u * VDIM : (u + 1) * VDIM]
            scores = cross(keys, own) * scale + bias[m]
            raised = jnp.exp(scores - jnp.max(scores, axis=0, keepdims=True))
            probs = raised * (1.0 / jnp.sum(raised, axis=0, keepdims=True))
            grad_probs = cross(pair[:, NOPE:], grad_rows)
            shift = jnp.sum(grad_probs * probs, axis=0, keepdims=True)
            back = low(probs * (grad_probs - shift))
            grad_own = dot(back.T, keys) * scale
            gqn[rows, u * NOPE : (u + 1) * NOPE] = low(grad_own[:, :NOPE])
            spread = lax.dot_general(
                grad_own[:, NOPE:],
                spread_matrix(quads, jnp.float32),
                (((1,), (0,)), ((), ())),
                precision=HIGHEST_PRECISION,
                preferred_element_type=jnp.float32,
            )
            gqa[rows, :] += jnp.where(ours, spread[:, :128], 0.0)
            gqb[rows, :] += jnp.where(ours, spread[:, 128:], 0.0)
            grad_keys = dot(back, own) * scale
            turned = grad_keys[:, NOPE:]
            turns_total = turned if turns_total is None else turns_total + turned
            grad_pairs.append(low(grad_keys[:, :NOPE]))
            grad_pairs.append(low(dot(low(probs), grad_rows)))
        gturns[m] += turns_total
        both = jnp.concatenate(grad_pairs, axis=1)
        glat[m] += cross(both, expand[...])
        part = dot(upright[m], both)
        expand_total = part if expand_total is None else expand_total + part
    gexp[...] = low(expand_total)

    @pl.when(head == pl.num_programs(0) - 1)
    def _():
        lane = lax.axis_index("expert")
        zeros[...] = jnp.zeros_like(zeros)
        for m in range(MICRO):
            gwindow[m, :, :LAT] = low(glat[m])
            gwindow[m, :, LAT:] = low(gturns[m])
        copies = []
        for slot in range(gline.shape[0]):
            j = slot - lane + span - 1
            inside = (j >= 0) & (j < span)
            start = pl.multiple_of(jnp.clip(j, 0, span - 1) * tokens, tokens)
            for m in range(MICRO):
                target = gline.at[slot, pl.ds(m * tokens, tokens)]
                sem = out_sems.at[slot, m]
                full = pltpu.make_async_copy(gwindow.at[m, pl.ds(start, tokens)], target, sem)
                empty = pltpu.make_async_copy(zeros, target, sem)
                pl.when(inside)(full.start)
                pl.when(jnp.logical_not(inside))(empty.start)
                copies.append(full)
        for copy in copies:
            copy.wait()


def whole_block(a):
    return pl.BlockSpec(a.shape, lambda h: (0,) * len(a.shape))


def attention_specs(rows, quads):
    return [
        pl.BlockSpec((rows, HEADS * NOPE), lambda h: (0, h)),
        pl.BlockSpec((rows, 128), lambda h: (0, h * HEADS // quads)),
        pl.BlockSpec((rows, 128), lambda h: (0, h * HEADS // quads)),
    ]


def attention_forward(tokens, span, scale, qn, qa, qb, line, expand, bias):
    rows = qn.shape[0]
    quads = 128 // (ROPE // 2)
    key_rows = bias.shape[2]
    return pl.pallas_call(
        functools.partial(attend_kernel, tokens, span, scale),
        grid=(H // HEADS,),
        out_shape=jax.ShapeDtypeStruct((rows, H * VDIM), jnp.bfloat16),
        in_specs=attention_specs(rows, quads)
        + [ANYWHERE, pl.BlockSpec((LAT, HEADS * (NOPE + VDIM)), lambda h: (0, h)), whole_block(bias)],
        out_specs=pl.BlockSpec((rows, HEADS * VDIM), lambda h: (0, h)),
        scratch_shapes=[
            pltpu.VMEM((MICRO, key_rows, line.shape[2]), jnp.bfloat16),
            pltpu.SemaphoreType.DMA((MICRO, span)),
        ],
        compiler_params=pltpu.CompilerParams(vmem_limit_bytes=56 << 20),
        cost_estimate=pl.CostEstimate(
            flops=10**9, bytes_accessed=10**6, transcendentals=0
        ),
    )(qn, qa, qb, line, expand, bias)


def attention_backward(tokens, span, scale, qn, qa, qb, grad, line, expand, bias):
    rows = qn.shape[0]
    quads = 128 // (ROPE // 2)
    key_rows = bias.shape[1]
    width = line.shape[2]
    single = jax.ShapeDtypeStruct
    return pl.pallas_call(
        functools.partial(attend_back_kernel, tokens, span, scale),
        grid=(H // HEADS,),
        out_shape=[
            single(qn.shape, jnp.bfloat16),
            single(qa.shape, jnp.float32),
            single(qb.shape, jnp.float32),
            single(line.shape, jnp.bfloat16),
            single(expand.shape, jnp.bfloat16),
        ],
        in_specs=attention_specs(rows, quads)
        + [pl.BlockSpec((rows, HEADS * VDIM), lambda h: (0, h)), ANYWHERE]
        + [pl.BlockSpec((LAT, HEADS * (NOPE + VDIM)), lambda h: (0, h)), whole_block(bias)],
        out_specs=attention_specs(rows, quads)
        + [ANYWHERE, pl.BlockSpec((LAT, HEADS * (NOPE + VDIM)), lambda h: (0, h))],
        scratch_shapes=[
            pltpu.VMEM((MICRO, key_rows, width), jnp.bfloat16),
            pltpu.VMEM((MICRO, LAT, key_rows), jnp.bfloat16),
            pltpu.VMEM((MICRO, key_rows, LAT), jnp.float32),
            pltpu.VMEM((MICRO, key_rows, 128), jnp.float32),
            pltpu.VMEM((MICRO, key_rows, width), jnp.bfloat16),
            pltpu.VMEM((tokens, width), jnp.bfloat16),
            pltpu.SemaphoreType.DMA((MICRO, span)),
            pltpu.SemaphoreType.DMA((line.shape[0], MICRO)),
        ],
        compiler_params=pltpu.CompilerParams(vmem_limit_bytes=56 << 20),
        cost_estimate=pl.CostEstimate(
            flops=60 * 10**9, bytes_accessed=30 * 10**6, transcendentals=0
        ),
    )(qn, qa, qb, grad, line, expand, bias)


def combine_kernel(picked, rows, left, right, out):
    beside = dot(left[...], right[...])
    height = picked.shape[1]
    for i in range(picked.shape[0]):
        part = slice(i * height, (i + 1) * height)
        out[part, :] = low(beside[part, :] + dot(picked[i], rows[i]))


def combine(picked, rows, left, right):
    groups, group_rows, slots = picked.shape
    total, inner = left.shape
    step = 2 if groups % 2 == 0 else 1
    return pl.pallas_call(
        combine_kernel,
        grid=(groups // step,),
        out_shape=jax.ShapeDtypeStruct((total, D), jnp.bfloat16),
        in_specs=[
            pl.BlockSpec((step, group_rows, slots), lambda g: (g, 0, 0)),
            pl.BlockSpec((step, slots, D), lambda g: (g, 0, 0)),
            pl.BlockSpec((step * group_rows, inner), lambda g: (g, 0)),
            pl.BlockSpec((inner, D), lambda g: (0, 0)),
        ],
        out_specs=pl.BlockSpec((step * group_rows, D), lambda g: (g, 0)),
        compiler_params=pltpu.CompilerParams(vmem_limit_bytes=48 << 20),
        cost_estimate=pl.CostEstimate(
            flops=2 * total * (slots + inner) * D,
            bytes_accessed=total * D * 4,
            transcendentals=0,
        ),
    )(picked, rows.reshape(groups, slots, D), left, right)


def halves_of(x):
    parts = 2 if x.shape[0] % 32 == 0 else 1
    return x.reshape(parts, x.shape[0] // parts, x.shape[1])


def body(
    layer_input,
    cotangent,
    doc_lengths,
    routes,
    attention_gain,
    query_weight,
    latent_weight,
    latent_gain,
    expand_weight,
    output_weight,
    feed_gain,
    router_weight,
    shared_gate,
    shared_up,
    shared_down,
    expert_gate,
    expert_up,
    expert_down,
):
    n_dp = lax.axis_size("dp")
    n_expert = lax.axis_size("expert")
    devices = n_dp * n_expert
    lane = lax.axis_index("expert")
    tokens = layer_input.shape[2]
    rows = MICRO * tokens
    experts_count = router_weight.shape[1]
    score_scale = (NOPE + ROPE) ** (-0.5)
    head_width = NOPE + ROPE
    key_width = H * head_width

    shard = query_weight.shape[0]
    small_latent = latent_gain.shape[0]
    small = jnp.concatenate(
        [
            router_weight,
            attention_gain[:, None],
            feed_gain[:, None],
            jnp.pad(latent_gain, (0, shard - small_latent))[:, None],
        ],
        axis=1,
    )
    small = jnp.pad(small, ((0, 0), (0, 128 - small.shape[1])))
    by_head = query_weight.reshape(shard, H, head_width)
    split_query = jnp.concatenate(
        [
            by_head[..., :NOPE].reshape(shard, H * NOPE),
            by_head[..., NOPE : NOPE + ROPE // 2].reshape(shard, H * ROPE // 2),
            by_head[..., NOPE + ROPE // 2 :].reshape(shard, H * ROPE // 2),
        ],
        axis=1,
    )
    all_query, all_latent, all_expand, all_output, small = gather(
        [
            halves_of(split_query),
            latent_weight,
            expand_weight.reshape(16, -1),
            halves_of(output_weight.T),
            small,
        ],
        ALL_ORDERS,
        1,
    )
    all_query = all_query.reshape(D, key_width)
    all_latent = all_latent.reshape(D, LAT + ROPE)
    all_expand = all_expand.reshape(LAT, H * (NOPE + VDIM))
    all_output = all_output.reshape(D, H * VDIM)
    gain_latent = small[:, :small_latent, experts_count + 2].reshape(LAT).astype(jnp.float32)
    small = small.reshape(D, 128)
    all_router = small[:, :experts_count]
    gain_first = small[:, experts_count].astype(jnp.float32)
    gain_second = small[:, experts_count + 1].astype(jnp.float32)

    (later, all_query) = lax.optimization_barrier(
        (
            (expert_gate, expert_up, expert_down, shared_gate, shared_up, shared_down),
            all_query,
        )
    )
    expert_gate, expert_up, expert_down, shared_gate, shared_up, shared_down = later
    parts_gate = fetch_dp(expert_gate[0], 0)
    parts_up = fetch_dp(expert_up[0], 0)
    parts_down = fetch_dp(expert_down[0], 1)
    units = shared_down.shape[0]
    mine = n_dp * units
    both = jnp.stack([shared_gate, shared_up], axis=1).reshape(shard, 2, n_dp, n_expert, units)
    both = both.transpose(3, 0, 1, 2, 4).reshape(n_expert, shard, 2 * mine)
    both = lax.all_to_all(both, "expert", split_axis=0, concat_axis=0, tiled=True)
    parts_in = fetch_dp(both.reshape(n_expert * shard, 2 * mine), 0)
    parts_out = fetch_dp(shared_down, 0)

    positions = lane * tokens + jnp.arange(tokens, dtype=jnp.int32)
    cosine_table, sine_table = angles(positions)
    cosine_rows = jnp.tile(cosine_table, (MICRO, 1))
    sine_rows = jnp.tile(sine_table, (MICRO, 1))
    head_cosine = jnp.tile(cosine_rows, (1, H))
    head_sine = jnp.tile(sine_rows, (1, H))
    inputs = layer_input[0].reshape(rows, D).astype(jnp.float32)
    hidden = low(root_normalize(inputs, gain_first))
    latent = dot(hidden, all_latent)
    compressed = low(root_normalize(latent[:, :LAT], gain_latent))
    key_rope = low(rotate(latent[:, LAT:], cosine_rows, sine_rows))
    payload = jnp.concatenate(
        [compressed, key_rope, jnp.zeros((rows, 128 - ROPE), jnp.bfloat16)], axis=1
    )
    columns = jnp.pad(routes[0].reshape(rows, TOP).T, ((0, 8 - TOP), (0, 0)))
    line, all_routes = gather([payload, columns], [PLANE, PLANE], 2)
    cotangent_rows = cotangent[0].reshape(rows, D)
    first_half, line = lax.optimization_barrier((cotangent_rows[:, : D // 2], line))
    first_half = gather_plane(first_half).reshape(n_expert * rows, D // 2)
    query = dot(hidden, all_query)
    plain = H * NOPE
    half = H * ROPE // 2
    query_plain = low(query[:, :plain])
    turn_first = query[:, plain : plain + half]
    turn_second = query[:, plain + half :]
    query_first = low(turn_first * head_cosine - turn_second * head_sine)
    query_second = low(turn_first * head_sine + turn_second * head_cosine)
    reach = (WINDOW + tokens - 2) // tokens
    span = reach + 1
    key_rows = -(-span * tokens // 128) * 128
    key_positions = (lane - reach) * tokens + jnp.arange(key_rows, dtype=jnp.int32)
    apart = positions[:, None] - key_positions[None, :]
    reachable = (key_positions[None, :] >= 0) & (apart >= 0) & (apart < WINDOW)
    allowed = jnp.stack(
        [
            reachable
            & (
                segment_of(positions, doc_lengths[0, m])[:, None]
                == segment_of(key_positions, doc_lengths[0, m])[None, :]
            )
            for m in range(MICRO)
        ]
    )
    bias = jnp.where(allowed, 0.0, NEGATIVE).astype(jnp.float32)
    mixture = attention_forward(
        tokens,
        span,
        score_scale,
        query_plain,
        query_first,
        query_second,
        line,
        all_expand,
        bias,
    )
    residual = inputs + transposed_right(mixture, all_output)
    normed = low(root_normalize(residual, gain_second))

    chunked = normed.reshape(CHUNKS, rows // CHUNKS, D)
    own_probs = jax.nn.softmax(dot(normed, all_router), axis=-1)
    all_normed, all_probs = gather([chunked, own_probs.T], [CHUNK_ORDERS, PLANE], 3)
    all_normed = all_normed.reshape(n_expert * rows, D)
    fetched = (parts_gate, parts_up, parts_down, parts_in, parts_out)
    second_half, all_normed = lax.optimization_barrier((cotangent_rows[:, D // 2 :], all_normed))
    fetched = [lax.optimization_barrier((pair, all_normed))[0] for pair in fetched]
    second_half = gather_plane(second_half).reshape(n_expert * rows, D // 2)
    cotangent_halves = (first_half, second_half)
    expert_gate, expert_up = joined(fetched[0], 0), joined(fetched[1], 0)
    expert_down = joined(fetched[2], 1)
    padded = -(-mine // 128) * 128
    shared_out_weight = jnp.pad(joined(fetched[4], 0), ((0, padded - mine), (0, 0)))
    total_rows = n_expert * rows
    capacity = (9 * tokens * TOP + 8 * experts_count - 1) // (8 * experts_count)
    per_group = max(1, 256 // tokens)
    group_rows = per_group * tokens
    groups = total_rows // group_rows
    slots = -(-per_group * capacity // 16) * 16
    named = jnp.any(all_routes[:, :TOP] == lane, axis=1).reshape(-1, tokens).astype(jnp.int32)
    rank = jnp.cumsum(named, axis=1) - named
    kept = (named > 0) & (rank < capacity)
    offset = (jnp.arange(named.shape[0], dtype=jnp.int32) % per_group) * capacity
    place = jnp.where(kept, rank + offset[:, None], -1).reshape(groups, 1, group_rows)
    picked_bool = place == jnp.arange(slots, dtype=jnp.int32)[None, :, None]
    picked = picked_bool.astype(jnp.bfloat16)
    picked_float = picked_bool.astype(jnp.float32)
    gate_rows = lax.dynamic_index_in_dim(all_probs, lane, 1, keepdims=False)
    gate_slots = jnp.sum(
        picked_float * gate_rows.reshape(groups, 1, group_rows), axis=2
    ).reshape(groups * slots, 1)

    def to_slots(x):
        return low(
            jnp.einsum(
                "gst,gtd->gsd",
                picked,
                x.reshape(groups, group_rows, x.shape[1]),
                preferred_element_type=jnp.float32,
            )
        ).reshape(groups * slots, x.shape[1])

    arrived = to_slots(all_normed)
    gate_pre = low(dot(arrived, expert_gate))
    up_pre = low(dot(arrived, expert_up))
    parts_in, gate_pre = lax.optimization_barrier((fetched[3], gate_pre))
    shared_in = jnp.pad(
        joined(parts_in, 0).reshape(D, 2, mine), ((0, 0), (0, 0), (0, padded - mine))
    ).reshape(D, 2 * padded)
    shared_pre = low(dot(all_normed, shared_in))
    expert_act = low(silu_product(wide(gate_pre), wide(up_pre)))
    expert_out = lax.optimization_barrier(low(dot(expert_act, expert_down)))
    shared_act = low(silu_product(wide(shared_pre[:, :padded]), wide(shared_pre[:, padded:])))
    spread = jnp.swapaxes(picked, 1, 2)
    partial_out = combine(
        spread, low(gate_slots * expert_out.astype(jnp.float32)), shared_act, shared_out_weight
    )
    expert_sum = scatter_plane(partial_out.reshape(n_expert, rows, D))
    layer_output = low(residual + expert_sum.astype(jnp.float32))

    arrived_grad = jnp.concatenate([to_slots(x) for x in cotangent_halves], axis=1)
    gate_dots = jnp.sum(
        expert_out.astype(jnp.float32) * arrived_grad.astype(jnp.float32), axis=1
    ).reshape(groups, slots, 1)
    gate_grad_rows = jnp.sum(picked_float * gate_dots, axis=1).reshape(n_expert, rows)
    gate_grads = lax.all_to_all(
        gate_grad_rows, "expert", split_axis=0, concat_axis=0, tiled=True
    ).T
    slot_grad = low(gate_slots * arrived_grad.astype(jnp.float32))
    expert_down_grad = low(transposed_left(expert_act, slot_grad))
    gate_back, up_back = silu_back(
        wide(gate_pre), wide(up_pre), transposed_right(slot_grad, expert_down)
    )
    gate_back = low(gate_back)
    up_back = low(up_back)
    expert_gate_grad = low(transposed_left(arrived, gate_back))
    expert_up_grad = low(transposed_left(arrived, up_back))
    rows_grad = low(
        transposed_right(gate_back, expert_gate) + transposed_right(up_back, expert_up)
    )
    shared_back = jnp.concatenate(
        silu_back(
            wide(shared_pre[:, :padded]),
            wide(shared_pre[:, padded:]),
            transposed_right(cotangent_halves[0], shared_out_weight[:, : D // 2])
            + transposed_right(cotangent_halves[1], shared_out_weight[:, D // 2 :]),
        ),
        axis=1,
    ).astype(jnp.bfloat16)
    partial_normed = combine(spread, rows_grad, shared_back, shared_in.T)
    partial_normed = partial_normed.reshape(n_expert, CHUNKS, rows // CHUNKS, D)
    (grad_normed,) = scatter([partial_normed], [CHUNK_ORDERS], 4)
    grad_normed = grad_normed.reshape(rows, D)
    sums = [
        send_dp(expert_gate_grad, 0),
        send_dp(expert_up_grad, 0),
        send_dp(expert_down_grad, 1),
        send_dp(
            jnp.concatenate(
                [low(transposed_left(shared_act, x)[:mine]) for x in cotangent_halves], axis=1
            ),
            0,
        ),
        send_dp(low(transposed_left(all_normed, shared_back)), 0),
    ]

    logit_grad = low(
        own_probs * (gate_grads - jnp.sum(gate_grads * own_probs, axis=-1, keepdims=True))
    )
    wide_logits = jnp.pad(logit_grad, ((0, 0), (0, 128 - experts_count)))
    router_weight_grad = transposed_left(normed, wide_logits)
    grad_normed = grad_normed + transposed_right(logit_grad, all_router)
    residual_extra, feed_gain_grad = normalize_back(residual, gain_second, grad_normed)
    grad_residual = cotangent[0].reshape(rows, D).astype(jnp.float32) + residual_extra

    grad_attn = low(grad_residual)
    output_grad = low(transposed_left(grad_attn, mixture))
    middle = output_grad.shape[1] // 2
    later_grad = output_grad[:, middle:].reshape(devices, shard, middle)
    output_grad = lax.psum_scatter(
        output_grad[:, :middle], ("dp", "expert"), scatter_dimension=0, tiled=True
    )
    grad_mixture = low(dot(grad_attn, all_output))
    grad_plain, grad_first, grad_second, grad_line, expand_grad = attention_backward(
        tokens,
        span,
        score_scale,
        query_plain,
        query_first,
        query_second,
        grad_mixture,
        line,
        all_expand,
        jnp.swapaxes(bias, 1, 2),
    )
    grad_query = jnp.concatenate(
        [
            grad_plain,
            low(grad_first * head_cosine + grad_second * head_sine),
            low(grad_second * head_cosine - grad_first * head_sine),
        ],
        axis=1,
    )
    query_grad = low(transposed_left(hidden, grad_query))
    grad_line, query_grad, expand_grad = scatter(
        [
            grad_line,
            query_grad.reshape(devices, shard, key_width),
            expand_grad.reshape(devices, 16, -1),
        ],
        [PLANE, ZYX, XYZ],
        5,
    )
    sums, grad_line = lax.optimization_barrier((sums, grad_line))
    expert_grads = [added(pair)[None] for pair in sums[:3]]
    shared_down_grad = added(sums[3])
    shared_in_grad = low(added(sums[4])).reshape(n_expert, shard, 2, padded)[..., :mine]
    shared_in_grad = lax.all_to_all(
        shared_in_grad.reshape(n_expert, shard, 2 * mine),
        "expert",
        split_axis=0,
        concat_axis=0,
        tiled=True,
    ).astype(jnp.float32)
    shared_in_grad = (
        shared_in_grad.reshape(n_expert, shard, 2, n_dp, units)
        .transpose(2, 1, 3, 0, 4)
        .reshape(2, shard, n_dp * n_expert * units)
    )
    latent_part, latent_gain_grad = normalize_back(
        latent[:, :LAT], gain_latent, grad_line[:, :LAT]
    )
    grad_key_rope = rotate(grad_line[:, LAT : LAT + ROPE], cosine_rows, -sine_rows)
    grad_latent = low(jnp.concatenate([latent_part, grad_key_rope], axis=1))
    latent_grad = transposed_left(hidden, grad_latent)
    grad_hidden = transposed_right(grad_latent, all_latent) + transposed_right(
        grad_query, all_query
    )
    input_extra, attention_gain_grad = normalize_back(inputs, gain_first, grad_hidden)
    input_grad = grad_residual + input_extra

    column = jnp.arange(128, dtype=jnp.int32)[None, :]
    latent_rows = jnp.pad(
        latent_gain_grad.reshape(devices, small_latent), ((0, 0), (0, shard - small_latent))
    ).reshape(D)
    small_grad = router_weight_grad
    for place, vector in enumerate((attention_gain_grad, feed_gain_grad, latent_rows)):
        small_grad = jnp.where(column == experts_count + place, vector[:, None], small_grad)
    small_grad = small_grad.reshape(devices, shard, 128)
    latent_grad, small_grad, later_grad = scatter(
        [low(latent_grad).reshape(devices, shard, LAT + ROPE), low(small_grad), later_grad],
        [ZYX, XYZ, ZXY],
        6,
    )
    query_grad = jnp.concatenate(
        [
            query_grad[:, :plain].reshape(shard, H, NOPE),
            query_grad[:, plain : plain + half].reshape(shard, H, ROPE // 2),
            query_grad[:, plain + half :].reshape(shard, H, ROPE // 2),
        ],
        axis=2,
    ).reshape(shard, key_width)
    return (
        layer_output.reshape(1, MICRO, tokens, D),
        input_grad.reshape(1, MICRO, tokens, D),
        small_grad[:, experts_count],
        query_grad,
        latent_grad,
        small_grad[:small_latent, experts_count + 2],
        expand_grad.reshape(expand_weight.shape),
        jnp.concatenate([wide(output_grad), later_grad], axis=1).T,
        small_grad[:, experts_count + 1],
        small_grad[:, :experts_count],
        shared_in_grad[0],
        shared_in_grad[1],
        shared_down_grad,
        expert_grads[0],
        expert_grads[1],
        expert_grads[2],
    )


def solution(mesh):
    placed = (
        P("dp", None, "expert", None),
        P("dp", None, "expert", None),
        P("dp", None, None),
        P("dp", None, "expert", None),
        P(("dp", "expert")),
        P(("dp", "expert"), None),
        P(("dp", "expert"), None),
        P(("dp", "expert")),
        P(("dp", "expert"), None),
        P(None, ("dp", "expert")),
        P(("dp", "expert")),
        P(("dp", "expert"), None),
        P(("dp", "expert"), None),
        P(("dp", "expert"), None),
        P(("dp", "expert"), None),
        P("expert", "dp", None),
        P("expert", "dp", None),
        P("expert", None, "dp"),
    )
    return jax.shard_map(
        body,
        mesh=mesh,
        in_specs=placed,
        out_specs=(
            P("dp", None, "expert", None),
            P("dp", None, "expert", None),
            P(("dp", "expert")),
            P(("dp", "expert"), None),
            P(("dp", "expert"), None),
            P(("dp", "expert")),
            P(("dp", "expert"), None),
            P(None, ("dp", "expert")),
            P(("dp", "expert")),
            P(("dp", "expert"), None),
            P(("dp", "expert"), None),
            P(("dp", "expert"), None),
            P(("dp", "expert"), None),
            P("expert", "dp", None),
            P("expert", "dp", None),
            P("expert", None, "dp"),
        ),
        check_vma=False,
    )
```
